32 devices in a mesh: leaf: 4 (over y, x), front: 8 (over z, core).
Axes of the slice: x: 2, y: 2, z: 4, core: 2. Of those that a mesh axis runs over, the one named last changes fastest.
Arguments:
- front: float32 [2048, 2048], P('leaf', 'front'), as said below
- updates: float32 [128, 128, 128], P(('leaf', 'front')), may hold values from -4 to 4
- target_owner: int32 [128], P(('leaf', 'front')), may hold values from 0 to 7, as said below
- target_slot: int32 [128], P(('leaf', 'front')), may hold values from 0 to 7
Outputs:
- factored: float32 [2048, 2048], P('leaf', 'front')
The draws below stay inside these ranges and needn't reach their ends.
Inputs may be any that keep to these rules, and one draw needn't show every extreme that they name: `target_owner`: among the 4 blocks of one device every owner index appears at most once; in every group of devices sharing an index of leaf, some owner index is named by every device of the group. The front is symmetric.
All inputs are finite; a program needn't handle non-finite values.
Results may differ from the reference program's by a relative error of at most 0.00015.
Values sent between devices are 32-bit elements; how exact they have to be, the bound alone decides.
No kernel may reach another device: no remote copies, remote signals or barrier semaphores. Data moves between devices by JAX's collectives and lax.ppermute only.
A program may use at most 128 MiB of HBM per device.

```python
import jax
import jax.numpy as jnp
from jax import lax

W = 256
TILE = 128
SENDS = 4
M = 2048
BAND = 512
TILES = 8
N_LEAF = 4
N_FRONT = 8


def draw_front(key, part):
    gram_key = jax.random.fold_in(key, 21)
    noise_key = jax.random.fold_in(key, 22)
    factor = jax.random.randint(gram_key, (M, W), -2, 3).astype(jnp.float32)
    spread = 2.0
    noise = jnp.clip(jax.random.normal(noise_key, (M, M), jnp.float32), -4.0, 4.0) * 0.3
    gram = jnp.dot(factor, factor.T, precision=lax.Precision.HIGHEST)
    balanced = 0.5 * (noise + noise.T)
    rows = jnp.arange(M, dtype=jnp.int32)
    shift = jnp.where(rows[:, None] == rows[None, :], jnp.float32(80.0), jnp.float32(0.0))
    return gram * jnp.float32(200.0 / (spread * W)) + balanced + shift


def draw_target_owner(key, part):
    senders = N_LEAF * N_FRONT
    common = jax.random.randint(jax.random.fold_in(key, 11), (N_LEAF,), 0, N_FRONT)

    def offsets(sub):
        picked = jax.random.permutation(sub, N_FRONT - 1)[:SENDS - 1].astype(jnp.int32) + 1
        return jnp.concatenate([jnp.zeros((1,), jnp.int32), picked])
    keys = jax.random.split(jax.random.fold_in(key, 12), senders)
    table = jax.vmap(offsets)(keys)
    base = jnp.repeat(common, N_FRONT)
    return ((base[:, None] + table) % N_FRONT).reshape(-1).astype(jnp.int32)


def place_ends(array, rng, low, high):
    longest = array.shape.index(max(array.shape))
    spots = []
    for shift in (0, 1):
        where = [jax.random.randint(jax.random.fold_in(rng, axis), (), 0, length) for axis, length in enumerate(array.shape)]
        where[longest] = (where[longest] + shift) % array.shape[longest]
        spots.append(tuple(where))
    return array.at[spots[0]].set(low).at[spots[1]].set(high)


def shard_levels(stream_key, dims, cuts, least, high):
    def one(position, parts):
        draws = jax.random.uniform(jax.random.fold_in(jax.random.fold_in(stream_key, 6), position), (parts,), jnp.float32, least / len(cuts), high / len(cuts))
        return jnp.repeat(jnp.exp(draws), dims[position] // parts).reshape((-1,) + (1,) * (len(dims) - position - 1))

    factor_of = one(*cuts[0])
    for cut in cuts[1:]:
        factor_of = factor_of * one(*cut)
    return factor_of


def centred(stream_key, dims, width, limit, cuts=(), kind=jnp.bfloat16):
    values = width * jax.random.normal(stream_key, dims, jnp.float32)
    if cuts:
        values = values * shard_levels(stream_key, dims, cuts, -0.22, 0.18)
    return jnp.clip(values, -limit, limit).astype(kind)


def setup_inputs(seed: int = 0) -> dict:
    arg_keys = jax.random.split(jax.random.key(seed), 5)
    return {
        "front": draw_front(jax.random.fold_in(arg_keys[4], 71), 0),
        "updates": centred(arg_keys[1], (N_LEAF * N_FRONT * SENDS, TILE, TILE), 0.5, 4.0, ((0, 32),), jnp.float32),
        "target_owner": draw_target_owner(jax.random.fold_in(arg_keys[4], 71), 0),
        "target_slot": place_ends(jax.random.randint(arg_keys[3], (N_LEAF * N_FRONT * SENDS,), 0, TILES), jax.random.fold_in(arg_keys[3], 1), 0, TILES - 1).astype(jnp.int32),
    }


def panel_step(matrix, start):
    diag = matrix[start:start + W, start:start + W]
    chol = jnp.linalg.cholesky(diag)
    eye = jnp.eye(W, dtype=jnp.float32)
    inverse = lax.linalg.triangular_solve(chol, eye, left_side=True, lower=True)
    panel = matrix[:, start:start + W]
    prod = jnp.dot(panel, inverse.T, precision=lax.Precision.HIGHEST)
    row_ids = jnp.arange(M, dtype=jnp.int32)
    lower = jnp.where(row_ids[:, None] >= start, prod, panel)
    trail = lower[start + W:]
    block = matrix[start + W:, start + W:] - jnp.dot(trail, trail.T, precision=lax.Precision.HIGHEST)
    matrix = matrix.at[start + W:, start + W:].set(block)
    return matrix.at[:, start:start + W].set(lower)

def reference(front, updates, target_owner, target_slot):
    row_tiles = BAND // TILE
    col_tiles = W // TILE
    total = N_LEAF * N_FRONT * SENDS
    group = jnp.arange(total, dtype=jnp.int32) // (N_FRONT * SENDS)
    grow = group * row_tiles + target_slot // col_tiles
    gcol = target_owner * col_tiles + target_slot % col_tiles
    grid = front.reshape(M // TILE, TILE, M // TILE, TILE)
    grid = grid.at[grow, :, gcol, :].add(updates)
    matrix = grid.reshape(M, M)
    matrix = panel_step(matrix, 0)
    matrix = panel_step(matrix, W)
    return matrix
```

```python
import functools

import jax
import jax.numpy as jnp
from jax import lax
from jax.experimental import pallas as pl
from jax.experimental.pallas import tpu as pltpu
from jax.sharding import PartitionSpec as P

F32 = jnp.float32
BF16 = jnp.bfloat16
AXES = ("leaf", "front")
EXACT = lax.Precision.HIGHEST
VMEM_LIMIT = 40 * 1024 * 1024


def spread(value, axis, source):
    kept = jnp.where(lax.axis_index(axis) == source, value, 0).astype(value.dtype)
    return lax.psum(kept, axis)


def assemble(front, updates, target_owner, target_slot):
    nrows, width = front.shape
    tile = updates.shape[1]
    nfront = lax.axis_size("front")
    buffer = jnp.zeros((nfront, tile, tile), F32).at[target_owner].set(updates)
    labels = jnp.zeros((nfront,), F32).at[target_owner].set(target_slot.astype(F32))
    arrived, places = (
        lax.all_to_all(buffer, "front", split_axis=0, concat_axis=0, tiled=True),
        lax.all_to_all(labels, "front", split_axis=0, concat_axis=0, tiled=True),
    )
    places = places.astype(jnp.int32)
    col_tiles = width // tile
    grid = front.reshape(nrows // tile, tile, col_tiles, tile)
    grid = grid.at[places // col_tiles, :, places % col_tiles, :].add(arrived)
    return grid.reshape(nrows, width)


def eliminate(shard, panel, start, row_ids, col_ids, column):
    nrows, width = panel.shape
    diag = spread(panel[start : start + width], "leaf", 0)
    chol = jnp.linalg.cholesky(diag)
    eye = jnp.eye(width, dtype=F32)
    inverse = lax.linalg.triangular_solve(chol, eye, left_side=True, lower=True)
    prod = jnp.dot(panel, inverse.T, precision=EXACT)
    lower = jnp.where(row_ids[:, None] >= start, prod, panel)
    owner_row = column * width // nrows
    offset = column * width - owner_row * nrows
    mine = lax.dynamic_slice_in_dim(lower, offset, width, 0)
    across = spread(mine, "leaf", owner_row)
    trail = jnp.where(row_ids[:, None] >= start + width, lower, 0.0)
    updated = shard - jnp.dot(trail, across.T, precision=EXACT)
    updated = jnp.where(col_ids[None, :] >= start + width, updated, shard)
    return (jnp.where(column == start // width, lower, updated), lower)


def general(front, updates, target_owner, target_slot):
    nrows, width = front.shape
    column = lax.axis_index("front")
    row_ids = lax.axis_index("leaf") * nrows + jnp.arange(nrows, dtype=jnp.int32)
    col_ids = column * width + jnp.arange(width, dtype=jnp.int32)
    shard = assemble(front, updates, target_owner, target_slot)
    first = spread(shard, "front", 0)
    shard, lower = eliminate(shard, first, 0, row_ids, col_ids, column)
    second = spread(shard, "front", 1)
    shard, lower = eliminate(shard, second, width, row_ids, col_ids, column)
    return shard


def lane_of(x, c):
    return jnp.take_along_axis(x, jnp.full(x.shape, c, jnp.int32), axis=1)


def row_of(x, i):
    return jnp.broadcast_to(x[i : i + 1, :], x.shape)


def parts(x):
    high = x.astype(BF16).astype(F32)
    rest = x - high
    mid = rest.astype(BF16).astype(F32)
    return high, mid, (rest - mid).astype(BF16).astype(F32)


def factor_inverse(a):
    n = a.shape[0]
    panels, per = n // 8, 2
    sub = lax.broadcasted_iota(jnp.int32, (8, n), 0)
    lane = lax.broadcasted_iota(jnp.int32, (8, n), 1)
    work = [
        [a[8 * k : 8 * k + 8, :], jnp.where(lane == sub + 8 * k, 1.0, 0.0).astype(F32)]
        for k in range(panels)
    ]
    out, held = [], []
    for k in range(panels):
        rows, ident = work[k]
        cols = [lane_of(rows, 8 * k + j) for j in range(8)]
        d = {(i, j): row_of(cols[j], i) for j in range(8) for i in range(j, 8)}
        up = [row_of(rows, j) for j in range(8)]
        inv = [row_of(ident, j) for j in range(8)]
        last = min(panels - 1, (k // per + 1) * per - 1)
        below = {
            b: [lane_of(work[b][0], 8 * k + j) for j in range(8)]
            for b in range(k + 1, last + 1)
        }
        for j in range(8):
            r = lax.rsqrt(d[j, j])
            for i in range(j + 1, 8):
                d[i, j] = d[i, j] * r
            for i in range(j + 1, 8):
                for m in range(j + 1, i + 1):
                    d[i, m] = d[i, m] - d[i, j] * d[m, j]
            up[j] = up[j] * r
            inv[j] = inv[j] * r
            for i in range(j + 1, 8):
                up[i] = up[i] - d[i, j] * up[j]
                inv[i] = inv[i] - d[i, j] * inv[j]
            for b, c in below.items():
                c[j] = c[j] * r
                for i in range(j + 1, 8):
                    c[i] = c[i] - d[i, j] * c[j]
                work[b] = [work[b][0] - c[j] * up[j], work[b][1] - c[j] * inv[j]]
        u, w = up[0], inv[0]
        for j in range(1, 8):
            u = jnp.where(sub == j, up[j], u)
            w = jnp.where(sub == j, inv[j], w)
        out.append(w)
        held.append((u, w))
        if k % per == per - 1 and k + 1 < panels:
            us = jnp.concatenate([p[0] for p in held], 0)
            ws = jnp.concatenate([p[1] for p in held], 0)
            uh, um, ul = parts(us)
            wh, wm, wl = parts(ws)
            right = jnp.concatenate(
                [
                    jnp.concatenate([uh, um, ul, uh, um, uh], 0),
                    jnp.concatenate([wh, wm, wl, wh, wm, wh], 0),
                ],
                1,
            ).astype(BF16)
            left = jnp.concatenate([uh, uh, uh, um, um, ul], 0).T
            left = left[8 * (k + 1) :, :].astype(BF16)
            change = jnp.dot(left, right, preferred_element_type=F32)
            for b in range(k + 1, panels):
                part = change[8 * (b - k - 1) : 8 * (b - k), :]
                work[b] = [work[b][0] - part[:, :n], work[b][1] - part[:, n:]]
            held = []
    return jnp.concatenate(out, 0)


def dot(a, b):
    return jnp.dot(a, b, precision=EXACT, preferred_element_type=F32)


def dot_t(a, b):
    return lax.dot_general(
        a, b, (((1,), (1,)), ((), ())), precision=EXACT, preferred_element_type=F32
    )


def factor_pair(a):
    h = a.shape[0] // 2
    w11 = factor_inverse(a[:h, :h])
    l21 = dot_t(a[h:, :h], w11)
    w22 = factor_inverse(a[h:, h:] - dot_t(l21, l21))
    w21 = -dot(w22, dot(l21, w11))
    return w11, w21, w22


def store_inverse(ref, blocks):
    w11, w21, w22 = blocks
    h = w11.shape[0]
    ref[:h, :h] = w11
    ref[:h, h:] = jnp.zeros_like(w11)
    ref[h:, :h] = w21
    ref[h:, h:] = w22


def symmetric(a):
    return (a + a.T) * 0.5


def add_blocks(ref, labels, blocks, owner, tile, rows):
    for i in range(blocks.shape[0]):
        place = labels[2 * i + owner]
        down = pl.multiple_of(place // 2 * tile, tile)
        right = pl.multiple_of(place % 2 * tile, tile)
        ref[pl.ds(down, tile), pl.ds(right, tile)] += blocks[
            i, owner * tile : (owner + 1) * tile, :
        ]


def first_kernel(labels, front, blocks, w_ref, l_ref, work):
    tile = blocks.shape[2]
    width = front.shape[1]
    work[...] = front[...]
    add_blocks(work, labels, blocks, 0, tile, None)
    store_inverse(w_ref, factor_pair(symmetric(work[:width, :])))
    l_ref[...] = dot_t(work[width:, :], w_ref[...])


def second_kernel(labels, front, blocks, lower, w_ref, work):
    tile = blocks.shape[2]
    width = front.shape[1]
    work[...] = jnp.concatenate([jnp.zeros_like(front), front[...]], 0)
    add_blocks(work, labels, blocks, 1, tile, None)
    diag = work[width:, :] - dot_t(lower[...], lower[...])
    store_inverse(w_ref, factor_pair(symmetric(diag)))


def matched_kernel(labels, half, front, blocks, out_ref, work):
    tile = blocks.shape[2]
    width = front.shape[1]
    work[...] = jnp.zeros_like(work)
    for owner in range(2):
        for i in range(blocks.shape[0]):
            place = labels[2 * i + owner]
            down = pl.multiple_of(place // 2 * tile, tile)
            right = pl.multiple_of(owner * width + place % 2 * tile, tile)
            work[pl.ds(down, tile), pl.ds(right, tile)] += blocks[
                i, owner * tile : (owner + 1) * tile, :
            ]
    start = pl.multiple_of(half[0] * width, width)
    out_ref[...] = front[...].T + work[pl.ds(start, width), :]


def last_kernel(
    labels, info, places, shard, arrived, pieces, blocks, matched, w1, l21, w2, out_ref, band
):
    tile = blocks.shape[2]
    nrows, width = shard.shape
    group, column = info[0], info[1]
    out_ref[...] = shard[...]
    for i in range(arrived.shape[0]):
        place = places[i]
        down = pl.multiple_of(place // 2 * tile, tile)
        right = pl.multiple_of(place % 2 * tile, tile)
        out_ref[pl.ds(down, tile), pl.ds(right, tile)] += arrived[i, :tile, :]
    for i in range(pieces.shape[0]):
        r, c = i // 2 * tile, i % 2 * width
        band[r : r + tile, c : c + width] = pieces[i]
    for owner in range(2):
        for i in range(blocks.shape[0]):
            place = labels[2 * i + owner]
            down = pl.multiple_of(place // 2 * tile, tile)
            right = pl.multiple_of(owner * width + place % 2 * tile, tile)
            band[pl.ds(down, tile), pl.ds(right, tile)] += blocks[
                i, owner * tile : (owner + 1) * tile, :
            ]
    rows = group * nrows + lax.broadcasted_iota(jnp.int32, (nrows, width), 0)
    first = dot_t(band[:, :width], w1[...])
    raw = band[:, width:]
    second = dot_t(raw - dot_t(first, l21[...]), w2[...])

    @pl.when(column == 0)
    def _():
        out_ref[...] = first

    @pl.when(column == 1)
    def _():
        out_ref[...] = jnp.where(rows >= width, second, raw)

    @pl.when(column >= 2)
    def _():
        m1 = dot_t(matched[:, :width], w1[...])
        m2 = dot_t(matched[:, width:] - dot_t(m1, l21[...]), w2[...])
        t1 = jnp.where(rows >= width, first, 0.0)
        t2 = jnp.where(rows >= 2 * width, second, 0.0)
        out_ref[...] = out_ref[...] - (dot_t(t1, m1) + dot_t(t2, m2))


def kernel(body, outs, scratch, smem, n_vmem, flops):
    spec = [pl.BlockSpec(memory_space=pltpu.SMEM)] * smem
    spec += [pl.BlockSpec(memory_space=pltpu.VMEM)] * n_vmem
    return pl.pallas_call(
        body,
        out_shape=outs,
        in_specs=spec,
        scratch_shapes=[pltpu.VMEM(s, F32) for s in scratch],
        compiler_params=pltpu.CompilerParams(vmem_limit_bytes=VMEM_LIMIT),
        cost_estimate=pl.CostEstimate(
            flops=flops, bytes_accessed=1 << 20, transcendentals=0
        ),
    )


def aligned(front, updates, target_owner, target_slot):
    nrows, width = front.shape
    sends, tile = updates.shape[:2]
    nleaf, nfront = lax.axis_size("leaf"), lax.axis_size("front")
    nz = nfront // 2
    group, column = lax.axis_index("leaf"), lax.axis_index("front")
    layer, core = column // 2, column % 2

    def dev(g, z, c):
        return g * nfront + 2 * z + c

    def send(x, pairs):
        return lax.ppermute(x, AXES, pairs)

    cores = [
        (dev(g, z, c), dev(g, z, 1 - c))
        for g in range(nleaf)
        for z in range(nz)
        for c in range(2)
    ]
    slots = target_slot.astype(F32)
    hit = target_owner[None, :] == jnp.arange(nfront, dtype=jnp.int32)[:, None]
    buffer = jnp.zeros((nfront, tile, tile), F32)
    place = jnp.zeros((nfront,), F32)
    for j in range(sends):
        buffer = buffer + jnp.where(hit[:, j, None, None], updates[j][None], 0.0)
        place = place + jnp.where(hit[:, j], slots[j], 0.0)
    tags = jnp.broadcast_to(place[:, None, None], (nfront, 8, tile))
    payload = jnp.concatenate([buffer[0], buffer[1], tags[0], tags[1]], 0)

    got = [payload]
    for s in range(1, nz):
        pairs = [
            (dev(g, z, c), dev(g, z ^ s, c))
            for g in range(nleaf)
            for z in range(nz)
            for c in range(2)
        ]
        got.append(send(payload, pairs))
    mine = jnp.stack(got)
    blocks = jnp.concatenate([mine, send(mine, cores)], 0)
    labels = blocks[:, 2 * tile :: 8, 0].reshape(-1).astype(jnp.int32)

    diag_front = send(front[width:], [(dev(0, 0, 1), dev(0, 0, 0))])
    piece = jnp.where(layer == 0, front[:tile], 0.0)
    for s in range(1, nz):
        pairs = [(dev(g, 0, c), dev(g, s, c)) for g in range(nleaf) for c in range(2)]
        piece = piece + send(front[s * tile : (s + 1) * tile], pairs)
    pieces = lax.all_gather(piece, "front", axis=0, tiled=False)
    turned = send(front, [(dev(0, z, c), dev(z, z, c)) for z in range(1, nz) for c in range(2)])

    half = core.reshape(1)
    matched = kernel(
        matched_kernel,
        jax.ShapeDtypeStruct((width, 2 * width), F32),
        [(nrows, 2 * width)],
        2,
        2,
        1 << 20,
    )(labels, half, turned, blocks)
    away = jnp.where(layer == group, matched, 0.0)
    for s in range(1, nleaf):
        pairs = [(dev(z, z, c), dev(z ^ s, z, c)) for z in range(1, nz) for c in range(2)]
        away = away + send(matched, pairs)

    def share(x):
        for_group = jnp.where(group == 0, x, 0.0)
        for s in range(1, nleaf):
            for_group = for_group + send(x, [(dev(0, 0, 0), dev(s, 0, 0))])
        for_layer = jnp.where(layer == 0, for_group, 0.0)
        for s in range(1, nz):
            for_layer = for_layer + send(
                for_group, [(dev(g, 0, 0), dev(g, s, 0)) for g in range(nleaf)]
            )
        other = send(for_layer, [(dev(g, z, 0), dev(g, z, 1)) for g in range(nleaf) for z in range(nz)])
        return jnp.where(core == 0, for_layer, other)

    square = jax.ShapeDtypeStruct((width, width), F32)
    w1, l21 = kernel(first_kernel, (square, square), [(nrows, width)], 1, 2, 1 << 31)(
        labels, front, blocks
    )
    w2 = kernel(second_kernel, square, [(nrows, width)], 1, 3, 1 << 31)(
        labels, diag_front, blocks, l21
    )
    early = share(jnp.concatenate([w1, l21], 0))
    w2 = share(w2)

    outgoing = jnp.concatenate([buffer, tags], 1)
    arrived = lax.all_to_all(outgoing, "front", split_axis=0, concat_axis=0, tiled=True)
    places = arrived[:, tile, 0].astype(jnp.int32)
    info = jnp.stack([group, column]).astype(jnp.int32)
    return kernel(
        last_kernel,
        jax.ShapeDtypeStruct((nrows, width), F32),
        [(nrows, 2 * width)],
        3,
        8,
        1 << 31,
    )(labels, info, places, front, arrived, pieces, blocks, away, early[:width], early[width:], w2)


def solution(mesh):
    nleaf, nfront = mesh.shape["leaf"], mesh.shape["front"]

    def shards(front, updates, target_owner, target_slot):
        nrows, width = front.shape
        tile = updates.shape[1]
        lines_up = (
            nrows == 2 * width
            and width == 2 * tile
            and nfront == 2 * nleaf
            and nleaf == nrows // tile
        )
        plan = aligned if lines_up else general
        return plan(front, updates, target_owner, target_slot)

    return jax.shard_map(
        shards,
        mesh=mesh,
        in_specs=(
            P("leaf", "front"),
            P(("leaf", "front"), None, None),
            P(("leaf", "front")),
            P(("leaf", "front")),
        ),
        out_specs=P("leaf", "front"),
        check_vma=False,
    )
```

```python
import functools

import jax
import jax.numpy as jnp
from jax import lax
from jax.experimental import pallas as pl
from jax.experimental.pallas import tpu as pltpu
from jax.sharding import PartitionSpec as P

F32 = jnp.float32
BF16 = jnp.bfloat16
AXES = ("leaf", "front")
EXACT = lax.Precision.HIGHEST
VMEM_LIMIT = 40 * 1024 * 1024


def spread(value, axis, source):
    kept = jnp.where(lax.axis_index(axis) == source, value, 0).astype(value.dtype)
    return lax.psum(kept, axis)


def assemble(front, updates, target_owner, target_slot):
    nrows, width = front.shape
    tile = updates.shape[1]
    nfront = lax.axis_size("front")
    buffer = jnp.zeros((nfront, tile, tile), F32).at[target_owner].set(updates)
    labels = jnp.zeros((nfront,), F32).at[target_owner].set(target_slot.astype(F32))
    arrived, places = (
        lax.all_to_all(buffer, "front", split_axis=0, concat_axis=0, tiled=True),
        lax.all_to_all(labels, "front", split_axis=0, concat_axis=0, tiled=True),
    )
    places = places.astype(jnp.int32)
    col_tiles = width // tile
    grid = front.reshape(nrows // tile, tile, col_tiles, tile)
    grid = grid.at[places // col_tiles, :, places % col_tiles, :].add(arrived)
    return grid.reshape(nrows, width)


def eliminate(shard, panel, start, row_ids, col_ids, column):
    nrows, width = panel.shape
    diag = spread(panel[start : start + width], "leaf", 0)
    chol = jnp.linalg.cholesky(diag)
    eye = jnp.eye(width, dtype=F32)
    inverse = lax.linalg.triangular_solve(chol, eye, left_side=True, lower=True)
    prod = jnp.dot(panel, inverse.T, precision=EXACT)
    lower = jnp.where(row_ids[:, None] >= start, prod, panel)
    owner_row = column * width // nrows
    offset = column * width - owner_row * nrows
    mine = lax.dynamic_slice_in_dim(lower, offset, width, 0)
    across = spread(mine, "leaf", owner_row)
    trail = jnp.where(row_ids[:, None] >= start + width, lower, 0.0)
    updated = shard - jnp.dot(trail, across.T, precision=EXACT)
    updated = jnp.where(col_ids[None, :] >= start + width, updated, shard)
    return (jnp.where(column == start // width, lower, updated), lower)


def general(front, updates, target_owner, target_slot):
    nrows, width = front.shape
    column = lax.axis_index("front")
    row_ids = lax.axis_index("leaf") * nrows + jnp.arange(nrows, dtype=jnp.int32)
    col_ids = column * width + jnp.arange(width, dtype=jnp.int32)
    shard = assemble(front, updates, target_owner, target_slot)
    first = spread(shard, "front", 0)
    shard, lower = eliminate(shard, first, 0, row_ids, col_ids, column)
    second = spread(shard, "front", 1)
    shard, lower = eliminate(shard, second, width, row_ids, col_ids, column)
    return shard


def lane_of(x, c):
    return jnp.take_along_axis(x, jnp.full(x.shape, c, jnp.int32), axis=1)


def row_of(x, i):
    return jnp.broadcast_to(x[i : i + 1, :], x.shape)


def parts(x):
    high = x.astype(BF16).astype(F32)
    rest = x - high
    mid = rest.astype(BF16).astype(F32)
    return high, mid, (rest - mid).astype(BF16).astype(F32)


def factor_inverse(a):
    n = a.shape[0]
    panels, per = n // 8, 2
    sub = lax.broadcasted_iota(jnp.int32, (8, n), 0)
    lane = lax.broadcasted_iota(jnp.int32, (8, n), 1)
    work = [
        [a[8 * k : 8 * k + 8, :], jnp.where(lane == sub + 8 * k, 1.0, 0.0).astype(F32)]
        for k in range(panels)
    ]
    out, held = [], []
    for k in range(panels):
        rows, ident = work[k]
        cols = [lane_of(rows, 8 * k + j) for j in range(8)]
        d = {(i, j): row_of(cols[j], i) for j in range(8) for i in range(j, 8)}
        up = [row_of(rows, j) for j in range(8)]
        inv = [row_of(ident, j) for j in range(8)]
        last = min(panels - 1, (k // per + 1) * per - 1)
        below = {
            b: [lane_of(work[b][0], 8 * k + j) for j in range(8)]
            for b in range(k + 1, last + 1)
        }
        for j in range(8):
            r = lax.rsqrt(d[j, j])
            for i in range(j + 1, 8):
                d[i, j] = d[i, j] * r
            for i in range(j + 1, 8):
                for m in range(j + 1, i + 1):
                    d[i, m] = d[i, m] - d[i, j] * d[m, j]
            up[j] = up[j] * r
            inv[j] = inv[j] * r
            for i in range(j + 1, 8):
                up[i] = up[i] - d[i, j] * up[j]
                inv[i] = inv[i] - d[i, j] * inv[j]
            for b, c in below.items():
                c[j] = c[j] * r
                for i in range(j + 1, 8):
                    c[i] = c[i] - d[i, j] * c[j]
                work[b] = [work[b][0] - c[j] * up[j], work[b][1] - c[j] * inv[j]]
        u, w = up[0], inv[0]
        for j in range(1, 8):
            u = jnp.where(sub == j, up[j], u)
            w = jnp.where(sub == j, inv[j], w)
        out.append(w)
        held.append((u, w))
        if k % per == per - 1 and k + 1 < panels:
            us = jnp.concatenate([p[0] for p in held], 0)
            ws = jnp.concatenate([p[1] for p in held], 0)
            uh, um, ul = parts(us)
            wh, wm, wl = parts(ws)
            right = jnp.concatenate(
                [
                    jnp.concatenate([uh, um, ul, uh, um, uh], 0),
                    jnp.concatenate([wh, wm, wl, wh, wm, wh], 0),
                ],
                1,
            ).astype(BF16)
            left = jnp.concatenate([uh, uh, uh, um, um, ul], 0).T
            left = left[8 * (k + 1) :, :].astype(BF16)
            change = jnp.dot(left, right, preferred_element_type=F32)
            for b in range(k + 1, panels):
                part = change[8 * (b - k - 1) : 8 * (b - k), :]
                work[b] = [work[b][0] - part[:, :n], work[b][1] - part[:, n:]]
            held = []
    return jnp.concatenate(out, 0)


def dot(a, b):
    return jnp.dot(a, b, precision=EXACT, preferred_element_type=F32)


def dot_t(a, b):
    return lax.dot_general(
        a, b, (((1,), (1,)), ((), ())), precision=EXACT, preferred_element_type=F32
    )


def factor_pair(a):
    h = a.shape[0] // 2
    w11 = factor_inverse(a[:h, :h])
    l21 = dot_t(a[h:, :h], w11)
    w22 = factor_inverse(a[h:, h:] - dot_t(l21, l21))
    w21 = -dot(w22, dot(l21, w11))
    return w11, w21, w22


def store_inverse(ref, blocks):
    w11, w21, w22 = blocks
    h = w11.shape[0]
    ref[:h, :h] = w11
    ref[:h, h:] = jnp.zeros_like(w11)
    ref[h:, :h] = w21
    ref[h:, h:] = w22


def symmetric(a):
    return (a + a.T) * 0.5


def place_of(tags):
    return tags[0, 0].astype(jnp.int32)


def add_block(ref, block, place, tile, start=0):
    down = pl.multiple_of(place // 2 * tile, tile)
    right = pl.multiple_of(start + place % 2 * tile, tile)
    ref[pl.ds(down, tile), pl.ds(right, tile)] += block


def add_band_blocks(ref, blocks, width):
    tile = blocks[0].shape[1]
    for owner in range(2):
        for b in blocks:
            tag = b[2 * tile + 8 * owner : 2 * tile + 8 * owner + 8, :]
            add_block(ref, b[owner * tile : (owner + 1) * tile, :], place_of(tag), tile, owner * width)


def sort_kernel(owner, slot, updates, out_ref, pay_ref):
    sends, tile = updates.shape[:2]
    out_ref[...] = jnp.zeros_like(out_ref)
    for j in range(sends):
        out_ref[owner[j], :tile, :] = updates[j]
        out_ref[owner[j], tile:, :] = jnp.full((8, tile), slot[j].astype(F32))
    for o in range(2):
        pay_ref[o * tile : (o + 1) * tile, :] = out_ref[o, :tile, :]
        pay_ref[2 * tile + 8 * o : 2 * tile + 8 * o + 8, :] = out_ref[o, tile:, :]


def matched_kernel(info, front, turned, *refs):
    blocks, out_ref, band = refs[:-2], refs[-2], refs[-1]
    width = front.shape[1]

    @pl.when(info[0] == info[1])
    def _():
        band[...] = jnp.zeros_like(band)
        add_band_blocks(band, blocks, width)
        start = pl.multiple_of(info[2] * width, width)
        own = jnp.where(info[0] == 0, front[...], turned[...])
        out_ref[...] = own.T + band[pl.ds(start, width), :]


def pack(ref, blocks):
    w11, w21, w22 = blocks
    n = w11.shape[0]
    row = lax.broadcasted_iota(jnp.int32, (n, n), 0)
    col = lax.broadcasted_iota(jnp.int32, (n, n), 1)
    ref[:n, :] = jnp.where(row >= col, w11, w22.T)
    ref[n : 2 * n, :] = w21
    diag = jnp.sum(jnp.where(row == col, w22, 0.0), 0, keepdims=True)
    ref[2 * n :, :] = jnp.broadcast_to(diag, (8, n))


def unpack(ref):
    n = ref.shape[1]
    row = lax.broadcasted_iota(jnp.int32, (n, n), 0)
    col = lax.broadcasted_iota(jnp.int32, (n, n), 1)
    both, zero = ref[:n, :], jnp.zeros((n, n), F32)
    w11 = jnp.where(row >= col, both, 0.0)
    w22 = jnp.where(row > col, both.T, jnp.where(row == col, ref[2 * n : 2 * n + 1, :], 0.0))
    return jnp.concatenate(
        [jnp.concatenate([w11, zero], 1), jnp.concatenate([ref[n : 2 * n, :], w22], 1)], 0
    )


def first_kernel(info, matched, w_ref):
    width = matched.shape[0]

    @pl.when(info[3] == 0)
    def _():
        pack(w_ref, factor_pair(symmetric(matched[:, :width])))


def second_kernel(info, below, w1, w_ref):
    width = below.shape[0]

    @pl.when(info[3] == 0)
    def _():
        lower = dot_t(below[:, :width], unpack(w1))
        pack(w_ref, factor_pair(symmetric(below[:, width:] - dot_t(lower, lower))))


def middle_kernel(info, shard, arrived, piece, piece2, matched, m1, m2, m3, diag, diag2, w, w2, *refs):
    blocks = refs[:8]
    out_ref, q_ref, n_ref, band, line, square, tri = refs[8:]
    tile = arrived.shape[2]
    nrows, width = shard.shape
    group, layer, core, column = info[0], info[1], info[2], info[4]
    out_ref[...] = shard[...]
    for i in range(arrived.shape[0]):
        add_block(out_ref, arrived[i, :tile, :], place_of(arrived[i, tile:, :]), tile)
    @pl.when(core == 1)
    def _():
        square[...] = diag[...]
        tri[...] = w[...]

    @pl.when(core == 0)
    def _():
        square[...] = diag2[...]
        tri[...] = w2[...]

    for k, m in enumerate((matched, m1, m2, m3)):

        @pl.when((group ^ layer) == k)
        def _(m=m):
            line[...] = m[...]

    w1 = unpack(tri)
    l21 = dot_t(square[...], w1)
    by_rows = ((group >= 2) & (layer >= 2)) | (group == layer)
    for c, (same, swapped) in enumerate(((piece, piece2), (piece2, piece))):

        @pl.when(by_rows & (core == 0))
        def _(c=c, p=same):
            band[c * width : (c + 1) * width, :] = p[...].T

        @pl.when(by_rows & (core == 1))
        def _(c=c, p=swapped):
            band[c * width : (c + 1) * width, :] = p[...].T

        @pl.when(~by_rows & (core == 0))
        def _(c=c, p=same):
            band[:, c * width : (c + 1) * width] = p[...]

        @pl.when(~by_rows & (core == 1))
        def _(c=c, p=swapped):
            band[:, c * width : (c + 1) * width] = p[...]

    add_band_blocks(band, blocks, width)

    @pl.when(column == 0)
    def _():
        out_ref[...] = dot_t(out_ref[...], w1)
        q_ref[...] = jnp.zeros_like(q_ref)
        n_ref[...] = jnp.zeros_like(n_ref)

    @pl.when(column > 0)
    def _():
        @pl.when(group == 0)
        def _():
            q_ref[:width, :] = jnp.zeros((width, width), F32)
            q_ref[width:, :] = l21

        @pl.when(group > 0)
        def _():
            q_ref[...] = dot_t(band[:, :width], w1)

        @pl.when(column == 1)
        def _():
            q_ref[...] = out_ref[...] - dot_t(q_ref[...], l21)
            n_ref[...] = jnp.zeros_like(n_ref)

        @pl.when(column > 1)
        def _():
            mine = dot_t(line[:, :width], w1)
            n_ref[...] = line[:, width:] - dot_t(mine, l21)
            out_ref[...] = out_ref[...] - dot_t(q_ref[...], mine)
            q_ref[...] = band[:, width:] - dot_t(q_ref[...], l21)


def last_kernel(info, out1, q, n, w, w2, out_ref, tri):
    nrows, width = out1.shape
    group, core, column = info[0], info[2], info[4]

    @pl.when(core == 0)
    def _():
        tri[...] = w[...]

    @pl.when(core == 1)
    def _():
        tri[...] = w2[...]

    @pl.when(column == 0)
    def _():
        out_ref[...] = out1[...]

    @pl.when(column > 0)
    def _():
        inverse = unpack(tri)
        second = dot_t(q[...], inverse)

        @pl.when(column == 1)
        def _():
            rows = group * nrows + lax.broadcasted_iota(jnp.int32, (nrows, width), 0)
            out_ref[...] = jnp.where(rows >= width, second, out1[...])

        @pl.when((column > 1) & (group == 0))
        def _():
            out_ref[...] = out1[...]

        @pl.when((column > 1) & (group > 0))
        def _():
            out_ref[...] = out1[...] - dot_t(second, dot_t(n[...], inverse))


def kernel(body, outs, args, smem=1, scratch=(), flops=1 << 20):
    spec = [pl.BlockSpec(memory_space=pltpu.SMEM)] * smem
    spec += [pl.BlockSpec(memory_space=pltpu.VMEM)] * (len(args) - smem)
    return pl.pallas_call(
        body,
        out_shape=outs,
        in_specs=spec,
        scratch_shapes=[pltpu.VMEM(s, F32) for s in scratch],
        compiler_params=pltpu.CompilerParams(vmem_limit_bytes=VMEM_LIMIT),
        cost_estimate=pl.CostEstimate(flops=flops, bytes_accessed=1 << 20, transcendentals=0),
    )(*args)


def aligned(front, updates, target_owner, target_slot):
    nrows, width = front.shape
    tile = updates.shape[1]
    nleaf, nfront = lax.axis_size("leaf"), lax.axis_size("front")
    groups, layers = range(nleaf), range(nfront // 2)
    group, column = lax.axis_index("leaf"), lax.axis_index("front")
    layer, core = column // 2, column % 2
    info = jnp.stack([group, layer, core, group * nfront + column, column]).astype(jnp.int32)

    def dev(g, z, c):
        return g * nfront + 2 * z + c

    def send(x, pairs):
        return lax.ppermute(x, AXES, pairs)

    def out(*shape):
        return jax.ShapeDtypeStruct(shape, F32)

    both = range(2)
    swap = [(dev(g, z, c), dev(g, z, 1 - c)) for g in groups for z in layers for c in both]

    outgoing, payload = kernel(
        sort_kernel,
        (out(nfront, tile + 8, tile), out(2 * tile + 16, tile)),
        (target_owner, target_slot, updates),
        smem=2,
    )
    blocks = [payload]
    for s in layers[1:]:
        pairs = [(dev(g, z, c), dev(g, z ^ s, c)) for g in groups for z in layers for c in both]
        blocks.append(send(payload, pairs))
    blocks += [send(b, swap) for b in blocks]

    turned = send(front, [(dev(0, z, c), dev(z, z, c)) for z in layers[1:] for c in both])
    matched = kernel(
        matched_kernel, out(width, 2 * width), (info, front, turned, *blocks), scratch=[(nrows, 2 * width)]
    )
    below = send(matched, [(dev(0, 0, 1), dev(0, 0, 0))])
    away = [
        send(
            matched,
            [(dev(z, z, c), dev(z ^ s, z, c)) for z in layers for c in both if (z, c) != (0, 0)],
        )
        for s in groups[1:]
    ]
    diag = jnp.where(group == 0, matched, away[0] + away[1] + away[2])[:, :width]
    moved = [send(diag, [(dev(g, 0, 1), dev(g, s, 1)) for g in groups]) for s in layers[1:]]
    diag = jnp.where(layer == 0, diag, moved[0] + moved[1] + moved[2])
    diag2 = send(diag, [(dev(g, z, 1), dev(g, z, 0)) for g in groups for z in layers])

    near = send(
        front, [(dev(g, 0, c), dev(g, z, c)) for g, z in ((1, 2), (2, 1), (3, 1)) for c in both]
    )
    far = send(
        jnp.where(group == layer, turned, near),
        [(dev(g, z, c), dev(g, 5 - z, c)) for g, z in ((1, 2), (2, 2), (3, 3)) for c in both],
    )
    piece = jnp.where(layer == 0, front, jnp.where(group == layer, turned, near + far))
    piece2 = send(piece, swap)

    def share(x, c):
        got = [send(x, [(dev(0, 0, c), dev(0, s, c))]) for s in layers[1:]]
        x = jnp.where(layer == 0, x, got[0] + got[1] + got[2])
        got = [send(x, [(dev(0, z, c), dev(s, z, c)) for z in layers]) for s in groups[1:]]
        x = jnp.where(group == 0, x, got[0] + got[1] + got[2])
        return x, send(x, [(dev(g, z, c), dev(g, z, 1 - c)) for g in groups for z in layers])

    packed = out(2 * tile + 8, tile)
    w1 = kernel(first_kernel, packed, (info, matched), flops=1 << 32)
    w2 = kernel(second_kernel, packed, (info, below, w1), flops=1 << 32)
    w1, w1x = share(send(w1, [(dev(0, 0, 0), dev(0, 0, 1))]), 1)
    w2, w2x = share(w2, 0)

    arrived = lax.all_to_all(outgoing, "front", split_axis=0, concat_axis=0, tiled=True)
    out1, q, n = kernel(
        middle_kernel,
        (out(nrows, width), out(nrows, width), out(width, width)),
        (info, front, arrived, piece, piece2, matched, *away, diag, diag2, w1, w1x, *blocks),
        scratch=[(nrows, 2 * width), (width, 2 * width), (width, width), (2 * tile + 8, tile)],
        flops=1 << 31,
    )
    return kernel(
        last_kernel, out(nrows, width), (info, out1, q, n, w2, w2x), scratch=[(2 * tile + 8, tile)], flops=1 << 30
    )


def solution(mesh):
    nleaf, nfront = mesh.shape["leaf"], mesh.shape["front"]

    def shards(front, updates, target_owner, target_slot):
        nrows, width = front.shape
        tile = updates.shape[1]
        lines_up = (
            nrows == 2 * width
            and width == 2 * tile
            and nleaf == 4
            and nfront == 8
        )
        plan = aligned if lines_up else general
        return plan(front, updates, target_owner, target_slot)

    return jax.shard_map(
        shards,
        mesh=mesh,
        in_specs=(
            P("leaf", "front"),
            P(("leaf", "front"), None, None),
            P(("leaf", "front")),
            P(("leaf", "front")),
        ),
        out_specs=P("leaf", "front"),
        check_vma=False,
    )
```

```python
import functools

import jax
import jax.numpy as jnp
from jax import lax
from jax.experimental import pallas as pl
from jax.experimental.pallas import tpu as pltpu
from jax.sharding import PartitionSpec as P

F32 = jnp.float32
BF16 = jnp.bfloat16
AXES = ("leaf", "front")
EXACT = lax.Precision.HIGHEST
VMEM_LIMIT = 40 * 1024 * 1024


def spread(value, axis, source):
    kept = jnp.where(lax.axis_index(axis) == source, value, 0).astype(value.dtype)
    return lax.psum(kept, axis)


def assemble(front, updates, target_owner, target_slot):
    nrows, width = front.shape
    tile = updates.shape[1]
    nfront = lax.axis_size("front")
    buffer = jnp.zeros((nfront, tile, tile), F32).at[target_owner].set(updates)
    labels = jnp.zeros((nfront,), F32).at[target_owner].set(target_slot.astype(F32))
    arrived, places = (
        lax.all_to_all(buffer, "front", split_axis=0, concat_axis=0, tiled=True),
        lax.all_to_all(labels, "front", split_axis=0, concat_axis=0, tiled=True),
    )
    places = places.astype(jnp.int32)
    col_tiles = width // tile
    grid = front.reshape(nrows // tile, tile, col_tiles, tile)
    grid = grid.at[places // col_tiles, :, places % col_tiles, :].add(arrived)
    return grid.reshape(nrows, width)


def eliminate(shard, panel, start, row_ids, col_ids, column):
    nrows, width = panel.shape
    diag = spread(panel[start : start + width], "leaf", 0)
    chol = jnp.linalg.cholesky(diag)
    eye = jnp.eye(width, dtype=F32)
    inverse = lax.linalg.triangular_solve(chol, eye, left_side=True, lower=True)
    prod = jnp.dot(panel, inverse.T, precision=EXACT)
    lower = jnp.where(row_ids[:, None] >= start, prod, panel)
    owner_row = column * width // nrows
    offset = column * width - owner_row * nrows
    mine = lax.dynamic_slice_in_dim(lower, offset, width, 0)
    across = spread(mine, "leaf", owner_row)
    trail = jnp.where(row_ids[:, None] >= start + width, lower, 0.0)
    updated = shard - jnp.dot(trail, across.T, precision=EXACT)
    updated = jnp.where(col_ids[None, :] >= start + width, updated, shard)
    return (jnp.where(column == start // width, lower, updated), lower)


def general(front, updates, target_owner, target_slot):
    nrows, width = front.shape
    column = lax.axis_index("front")
    row_ids = lax.axis_index("leaf") * nrows + jnp.arange(nrows, dtype=jnp.int32)
    col_ids = column * width + jnp.arange(width, dtype=jnp.int32)
    shard = assemble(front, updates, target_owner, target_slot)
    first = spread(shard, "front", 0)
    shard, lower = eliminate(shard, first, 0, row_ids, col_ids, column)
    second = spread(shard, "front", 1)
    shard, lower = eliminate(shard, second, width, row_ids, col_ids, column)
    return shard


def lane_of(x, c):
    return jnp.take_along_axis(x, jnp.full(x.shape, c, jnp.int32), axis=1)


def row_of(x, i):
    return jnp.broadcast_to(x[i : i + 1, :], x.shape)


def parts(x):
    high = x.astype(BF16).astype(F32)
    rest = x - high
    mid = rest.astype(BF16).astype(F32)
    return high, mid, (rest - mid).astype(BF16).astype(F32)


def factor_inverse(a):
    n = a.shape[0]
    panels, per, ahead = n // 8, 2, 2
    sub = lax.broadcasted_iota(jnp.int32, (8, n), 0)
    lane = lax.broadcasted_iota(jnp.int32, (8, n), 1)
    work = [
        [a[8 * k : 8 * k + 8, :], jnp.where(lane == sub + 8 * k, 1.0, 0.0).astype(F32)]
        for k in range(panels)
    ]
    out, held = [], []
    for k in range(panels):
        rows, ident = work[k]
        cols = [lane_of(rows, 8 * k + j) for j in range(8)]
        d = {(i, j): row_of(cols[j], i) for j in range(8) for i in range(j, 8)}
        up = [row_of(rows, j) for j in range(8)]
        inv = [row_of(ident, j) for j in range(8)]
        last = min(panels - 1, (k // per + 1) * per - 1 + ahead)
        below = {
            b: [lane_of(work[b][0], 8 * k + j) for j in range(8)]
            for b in range(k + 1, last + 1)
        }
        for j in range(8):
            r = lax.rsqrt(d[j, j])
            for i in range(j + 1, 8):
                d[i, j] = d[i, j] * r
            for i in range(j + 1, 8):
                for m in range(j + 1, i + 1):
                    d[i, m] = d[i, m] - d[i, j] * d[m, j]
            up[j] = up[j] * r
            inv[j] = inv[j] * r
            for i in range(j + 1, 8):
                up[i] = up[i] - d[i, j] * up[j]
                inv[i] = inv[i] - d[i, j] * inv[j]
            for b, c in below.items():
                c[j] = c[j] * r
                for i in range(j + 1, 8):
                    c[i] = c[i] - d[i, j] * c[j]
                work[b] = [work[b][0] - c[j] * up[j], work[b][1] - c[j] * inv[j]]
        u, w = up[0], inv[0]
        for j in range(1, 8):
            u = jnp.where(sub == j, up[j], u)
            w = jnp.where(sub == j, inv[j], w)
        out.append(w)
        held.append((u, w))
        first = k + 1 + ahead
        if k % per == per - 1 and first < panels:
            us = jnp.concatenate([p[0] for p in held], 0)
            ws = jnp.concatenate([p[1] for p in held], 0)
            uh, um, ul = parts(us)
            wh, wm, wl = parts(ws)
            right = jnp.concatenate(
                [
                    jnp.concatenate([uh, um, ul, uh, um, uh], 0),
                    jnp.concatenate([wh, wm, wl, wh, wm, wh], 0),
                ],
                1,
            ).astype(BF16)
            left = jnp.concatenate([uh, uh, uh, um, um, ul], 0).T
            left = left[8 * first :, :].astype(BF16)
            change = jnp.dot(left, right, preferred_element_type=F32)
            for b in range(first, panels):
                part = change[8 * (b - first) : 8 * (b - first + 1), :]
                work[b] = [work[b][0] - part[:, :n], work[b][1] - part[:, n:]]
        if k % per == per - 1:
            held = []
    return jnp.concatenate(out, 0)


def dot(a, b):
    return jnp.dot(a, b, precision=EXACT, preferred_element_type=F32)


def dot_t(a, b):
    return lax.dot_general(
        a, b, (((1,), (1,)), ((), ())), precision=EXACT, preferred_element_type=F32
    )


def factor_pair(a):
    h = a.shape[0] // 2
    w11 = factor_inverse(a[:h, :h])
    l21 = dot_t(a[h:, :h], w11)
    w22 = factor_inverse(a[h:, h:] - dot_t(l21, l21))
    w21 = -dot(w22, dot(l21, w11))
    return w11, w21, w22


def store_inverse(ref, blocks):
    w11, w21, w22 = blocks
    h = w11.shape[0]
    ref[:h, :h] = w11
    ref[:h, h:] = jnp.zeros_like(w11)
    ref[h:, :h] = w21
    ref[h:, h:] = w22


def symmetric(a):
    return (a + a.T) * 0.5


def place_of(tags):
    return tags[0, 0].astype(jnp.int32)


def add_block(ref, block, place, tile, start=0):
    down = pl.multiple_of(place // 2 * tile, tile)
    right = pl.multiple_of(start + place % 2 * tile, tile)
    ref[pl.ds(down, tile), pl.ds(right, tile)] += block


def add_band_blocks(ref, blocks, width):
    for b in blocks:
        tile = b.shape[2]
        for i in range(b.shape[0]):
            for owner in range(2):
                tag = b[i, 2 * tile + 8 * owner : 2 * tile + 8 * owner + 8, :]
                block = b[i, owner * tile : (owner + 1) * tile, :]
                add_block(ref, block, place_of(tag), tile, owner * width)


def square_ids(n):
    return lax.broadcasted_iota(jnp.int32, (n, n), 0), lax.broadcasted_iota(jnp.int32, (n, n), 1)


def pack(ref, s):
    n = s.shape[0] // 2
    row, col = square_ids(n)
    ref[:n, :] = jnp.where(row >= col, s[:n, :n], s[n:, n:])
    ref[n : 2 * n, :] = s[n:, :n]
    diag = jnp.sum(jnp.where(row == col, s[n:, n:], 0.0), 0, keepdims=True)
    ref[2 * n : 2 * n + 8, :] = jnp.broadcast_to(diag, (8, n))


def unpack(ref):
    n = ref.shape[1]
    row, col = square_ids(n)
    both, low = ref[:n, :], ref[n : 2 * n, :]
    turned = both.T
    s00 = jnp.where(row >= col, both, turned)
    s11 = jnp.where(row < col, both, jnp.where(row > col, turned, ref[2 * n : 2 * n + 1, :]))
    return jnp.concatenate(
        [jnp.concatenate([s00, low.T], 1), jnp.concatenate([low, s11], 1)], 0
    )


def put_rows(ref, start, rows):
    n = ref.shape[1]
    ref[start : start + n, :] = rows[:, :n]
    ref[start + n : start + 2 * n, :] = rows[:, n:]


def get_rows(ref, start):
    n = ref.shape[1]
    return jnp.concatenate([ref[start : start + n, :], ref[start + n : start + 2 * n, :]], 1)


def sort_kernel(owner, slot, info, updates, front, out_ref, pay_ref, diag_ref):
    sends, tile = updates.shape[:2]
    width = front.shape[1]
    out_ref[...] = jnp.zeros_like(out_ref)
    for j in range(sends):
        out_ref[owner[j], :tile, :] = updates[j]
        out_ref[owner[j], tile:, :] = jnp.full((8, tile), slot[j].astype(F32))
    for o in range(2):
        pay_ref[o * tile : (o + 1) * tile, :] = out_ref[o, :tile, :]
        pay_ref[2 * tile + 8 * o : 2 * tile + 8 * o + 8, :] = out_ref[o, tile:, :]

    @pl.when(info[3] == 0)
    def _():
        pack(diag_ref, front[:width, :])
        put_rows(diag_ref, width + 8, front[width : width + tile, :])

    @pl.when(info[3] == 1)
    def _():
        pack(diag_ref, front[width:, :])
        put_rows(diag_ref, width + 8, front[:width, tile:].T)


def rows_kernel(info, front, turned, diag, d1, d2, d3, here, there, diag_ref, out_ref, band, part):
    width = front.shape[1]
    tile = width // 2
    group, layer, core = info[0], info[1], info[2]

    @pl.when((group == 0) | (group == layer))
    def _():
        band[...] = jnp.zeros_like(band)
        add_band_blocks(band, (here, there), width)

    @pl.when(group == 0)
    def _():
        for z, d in enumerate((diag, d1, d2, d3)):

            @pl.when(layer == z)
            def _(d=d):
                diag_ref[...] = d[...]

        @pl.when(core == 0)
        def _():
            pack(part, symmetric(band[:width, :width]))
            put_rows(part, width + 8, band[width : width + tile, :width])

        @pl.when(core == 1)
        def _():
            pack(part, symmetric(band[width:, width:]))
            put_rows(part, width + 8, band[width + tile :, :width])

        diag_ref[...] += part[...]

    @pl.when((group == layer) & (group > 0))
    def _():
        start = pl.multiple_of(core * width, width)
        out_ref[...] = turned[...].T + band[pl.ds(start, width), :]


def first_kernel(info, here, there, w_ref, l_ref, top, bottom):
    tile = here.shape[1]
    width = 2 * tile

    @pl.when(info[2] == 0)
    def _():
        top[...] = here[...]
        bottom[...] = there[...]

    @pl.when(info[2] == 1)
    def _():
        top[...] = there[...]
        bottom[...] = here[...]

    store_inverse(w_ref, factor_pair(unpack(top)))
    w = w_ref[...]
    l_ref[:tile, :] = dot_t(get_rows(top, width + 8), w)
    l_ref[tile:, :] = dot_t(get_rows(bottom, width + 8), w)


def second_kernel(info, here, there, lower, w_ref, bottom):
    @pl.when(info[2] == 0)
    def _():
        bottom[...] = there[...]

    @pl.when(info[2] == 1)
    def _():
        bottom[...] = here[...]

    store_inverse(w_ref, factor_pair(unpack(bottom) - dot_t(lower[...], lower[...])))


def middle_kernel(
    info, shard, arrived, piece, piece2, matched, m1, m2, m3, w, lower, here, there, out_ref, q_ref, n_ref, band, line
):
    tile = arrived.shape[2]
    nrows, width = shard.shape
    group, layer, core, column = info[0], info[1], info[2], info[4]
    out_ref[...] = shard[...]
    for i in range(arrived.shape[0]):
        add_block(out_ref, arrived[i, :tile, :], place_of(arrived[i, tile:, :]), tile)
    for k, m in enumerate((matched, m1, m2, m3)):

        @pl.when((group ^ layer) == k)
        def _(m=m):
            line[...] = m[...]

    w1, l21 = w[...], lower[...]
    by_rows = ((group >= 2) & (layer >= 2)) | (group == layer)
    for c, (same, swapped) in enumerate(((piece, piece2), (piece2, piece))):

        @pl.when(by_rows & (core == 0))
        def _(c=c, p=same):
            band[c * width : (c + 1) * width, :] = p[...].T

        @pl.when(by_rows & (core == 1))
        def _(c=c, p=swapped):
            band[c * width : (c + 1) * width, :] = p[...].T

        @pl.when(~by_rows & (core == 0))
        def _(c=c, p=same):
            band[:, c * width : (c + 1) * width] = p[...]

        @pl.when(~by_rows & (core == 1))
        def _(c=c, p=swapped):
            band[:, c * width : (c + 1) * width] = p[...]

    add_band_blocks(band, (here, there), width)

    @pl.when(column == 0)
    def _():
        out_ref[...] = dot_t(out_ref[...], w1)
        q_ref[...] = jnp.zeros_like(q_ref)
        n_ref[...] = jnp.zeros_like(n_ref)

    @pl.when(column > 0)
    def _():
        @pl.when(group == 0)
        def _():
            q_ref[:width, :] = jnp.zeros((width, width), F32)
            q_ref[width:, :] = l21

        @pl.when(group > 0)
        def _():
            q_ref[...] = dot_t(band[:, :width], w1)

        @pl.when(column == 1)
        def _():
            q_ref[...] = out_ref[...] - dot_t(q_ref[...], l21)
            n_ref[...] = jnp.zeros_like(n_ref)

        @pl.when(column > 1)
        def _():
            mine = dot_t(line[:, :width], w1)
            n_ref[...] = line[:, width:] - dot_t(mine, l21)
            out_ref[...] = out_ref[...] - dot_t(q_ref[...], mine)
            q_ref[...] = band[:, width:] - dot_t(q_ref[...], l21)


def last_kernel(info, out1, q, n, w, out_ref):
    nrows, width = out1.shape
    group, column = info[0], info[4]

    @pl.when((column == 0) | ((column > 1) & (group == 0)))
    def _():
        out_ref[...] = out1[...]

    @pl.when(column == 1)
    def _():
        rows = group * nrows + lax.broadcasted_iota(jnp.int32, (nrows, width), 0)
        out_ref[...] = jnp.where(rows >= width, dot_t(q[...], w[...]), out1[...])

    @pl.when((column > 1) & (group > 0))
    def _():
        second = dot_t(q[...], w[...])
        out_ref[...] = out1[...] - dot_t(second, dot_t(n[...], w[...]))


def kernel(body, outs, args, smem=1, scratch=(), flops=1 << 20):
    spec = [pl.BlockSpec(memory_space=pltpu.SMEM)] * smem
    spec += [pl.BlockSpec(memory_space=pltpu.VMEM)] * (len(args) - smem)
    return pl.pallas_call(
        body,
        out_shape=outs,
        in_specs=spec,
        scratch_shapes=[pltpu.VMEM(s, F32) for s in scratch],
        compiler_params=pltpu.CompilerParams(vmem_limit_bytes=VMEM_LIMIT),
        cost_estimate=pl.CostEstimate(flops=flops, bytes_accessed=1 << 20, transcendentals=0),
    )(*args)


def aligned(front, updates, target_owner, target_slot):
    nrows, width = front.shape
    tile = updates.shape[1]
    nleaf, nfront = lax.axis_size("leaf"), lax.axis_size("front")
    groups, layers = range(nleaf), range(nfront // 2)
    group, column = lax.axis_index("leaf"), lax.axis_index("front")
    layer, core = column // 2, column % 2
    info = jnp.stack([group, layer, core, group * nfront + column, column]).astype(jnp.int32)

    def dev(g, z, c):
        return g * nfront + 2 * z + c

    def send(x, pairs):
        return lax.ppermute(x, AXES, pairs)

    def out(*shape):
        return jax.ShapeDtypeStruct(shape, F32)

    both = range(2)
    swap = [(dev(g, z, c), dev(g, z, 1 - c)) for g in groups for z in layers for c in both]

    packed = out(2 * width + 8, tile)
    outgoing, payload, diag = kernel(
        sort_kernel,
        (out(nfront, tile + 8, tile), out(2 * tile + 16, tile), packed),
        (target_owner, target_slot, info, updates, front),
        smem=3,
    )
    diags = [send(diag, [(dev(0, 0, c), dev(0, s, c)) for c in both]) for s in layers[1:]]
    turned = send(front, [(dev(0, z, c), dev(z, z, c)) for z in layers[1:] for c in both])
    near = send(
        front, [(dev(g, 0, c), dev(g, z, c)) for g, z in ((1, 2), (2, 1), (3, 1)) for c in both]
    )
    here = lax.all_gather(
        payload, "front", axis_index_groups=[[2 * z + c for z in layers] for c in both]
    )
    there = send(here, swap)

    diag, matched = kernel(
        rows_kernel,
        (packed, out(width, 2 * width)),
        (info, front, turned, diag, *diags, here, there),
        scratch=[(nrows, 2 * width), packed.shape],
    )
    got = [
        send(diag, [(dev(0, z, c), dev(s, z, c)) for z in layers for c in both]) for s in groups[1:]
    ]
    away = [
        send(matched, [(dev(z, z, c), dev(z ^ s, z, c)) for z in layers[1:] for c in both])
        for s in groups[1:]
    ]
    diag = jnp.where(group == 0, diag, got[0] + got[1] + got[2])
    diag2 = send(diag, swap)

    far = send(
        jnp.where(group == layer, turned, near),
        [(dev(g, z, c), dev(g, 5 - z, c)) for g, z in ((1, 2), (2, 2), (3, 3)) for c in both],
    )
    piece = jnp.where(layer == 0, front, jnp.where(group == layer, turned, near + far))
    piece2 = send(piece, swap)
    arrived = lax.all_to_all(outgoing, "front", split_axis=0, concat_axis=0, tiled=True)

    square = out(width, width)
    w1, l21 = kernel(
        first_kernel, (square, square), (info, diag, diag2), scratch=[packed.shape] * 2, flops=1 << 32
    )
    w2 = kernel(second_kernel, square, (info, diag, diag2, l21), scratch=[packed.shape], flops=1 << 32)
    out1, q, n = kernel(
        middle_kernel,
        (out(nrows, width), out(nrows, width), square),
        (info, front, arrived, piece, piece2, matched, *away, w1, l21, here, there),
        scratch=[(nrows, 2 * width), (width, 2 * width)],
        flops=1 << 31,
    )
    return kernel(last_kernel, out(nrows, width), (info, out1, q, n, w2), flops=1 << 30)


def solution(mesh):
    nleaf, nfront = mesh.shape["leaf"], mesh.shape["front"]

    def shards(front, updates, target_owner, target_slot):
        nrows, width = front.shape
        tile = updates.shape[1]
        lines_up = (
            nrows == 2 * width
            and width == 2 * tile
            and nleaf == 4
            and nfront == 8
        )
        plan = aligned if lines_up else general
        return plan(front, updates, target_owner, target_slot)

    return jax.shard_map(
        shards,
        mesh=mesh,
        in_specs=(
            P("leaf", "front"),
            P(("leaf", "front"), None, None),
            P(("leaf", "front")),
            P(("leaf", "front")),
        ),
        out_specs=P("leaf", "front"),
        check_vma=False,
    )
```

```python
import functools

import jax
import jax.numpy as jnp
from jax import lax
from jax.experimental import pallas as pl
from jax.experimental.pallas import tpu as pltpu
from jax.sharding import PartitionSpec as P

F32 = jnp.float32
BF16 = jnp.bfloat16
AXES = ("leaf", "front")
EXACT = lax.Precision.HIGHEST
VMEM_LIMIT = 40 * 1024 * 1024


def spread(value, axis, source):
    kept = jnp.where(lax.axis_index(axis) == source, value, 0).astype(value.dtype)
    return lax.psum(kept, axis)


def assemble(front, updates, target_owner, target_slot):
    nrows, width = front.shape
    tile = updates.shape[1]
    nfront = lax.axis_size("front")
    buffer = jnp.zeros((nfront, tile, tile), F32).at[target_owner].set(updates)
    labels = jnp.zeros((nfront,), F32).at[target_owner].set(target_slot.astype(F32))
    arrived, places = (
        lax.all_to_all(buffer, "front", split_axis=0, concat_axis=0, tiled=True),
        lax.all_to_all(labels, "front", split_axis=0, concat_axis=0, tiled=True),
    )
    places = places.astype(jnp.int32)
    col_tiles = width // tile
    grid = front.reshape(nrows // tile, tile, col_tiles, tile)
    grid = grid.at[places // col_tiles, :, places % col_tiles, :].add(arrived)
    return grid.reshape(nrows, width)


def eliminate(shard, panel, start, row_ids, col_ids, column):
    nrows, width = panel.shape
    diag = spread(panel[start : start + width], "leaf", 0)
    chol = jnp.linalg.cholesky(diag)
    eye = jnp.eye(width, dtype=F32)
    inverse = lax.linalg.triangular_solve(chol, eye, left_side=True, lower=True)
    prod = jnp.dot(panel, inverse.T, precision=EXACT)
    lower = jnp.where(row_ids[:, None] >= start, prod, panel)
    owner_row = column * width // nrows
    offset = column * width - owner_row * nrows
    mine = lax.dynamic_slice_in_dim(lower, offset, width, 0)
    across = spread(mine, "leaf", owner_row)
    trail = jnp.where(row_ids[:, None] >= start + width, lower, 0.0)
    updated = shard - jnp.dot(trail, across.T, precision=EXACT)
    updated = jnp.where(col_ids[None, :] >= start + width, updated, shard)
    return (jnp.where(column == start // width, lower, updated), lower)


def general(front, updates, target_owner, target_slot):
    nrows, width = front.shape
    column = lax.axis_index("front")
    row_ids = lax.axis_index("leaf") * nrows + jnp.arange(nrows, dtype=jnp.int32)
    col_ids = column * width + jnp.arange(width, dtype=jnp.int32)
    shard = assemble(front, updates, target_owner, target_slot)
    first = spread(shard, "front", 0)
    shard, lower = eliminate(shard, first, 0, row_ids, col_ids, column)
    second = spread(shard, "front", 1)
    shard, lower = eliminate(shard, second, width, row_ids, col_ids, column)
    return shard


def lane_of(x, c):
    return jnp.take_along_axis(x, jnp.full(x.shape, c, jnp.int32), axis=1)


def row_of(x, i):
    return jnp.broadcast_to(x[i : i + 1, :], x.shape)


def parts(x):
    high = x.astype(BF16).astype(F32)
    rest = x - high
    mid = rest.astype(BF16).astype(F32)
    return high, mid, (rest - mid).astype(BF16).astype(F32)


def factor_inverse(a):
    n = a.shape[0]
    panels, per, ahead = n // 8, 2, 2
    sub = lax.broadcasted_iota(jnp.int32, (8, n), 0)
    lane = lax.broadcasted_iota(jnp.int32, (8, n), 1)
    work = [
        [a[8 * k : 8 * k + 8, :], jnp.where(lane == sub + 8 * k, 1.0, 0.0).astype(F32)]
        for k in range(panels)
    ]
    out, held = [], []
    for k in range(panels):
        rows, ident = work[k]
        cols = [lane_of(rows, 8 * k + j) for j in range(8)]
        d = {(i, j): row_of(cols[j], i) for j in range(8) for i in range(j, 8)}
        up = [row_of(rows, j) for j in range(8)]
        inv = [row_of(ident, j) for j in range(8)]
        last = min(panels - 1, (k // per + 1) * per - 1 + ahead)
        below = {
            b: [lane_of(work[b][0], 8 * k + j) for j in range(8)]
            for b in range(k + 1, last + 1)
        }
        for j in range(8):
            r = lax.rsqrt(d[j, j])
            for i in range(j + 1, 8):
                d[i, j] = d[i, j] * r
            for i in range(j + 1, 8):
                for m in range(j + 1, i + 1):
                    d[i, m] = d[i, m] - d[i, j] * d[m, j]
            up[j] = up[j] * r
            inv[j] = inv[j] * r
            for i in range(j + 1, 8):
                up[i] = up[i] - d[i, j] * up[j]
                inv[i] = inv[i] - d[i, j] * inv[j]
            for b, c in below.items():
                c[j] = c[j] * r
                for i in range(j + 1, 8):
                    c[i] = c[i] - d[i, j] * c[j]
                work[b] = [work[b][0] - c[j] * up[j], work[b][1] - c[j] * inv[j]]
        u, w = up[0], inv[0]
        for j in range(1, 8):
            u = jnp.where(sub == j, up[j], u)
            w = jnp.where(sub == j, inv[j], w)
        out.append(w)
        held.append((u, w))
        first = k + 1 + ahead
        if k % per == per - 1 and first < panels:
            us = jnp.concatenate([p[0] for p in held], 0)
            ws = jnp.concatenate([p[1] for p in held], 0)
            uh, um, ul = parts(us)
            wh, wm, wl = parts(ws)
            right = jnp.concatenate(
                [
                    jnp.concatenate([uh, um, ul, uh, um, uh], 0),
                    jnp.concatenate([wh, wm, wl, wh, wm, wh], 0),
                ],
                1,
            ).astype(BF16)
            left = jnp.concatenate([uh, uh, uh, um, um, ul], 0).T
            left = left[8 * first :, :].astype(BF16)
            change = jnp.dot(left, right, preferred_element_type=F32)
            for b in range(first, panels):
                part = change[8 * (b - first) : 8 * (b - first + 1), :]
                work[b] = [work[b][0] - part[:, :n], work[b][1] - part[:, n:]]
        if k % per == per - 1:
            held = []
    return jnp.concatenate(out, 0)


def dot(a, b):
    return jnp.dot(a, b, precision=EXACT, preferred_element_type=F32)


def dot_t(a, b):
    return lax.dot_general(
        a, b, (((1,), (1,)), ((), ())), precision=EXACT, preferred_element_type=F32
    )


def factor_pair(a):
    h = a.shape[0] // 2
    w11 = factor_inverse(a[:h, :h])
    l21 = dot_t(a[h:, :h], w11)
    w22 = factor_inverse(a[h:, h:] - dot_t(l21, l21))
    w21 = -dot(w22, dot(l21, w11))
    return w11, w21, w22


def store_inverse(ref, blocks):
    w11, w21, w22 = blocks
    h = w11.shape[0]
    ref[:h, :h] = w11
    ref[:h, h:] = jnp.zeros_like(w11)
    ref[h:, :h] = w21
    ref[h:, h:] = w22


def symmetric(a):
    return (a + a.T) * 0.5


def place_of(tags):
    return tags[0, 0].astype(jnp.int32)


def add_block(ref, block, place, tile, start=0):
    down = pl.multiple_of(place // 2 * tile, tile)
    right = pl.multiple_of(start + place % 2 * tile, tile)
    ref[pl.ds(down, tile), pl.ds(right, tile)] += block


def add_band_blocks(ref, blocks, width):
    tile = blocks.shape[2]
    for i in range(blocks.shape[0]):
        for owner in range(2):
            tag = blocks[i, 2 * tile + 8 * owner : 2 * tile + 8 * owner + 8, :]
            block = blocks[i, owner * tile : (owner + 1) * tile, :]
            add_block(ref, block, place_of(tag), tile, owner * width)


def square_ids(n):
    return lax.broadcasted_iota(jnp.int32, (n, n), 0), lax.broadcasted_iota(jnp.int32, (n, n), 1)


def pack(ref, s):
    n = s.shape[0] // 2
    row, col = square_ids(n)
    ref[:n, :] = jnp.where(row >= col, s[:n, :n], s[n:, n:])
    ref[n : 2 * n, :] = s[n:, :n]
    diag = jnp.sum(jnp.where(row == col, s[n:, n:], 0.0), 0, keepdims=True)
    ref[2 * n : 2 * n + 8, :] = jnp.broadcast_to(diag, (8, n))


def unpack(ref):
    n = ref.shape[1]
    row, col = square_ids(n)
    both, low = ref[:n, :], ref[n : 2 * n, :]
    turned = both.T
    s00 = jnp.where(row >= col, both, turned)
    s11 = jnp.where(row < col, both, jnp.where(row > col, turned, ref[2 * n : 2 * n + 1, :]))
    return jnp.concatenate(
        [jnp.concatenate([s00, low.T], 1), jnp.concatenate([low, s11], 1)], 0
    )


def put_rows(ref, start, rows):
    n = ref.shape[1]
    ref[start : start + n, :] = rows[:, :n]
    ref[start + n : start + 2 * n, :] = rows[:, n:]


def get_rows(ref, start):
    n = ref.shape[1]
    return jnp.concatenate([ref[start : start + n, :], ref[start + n : start + 2 * n, :]], 1)


def sort_kernel(owner, slot, info, updates, front, out_ref, pay_ref, diag_ref):
    sends, tile = updates.shape[:2]
    width = front.shape[1]
    out_ref[...] = jnp.zeros_like(out_ref)
    for j in range(sends):
        out_ref[owner[j], :tile, :] = updates[j]
        out_ref[owner[j], tile:, :] = jnp.full((8, tile), slot[j].astype(F32))
    for o in range(2):
        pay_ref[o * tile : (o + 1) * tile, :] = out_ref[o, :tile, :]
        pay_ref[2 * tile + 8 * o : 2 * tile + 8 * o + 8, :] = out_ref[o, tile:, :]

    @pl.when(info[3] == 0)
    def _():
        pack(diag_ref, front[:width, :])
        put_rows(diag_ref, width + 8, front[width : width + tile, :])

    @pl.when(info[3] == 1)
    def _():
        pack(diag_ref, front[width:, :])
        put_rows(diag_ref, width + 8, front[:width, tile:].T)


def rows_kernel(info, front, turned, diag, d1, d2, d3, blocks, diag_ref, out_ref, band, part):
    width = front.shape[1]
    tile = width // 2
    group, layer, core = info[0], info[1], info[2]

    @pl.when((group == 0) | (group == layer))
    def _():
        band[...] = jnp.zeros_like(band)
        add_band_blocks(band, blocks, width)

    @pl.when(group == 0)
    def _():
        for z, d in enumerate((diag, d1, d2, d3)):

            @pl.when(layer == z)
            def _(d=d):
                diag_ref[...] = d[...]

        @pl.when(core == 0)
        def _():
            pack(part, symmetric(band[:width, :width]))
            put_rows(part, width + 8, band[width : width + tile, :width])

        @pl.when(core == 1)
        def _():
            pack(part, symmetric(band[width:, width:]))
            put_rows(part, width + 8, band[width + tile :, :width])

        diag_ref[...] += part[...]

    @pl.when((group == layer) & (group > 0))
    def _():
        start = pl.multiple_of(core * width, width)
        out_ref[...] = turned[...].T + band[pl.ds(start, width), :]


def first_kernel(info, here, there, w_ref, l_ref, top, bottom):
    tile = here.shape[1]
    width = 2 * tile

    @pl.when(info[2] == 0)
    def _():
        top[...] = here[...]
        bottom[...] = there[...]

    @pl.when(info[2] == 1)
    def _():
        top[...] = there[...]
        bottom[...] = here[...]

    store_inverse(w_ref, factor_pair(unpack(top)))
    w = w_ref[...]
    l_ref[:tile, :] = dot_t(get_rows(top, width + 8), w)
    l_ref[tile:, :] = dot_t(get_rows(bottom, width + 8), w)


def second_kernel(info, here, there, lower, w_ref, bottom):
    @pl.when(info[2] == 0)
    def _():
        bottom[...] = there[...]

    @pl.when(info[2] == 1)
    def _():
        bottom[...] = here[...]

    store_inverse(w_ref, factor_pair(unpack(bottom) - dot_t(lower[...], lower[...])))


def middle_kernel(
    info, shard, arrived, piece, piece2, matched, m1, m2, m3, w, lower, blocks, out_ref, q_ref, n_ref, band, line
):
    tile = arrived.shape[2]
    nrows, width = shard.shape
    group, layer, core, column = info[0], info[1], info[2], info[4]
    out_ref[...] = shard[...]
    for i in range(arrived.shape[0]):
        add_block(out_ref, arrived[i, :tile, :], place_of(arrived[i, tile:, :]), tile)
    for k, m in enumerate((matched, m1, m2, m3)):

        @pl.when((group ^ layer) == k)
        def _(m=m):
            line[...] = m[...]

    w1, l21 = w[...], lower[...]
    by_rows = ((group >= 2) & (layer >= 2)) | (group == layer)
    for c, (same, swapped) in enumerate(((piece, piece2), (piece2, piece))):

        @pl.when(by_rows & (core == 0))
        def _(c=c, p=same):
            band[c * width : (c + 1) * width, :] = p[...].T

        @pl.when(by_rows & (core == 1))
        def _(c=c, p=swapped):
            band[c * width : (c + 1) * width, :] = p[...].T

        @pl.when(~by_rows & (core == 0))
        def _(c=c, p=same):
            band[:, c * width : (c + 1) * width] = p[...]

        @pl.when(~by_rows & (core == 1))
        def _(c=c, p=swapped):
            band[:, c * width : (c + 1) * width] = p[...]

    add_band_blocks(band, blocks, width)

    @pl.when(column == 0)
    def _():
        out_ref[...] = dot_t(out_ref[...], w1)
        q_ref[...] = jnp.zeros_like(q_ref)
        n_ref[...] = jnp.zeros_like(n_ref)

    @pl.when(column > 0)
    def _():
        @pl.when(group == 0)
        def _():
            q_ref[:width, :] = jnp.zeros((width, width), F32)
            q_ref[width:, :] = l21

        @pl.when(group > 0)
        def _():
            q_ref[...] = dot_t(band[:, :width], w1)

        @pl.when(column == 1)
        def _():
            q_ref[...] = out_ref[...] - dot_t(q_ref[...], l21)
            n_ref[...] = jnp.zeros_like(n_ref)

        @pl.when(column > 1)
        def _():
            mine = dot_t(line[:, :width], w1)
            n_ref[...] = line[:, width:] - dot_t(mine, l21)
            out_ref[...] = out_ref[...] - dot_t(q_ref[...], mine)
            q_ref[...] = band[:, width:] - dot_t(q_ref[...], l21)


def last_kernel(info, out1, q, n, w, out_ref):
    nrows, width = out1.shape
    group, column = info[0], info[4]

    @pl.when((column == 0) | ((column > 1) & (group == 0)))
    def _():
        out_ref[...] = out1[...]

    @pl.when(column == 1)
    def _():
        rows = group * nrows + lax.broadcasted_iota(jnp.int32, (nrows, width), 0)
        out_ref[...] = jnp.where(rows >= width, dot_t(q[...], w[...]), out1[...])

    @pl.when((column > 1) & (group > 0))
    def _():
        second = dot_t(q[...], w[...])
        out_ref[...] = out1[...] - dot_t(second, dot_t(n[...], w[...]))


def kernel(body, outs, args, smem=1, scratch=(), flops=1 << 20):
    spec = [pl.BlockSpec(memory_space=pltpu.SMEM)] * smem
    spec += [pl.BlockSpec(memory_space=pltpu.VMEM)] * (len(args) - smem)
    return pl.pallas_call(
        body,
        out_shape=outs,
        in_specs=spec,
        scratch_shapes=[pltpu.VMEM(s, F32) for s in scratch],
        compiler_params=pltpu.CompilerParams(vmem_limit_bytes=VMEM_LIMIT),
        cost_estimate=pl.CostEstimate(flops=flops, bytes_accessed=1 << 20, transcendentals=0),
    )(*args)


def aligned(front, updates, target_owner, target_slot):
    nrows, width = front.shape
    tile = updates.shape[1]
    nleaf, nfront = lax.axis_size("leaf"), lax.axis_size("front")
    groups, layers = range(nleaf), range(nfront // 2)
    group, column = lax.axis_index("leaf"), lax.axis_index("front")
    layer, core = column // 2, column % 2
    info = jnp.stack([group, layer, core, group * nfront + column, column]).astype(jnp.int32)

    def dev(g, z, c):
        return g * nfront + 2 * z + c

    def send(x, pairs):
        return lax.ppermute(x, AXES, pairs)

    def out(*shape):
        return jax.ShapeDtypeStruct(shape, F32)

    both = range(2)
    swap = [(dev(g, z, c), dev(g, z, 1 - c)) for g in groups for z in layers for c in both]

    packed = out(2 * width + 8, tile)
    outgoing, payload, diag = kernel(
        sort_kernel,
        (out(nfront, tile + 8, tile), out(2 * tile + 16, tile), packed),
        (target_owner, target_slot, info, updates, front),
        smem=3,
    )
    diags = [send(diag, [(dev(0, 0, c), dev(0, s, c)) for c in both]) for s in layers[1:]]
    turned = send(front, [(dev(0, z, c), dev(z, z, c)) for z in layers[1:] for c in both])
    near = send(
        front, [(dev(g, 0, c), dev(g, z, c)) for g, z in ((1, 2), (2, 1), (3, 1)) for c in both]
    )
    blocks = lax.all_gather(payload, "front")
    arrived = lax.all_to_all(outgoing, "front", split_axis=0, concat_axis=0, tiled=True)
    blocks, turned, near, arrived, *diags = lax.optimization_barrier(
        (blocks, turned, near, arrived, *diags)
    )

    diag, matched = kernel(
        rows_kernel,
        (packed, out(width, 2 * width)),
        (info, front, turned, diag, *diags, blocks),
        scratch=[(nrows, 2 * width), packed.shape],
    )
    got = [
        send(diag, [(dev(0, z, c), dev(s, z, c)) for z in layers for c in both]) for s in groups[1:]
    ]
    away = [
        send(matched, [(dev(z, z, c), dev(z ^ s, z, c)) for z in layers[1:] for c in both])
        for s in groups[1:]
    ]
    far = send(
        jnp.where(group == layer, turned, near),
        [(dev(g, z, c), dev(g, 5 - z, c)) for g, z in ((1, 2), (2, 2), (3, 3)) for c in both],
    )
    diag = jnp.where(group == 0, diag, got[0] + got[1] + got[2])
    diag2 = send(diag, swap)
    diag, diag2, far = lax.optimization_barrier((diag, diag2, far))

    piece = jnp.where(layer == 0, front, jnp.where(group == layer, turned, near + far))
    piece2 = send(piece, swap)

    square = out(width, width)
    w1, l21 = kernel(
        first_kernel, (square, square), (info, diag, diag2), scratch=[packed.shape] * 2, flops=1 << 32
    )
    w2 = kernel(second_kernel, square, (info, diag, diag2, l21), scratch=[packed.shape], flops=1 << 32)
    out1, q, n = kernel(
        middle_kernel,
        (out(nrows, width), out(nrows, width), square),
        (info, front, arrived, piece, piece2, matched, *away, w1, l21, blocks),
        scratch=[(nrows, 2 * width), (width, 2 * width)],
        flops=1 << 31,
    )
    return kernel(last_kernel, out(nrows, width), (info, out1, q, n, w2), flops=1 << 30)


def solution(mesh):
    nleaf, nfront = mesh.shape["leaf"], mesh.shape["front"]

    def shards(front, updates, target_owner, target_slot):
        nrows, width = front.shape
        tile = updates.shape[1]
        lines_up = (
            nrows == 2 * width
            and width == 2 * tile
            and nleaf == 4
            and nfront == 8
        )
        plan = aligned if lines_up else general
        return plan(front, updates, target_owner, target_slot)

    return jax.shard_map(
        shards,
        mesh=mesh,
        in_specs=(
            P("leaf", "front"),
            P(("leaf", "front"), None, None),
            P(("leaf", "front")),
            P(("leaf", "front")),
        ),
        out_specs=P("leaf", "front"),
        check_vma=False,
    )
```

```python
import functools

import jax
import jax.numpy as jnp
from jax import lax
from jax.experimental import pallas as pl
from jax.experimental.pallas import tpu as pltpu
from jax.sharding import PartitionSpec as P

F32 = jnp.float32
BF16 = jnp.bfloat16
AXES = ("leaf", "front")
EXACT = lax.Precision.HIGHEST
VMEM_LIMIT = 40 * 1024 * 1024


def spread(value, axis, source):
    kept = jnp.where(lax.axis_index(axis) == source, value, 0).astype(value.dtype)
    return lax.psum(kept, axis)


def assemble(front, updates, target_owner, target_slot):
    nrows, width = front.shape
    tile = updates.shape[1]
    nfront = lax.axis_size("front")
    buffer = jnp.zeros((nfront, tile, tile), F32).at[target_owner].set(updates)
    labels = jnp.zeros((nfront,), F32).at[target_owner].set(target_slot.astype(F32))
    arrived, places = (
        lax.all_to_all(buffer, "front", split_axis=0, concat_axis=0, tiled=True),
        lax.all_to_all(labels, "front", split_axis=0, concat_axis=0, tiled=True),
    )
    places = places.astype(jnp.int32)
    col_tiles = width // tile
    grid = front.reshape(nrows // tile, tile, col_tiles, tile)
    grid = grid.at[places // col_tiles, :, places % col_tiles, :].add(arrived)
    return grid.reshape(nrows, width)


def eliminate(shard, panel, start, row_ids, col_ids, column):
    nrows, width = panel.shape
    diag = spread(panel[start : start + width], "leaf", 0)
    chol = jnp.linalg.cholesky(diag)
    eye = jnp.eye(width, dtype=F32)
    inverse = lax.linalg.triangular_solve(chol, eye, left_side=True, lower=True)
    prod = jnp.dot(panel, inverse.T, precision=EXACT)
    lower = jnp.where(row_ids[:, None] >= start, prod, panel)
    owner_row = column * width // nrows
    offset = column * width - owner_row * nrows
    mine = lax.dynamic_slice_in_dim(lower, offset, width, 0)
    across = spread(mine, "leaf", owner_row)
    trail = jnp.where(row_ids[:, None] >= start + width, lower, 0.0)
    updated = shard - jnp.dot(trail, across.T, precision=EXACT)
    updated = jnp.where(col_ids[None, :] >= start + width, updated, shard)
    return (jnp.where(column == start // width, lower, updated), lower)


def general(front, updates, target_owner, target_slot):
    nrows, width = front.shape
    column = lax.axis_index("front")
    row_ids = lax.axis_index("leaf") * nrows + jnp.arange(nrows, dtype=jnp.int32)
    col_ids = column * width + jnp.arange(width, dtype=jnp.int32)
    shard = assemble(front, updates, target_owner, target_slot)
    first = spread(shard, "front", 0)
    shard, lower = eliminate(shard, first, 0, row_ids, col_ids, column)
    second = spread(shard, "front", 1)
    shard, lower = eliminate(shard, second, width, row_ids, col_ids, column)
    return shard


def lane_of(x, c):
    return jnp.take_along_axis(x, jnp.full(x.shape, c, jnp.int32), axis=1)


def row_of(x, i):
    return jnp.broadcast_to(x[i : i + 1, :], x.shape)


def parts(x):
    high = x.astype(BF16).astype(F32)
    rest = x - high
    mid = rest.astype(BF16).astype(F32)
    return high, mid, (rest - mid).astype(BF16).astype(F32)


def factor_inverse(a):
    n = a.shape[0]
    panels, per, ahead = n // 8, 2, 2
    sub = lax.broadcasted_iota(jnp.int32, (8, n), 0)
    lane = lax.broadcasted_iota(jnp.int32, (8, n), 1)
    work = [
        [a[8 * k : 8 * k + 8, :], jnp.where(lane == sub + 8 * k, 1.0, 0.0).astype(F32)]
        for k in range(panels)
    ]
    out, held = [], []
    for k in range(panels):
        rows, ident = work[k]
        cols = [lane_of(rows, 8 * k + j) for j in range(8)]
        d = {(i, j): row_of(cols[j], i) for j in range(8) for i in range(j, 8)}
        up = [row_of(rows, j) for j in range(8)]
        inv = [row_of(ident, j) for j in range(8)]
        last = min(panels - 1, (k // per + 1) * per - 1 + ahead)
        below = {
            b: [lane_of(work[b][0], 8 * k + j) for j in range(8)]
            for b in range(k + 1, last + 1)
        }
        for j in range(8):
            r = lax.rsqrt(d[j, j])
            for i in range(j + 1, 8):
                d[i, j] = d[i, j] * r
            for i in range(j + 1, 8):
                for m in range(j + 1, i + 1):
                    d[i, m] = d[i, m] - d[i, j] * d[m, j]
            up[j] = up[j] * r
            inv[j] = inv[j] * r
            for i in range(j + 1, 8):
                up[i] = up[i] - d[i, j] * up[j]
                inv[i] = inv[i] - d[i, j] * inv[j]
            for b, c in below.items():
                c[j] = c[j] * r
                for i in range(j + 1, 8):
                    c[i] = c[i] - d[i, j] * c[j]
                work[b] = [work[b][0] - c[j] * up[j], work[b][1] - c[j] * inv[j]]
        u, w = up[0], inv[0]
        for j in range(1, 8):
            u = jnp.where(sub == j, up[j], u)
            w = jnp.where(sub == j, inv[j], w)
        out.append(w)
        held.append((u, w))
        first = k + 1 + ahead
        if k % per == per - 1 and first < panels:
            us = jnp.concatenate([p[0] for p in held], 0)
            ws = jnp.concatenate([p[1] for p in held], 0)
            uh, um, ul = parts(us)
            wh, wm, wl = parts(ws)
            right = jnp.concatenate(
                [
                    jnp.concatenate([uh, um, ul, uh, um, uh], 0),
                    jnp.concatenate([wh, wm, wl, wh, wm, wh], 0),
                ],
                1,
            ).astype(BF16)
            left = jnp.concatenate([uh, uh, uh, um, um, ul], 0).T
            left = left[8 * first :, :].astype(BF16)
            change = jnp.dot(left, right, preferred_element_type=F32)
            for b in range(first, panels):
                part = change[8 * (b - first) : 8 * (b - first + 1), :]
                work[b] = [work[b][0] - part[:, :n], work[b][1] - part[:, n:]]
        if k % per == per - 1:
            held = []
    return jnp.concatenate(out, 0)


def dot(a, b):
    return jnp.dot(a, b, precision=EXACT, preferred_element_type=F32)


def dot_t(a, b):
    return lax.dot_general(
        a, b, (((1,), (1,)), ((), ())), precision=EXACT, preferred_element_type=F32
    )


def factor_pair(a):
    h = a.shape[0] // 2
    w11 = factor_inverse(a[:h, :h])
    l21 = dot_t(a[h:, :h], w11)
    w22 = factor_inverse(a[h:, h:] - dot_t(l21, l21))
    w21 = -dot(w22, dot(l21, w11))
    return w11, w21, w22


def store_inverse(ref, blocks):
    w11, w21, w22 = blocks
    h = w11.shape[0]
    ref[:h, :h] = w11
    ref[:h, h:] = jnp.zeros_like(w11)
    ref[h:, :h] = w21
    ref[h:, h:] = w22


def symmetric(a):
    return (a + a.T) * 0.5


def place_of(tags):
    return tags[0, 0].astype(jnp.int32)


def add_block(ref, block, place, tile, start=0):
    down = pl.multiple_of(place // 2 * tile, tile)
    right = pl.multiple_of(start + place % 2 * tile, tile)
    ref[pl.ds(down, tile), pl.ds(right, tile)] += block


def add_band_blocks(ref, blocks, width):
    tile = blocks.shape[2]
    for i in range(blocks.shape[0]):
        for owner in range(2):
            tag = blocks[i, 2 * tile + 8 * owner : 2 * tile + 8 * owner + 8, :]
            block = blocks[i, owner * tile : (owner + 1) * tile, :]
            add_block(ref, block, place_of(tag), tile, owner * width)


def square_ids(n):
    return lax.broadcasted_iota(jnp.int32, (n, n), 0), lax.broadcasted_iota(jnp.int32, (n, n), 1)


def pack(ref, s):
    n = s.shape[0] // 2
    row, col = square_ids(n)
    ref[:n, :] = jnp.where(row >= col, s[:n, :n], s[n:, n:])
    ref[n : 2 * n, :] = s[n:, :n]
    diag = jnp.sum(jnp.where(row == col, s[n:, n:], 0.0), 0, keepdims=True)
    ref[2 * n : 2 * n + 8, :] = jnp.broadcast_to(diag, (8, n))


def unpack(ref):
    n = ref.shape[1]
    row, col = square_ids(n)
    both, low = ref[:n, :], ref[n : 2 * n, :]
    turned = both.T
    s00 = jnp.where(row >= col, both, turned)
    s11 = jnp.where(row < col, both, jnp.where(row > col, turned, ref[2 * n : 2 * n + 1, :]))
    return jnp.concatenate(
        [jnp.concatenate([s00, low.T], 1), jnp.concatenate([low, s11], 1)], 0
    )


def put_rows(ref, start, rows):
    n = ref.shape[1]
    ref[start : start + n, :] = rows[:, :n]
    ref[start + n : start + 2 * n, :] = rows[:, n:]


def get_rows(ref, start):
    n = ref.shape[1]
    return jnp.concatenate([ref[start : start + n, :], ref[start + n : start + 2 * n, :]], 1)


def sort_kernel(owner, slot, info, updates, front, out_ref, pay_ref, diag_ref):
    sends, tile = updates.shape[:2]
    width = front.shape[1]
    out_ref[...] = jnp.zeros_like(out_ref)
    for j in range(sends):
        out_ref[owner[j], :tile, :] = updates[j]
        out_ref[owner[j], tile:, :] = jnp.full((8, tile), slot[j].astype(F32))
    for o in range(2):
        pay_ref[o * tile : (o + 1) * tile, :] = out_ref[o, :tile, :]
        pay_ref[2 * tile + 8 * o : 2 * tile + 8 * o + 8, :] = out_ref[o, tile:, :]

    @pl.when(info[3] == 0)
    def _():
        pack(diag_ref, front[:width, :])
        put_rows(diag_ref, width + 8, front[width : width + tile, :])

    @pl.when(info[3] == 1)
    def _():
        pack(diag_ref, front[width:, :])
        put_rows(diag_ref, width + 8, front[:width, tile:].T)


def rows_kernel(info, front, turned, diag, d1, d2, d3, blocks, diag_ref, out_ref, band, part):
    width = front.shape[1]
    tile = width // 2
    group, layer, core = info[0], info[1], info[2]

    @pl.when((group == 0) | (group == layer))
    def _():
        band[...] = jnp.zeros_like(band)
        add_band_blocks(band, blocks, width)

    @pl.when(group == 0)
    def _():
        for z, d in enumerate((diag, d1, d2, d3)):

            @pl.when(layer == z)
            def _(d=d):
                diag_ref[...] = d[...]

        @pl.when(core == 0)
        def _():
            pack(part, symmetric(band[:width, :width]))
            put_rows(part, width + 8, band[width : width + tile, :width])

        @pl.when(core == 1)
        def _():
            pack(part, symmetric(band[width:, width:]))
            put_rows(part, width + 8, band[width + tile :, :width])

        diag_ref[...] += part[...]

    @pl.when((group == layer) & (group > 0))
    def _():
        start = pl.multiple_of(core * width, width)
        out_ref[...] = turned[...].T + band[pl.ds(start, width), :]


def factor_kernel(info, here, there, w_ref, l_ref, v_ref, top, bottom):
    tile = here.shape[1]
    width = 2 * tile

    @pl.when(info[2] == 0)
    def _():
        top[...] = here[...]
        bottom[...] = there[...]

    @pl.when(info[2] == 1)
    def _():
        top[...] = there[...]
        bottom[...] = here[...]

    store_inverse(w_ref, factor_pair(unpack(top)))
    w = w_ref[...]
    l_ref[:tile, :] = dot_t(get_rows(top, width + 8), w)
    l_ref[tile:, :] = dot_t(get_rows(bottom, width + 8), w)
    lower = l_ref[...]
    store_inverse(v_ref, factor_pair(unpack(bottom) - dot_t(lower, lower)))


def last_kernel(
    info, shard, arrived, piece, piece2, matched, m1, m2, m3, w, lower, v, blocks, out_ref, band, line, work
):
    tile = arrived.shape[2]
    nrows, width = shard.shape
    group, layer, core, column = info[0], info[1], info[2], info[4]
    out_ref[...] = shard[...]
    for i in range(arrived.shape[0]):
        add_block(out_ref, arrived[i, :tile, :], place_of(arrived[i, tile:, :]), tile)
    for k, m in enumerate((matched, m1, m2, m3)):

        @pl.when((group ^ layer) == k)
        def _(m=m):
            line[...] = m[...]

    w1, l21 = w[...], lower[...]
    by_rows = (layer > 0) & (((group == 1) & (layer < 3)) | ((group > 1) & (layer > 1)))
    for c, (same, swapped) in enumerate(((piece, piece2), (piece2, piece))):

        @pl.when(by_rows & (core == 0))
        def _(c=c, p=same):
            band[c * width : (c + 1) * width, :] = p[...].T

        @pl.when(by_rows & (core == 1))
        def _(c=c, p=swapped):
            band[c * width : (c + 1) * width, :] = p[...].T

        @pl.when(~by_rows & (core == 0))
        def _(c=c, p=same):
            band[:, c * width : (c + 1) * width] = p[...]

        @pl.when(~by_rows & (core == 1))
        def _(c=c, p=swapped):
            band[:, c * width : (c + 1) * width] = p[...]

    @pl.when(group > 0)
    def _():
        add_band_blocks(band, blocks, width)

    @pl.when(column == 0)
    def _():
        out_ref[...] = dot_t(out_ref[...], w1)

    @pl.when(column > 0)
    def _():
        @pl.when(group == 0)
        def _():
            work[:width, :] = jnp.zeros((width, width), F32)
            work[width:, :] = l21

        @pl.when(group > 0)
        def _():
            work[...] = dot_t(band[:, :width], w1)

        first = work[...]

        @pl.when(column == 1)
        def _():
            rows = group * nrows + lax.broadcasted_iota(jnp.int32, (nrows, width), 0)
            own = out_ref[...]
            out_ref[...] = jnp.where(rows >= width, dot_t(own - dot_t(first, l21), v[...]), own)

        @pl.when(column > 1)
        def _():
            mine = dot_t(line[:, :width], w1)
            out_ref[...] -= dot_t(first, mine)

            @pl.when(group > 0)
            def _():
                second = dot_t(band[:, width:] - dot_t(first, l21), v[...])
                out_ref[...] -= dot_t(second, dot_t(line[:, width:] - dot_t(mine, l21), v[...]))


def kernel(body, outs, args, smem=1, scratch=(), flops=1 << 20):
    spec = [pl.BlockSpec(memory_space=pltpu.SMEM)] * smem
    spec += [pl.BlockSpec(memory_space=pltpu.VMEM)] * (len(args) - smem)
    return pl.pallas_call(
        body,
        out_shape=outs,
        in_specs=spec,
        scratch_shapes=[pltpu.VMEM(s, F32) for s in scratch],
        compiler_params=pltpu.CompilerParams(vmem_limit_bytes=VMEM_LIMIT),
        cost_estimate=pl.CostEstimate(flops=flops, bytes_accessed=1 << 20, transcendentals=0),
    )(*args)


def aligned(front, updates, target_owner, target_slot):
    nrows, width = front.shape
    tile = updates.shape[1]
    nleaf, nfront = lax.axis_size("leaf"), lax.axis_size("front")
    groups, layers = range(nleaf), range(nfront // 2)
    group, column = lax.axis_index("leaf"), lax.axis_index("front")
    layer, core = column // 2, column % 2
    info = jnp.stack([group, layer, core, group * nfront + column, column]).astype(jnp.int32)

    def dev(g, z, c):
        return g * nfront + 2 * z + c

    def send(x, pairs):
        return lax.ppermute(x, AXES, pairs)

    def out(*shape):
        return jax.ShapeDtypeStruct(shape, F32)

    both = range(2)
    swap = [(dev(g, z, c), dev(g, z, 1 - c)) for g in groups for z in layers for c in both]

    packed = out(2 * width + 8, tile)
    outgoing, payload, diag = kernel(
        sort_kernel,
        (out(nfront, tile + 8, tile), out(2 * tile + 16, tile), packed),
        (target_owner, target_slot, info, updates, front),
        smem=3,
    )
    diags = [send(diag, [(dev(0, 0, c), dev(0, s, c)) for c in both]) for s in layers[1:]]
    turned = send(front, [(dev(0, z, c), dev(z, z, c)) for z in layers[1:] for c in both])
    near = send(
        front, [(dev(g, 0, c), dev(g, z, c)) for g, z in ((1, 3), (2, 1), (3, 1)) for c in both]
    )
    blocks = lax.all_gather(payload, "front")
    far = send(
        turned,
        [(dev(g, z, c), dev(g, y, c)) for g, z, y in ((1, 1, 2), (2, 2, 3), (3, 3, 2)) for c in both],
    )
    outgoing, blocks, turned, *diags = lax.optimization_barrier((outgoing, blocks, turned, *diags))
    arrived = lax.all_to_all(outgoing, "front", split_axis=0, concat_axis=0, tiled=True)

    diag, matched = kernel(
        rows_kernel,
        (packed, out(width, 2 * width)),
        (info, front, turned, diag, *diags, blocks),
        scratch=[(nrows, 2 * width), packed.shape],
    )
    got = [
        send(diag, [(dev(0, z, c), dev(s, z, c)) for z in layers for c in both]) for s in groups[1:]
    ]
    away = [
        send(matched, [(dev(z, z, c), dev(z ^ s, z, c)) for z in layers[1:] for c in both])
        for s in groups[1:]
    ]
    diag = jnp.where(group == 0, diag, got[0] + got[1] + got[2])
    diag2 = send(diag, swap)

    piece = jnp.where(layer == 0, front, jnp.where(group == layer, turned, near + far))
    piece2 = send(piece, swap)

    square = out(width, width)
    w1, l21, w2 = kernel(
        factor_kernel, (square,) * 3, (info, diag, diag2), scratch=[packed.shape] * 2, flops=1 << 33
    )
    return kernel(
        last_kernel,
        out(nrows, width),
        (info, front, arrived, piece, piece2, matched, *away, w1, l21, w2, blocks),
        scratch=[(nrows, 2 * width), (width, 2 * width), (nrows, width)],
        flops=1 << 31,
    )


def solution(mesh):
    nleaf, nfront = mesh.shape["leaf"], mesh.shape["front"]

    def shards(front, updates, target_owner, target_slot):
        nrows, width = front.shape
        tile = updates.shape[1]
        lines_up = (
            nrows == 2 * width
            and width == 2 * tile
            and nleaf == 4
            and nfront == 8
        )
        plan = aligned if lines_up else general
        return plan(front, updates, target_owner, target_slot)

    return jax.shard_map(
        shards,
        mesh=mesh,
        in_specs=(
            P("leaf", "front"),
            P(("leaf", "front"), None, None),
            P(("leaf", "front")),
            P(("leaf", "front")),
        ),
        out_specs=P("leaf", "front"),
        check_vma=False,
    )
```

```python
import math

import jax
import jax.numpy as jnp
from jax import lax
from jax.experimental import pallas as pl
from jax.experimental.pallas import tpu as pltpu
from jax.sharding import PartitionSpec as P

F32 = jnp.float32
BF16 = jnp.bfloat16
AXES = ("leaf", "front")
EXACT = lax.Precision.HIGHEST


def spread(value, axis, source):
    kept = jnp.where(lax.axis_index(axis) == source, value, 0).astype(value.dtype)
    return lax.psum(kept, axis)


def assemble(front, updates, target_owner, target_slot):
    nrows, width = front.shape
    tile = updates.shape[1]
    nfront = lax.axis_size("front")
    buffer = jnp.zeros((nfront, tile, tile), F32).at[target_owner].set(updates)
    labels = jnp.zeros((nfront,), F32).at[target_owner].set(target_slot.astype(F32))
    arrived, places = (
        lax.all_to_all(buffer, "front", split_axis=0, concat_axis=0, tiled=True),
        lax.all_to_all(labels, "front", split_axis=0, concat_axis=0, tiled=True),
    )
    places = places.astype(jnp.int32)
    col_tiles = width // tile
    grid = front.reshape(nrows // tile, tile, col_tiles, tile)
    grid = grid.at[places // col_tiles, :, places % col_tiles, :].add(arrived)
    return grid.reshape(nrows, width)


def eliminate(shard, panel, start, row_ids, col_ids, column):
    nrows, width = panel.shape
    diag = spread(panel[start : start + width], "leaf", 0)
    chol = jnp.linalg.cholesky(diag)
    eye = jnp.eye(width, dtype=F32)
    inverse = lax.linalg.triangular_solve(chol, eye, left_side=True, lower=True)
    prod = jnp.dot(panel, inverse.T, precision=EXACT)
    lower = jnp.where(row_ids[:, None] >= start, prod, panel)
    owner_row = column * width // nrows
    offset = column * width - owner_row * nrows
    mine = lax.dynamic_slice_in_dim(lower, offset, width, 0)
    across = spread(mine, "leaf", owner_row)
    trail = jnp.where(row_ids[:, None] >= start + width, lower, 0.0)
    updated = shard - jnp.dot(trail, across.T, precision=EXACT)
    updated = jnp.where(col_ids[None, :] >= start + width, updated, shard)
    return (jnp.where(column == start // width, lower, updated), lower)


def general(front, updates, target_owner, target_slot):
    nrows, width = front.shape
    column = lax.axis_index("front")
    row_ids = lax.axis_index("leaf") * nrows + jnp.arange(nrows, dtype=jnp.int32)
    col_ids = column * width + jnp.arange(width, dtype=jnp.int32)
    shard = assemble(front, updates, target_owner, target_slot)
    first = spread(shard, "front", 0)
    shard, lower = eliminate(shard, first, 0, row_ids, col_ids, column)
    second = spread(shard, "front", 1)
    shard, lower = eliminate(shard, second, width, row_ids, col_ids, column)
    return shard


def lane_of(x, c):
    return jnp.take_along_axis(x, jnp.full(x.shape, c, jnp.int32), axis=1)


def row_of(x, i):
    return jnp.broadcast_to(x[i : i + 1, :], x.shape)


def parts(x):
    high = x.astype(BF16).astype(F32)
    rest = x - high
    mid = rest.astype(BF16).astype(F32)
    return high, mid, (rest - mid).astype(BF16).astype(F32)


def factor_inverse(a):
    n = a.shape[0]
    panels, per, ahead = n // 8, 2, 2
    sub = lax.broadcasted_iota(jnp.int32, (8, n), 0)
    lane = lax.broadcasted_iota(jnp.int32, (8, n), 1)
    work = [
        [a[8 * k : 8 * k + 8, :], jnp.where(lane == sub + 8 * k, 1.0, 0.0).astype(F32)]
        for k in range(panels)
    ]
    out, held = [], []
    for k in range(panels):
        rows, ident = work[k]
        cols = [lane_of(rows, 8 * k + j) for j in range(8)]
        d = {(i, j): row_of(cols[j], i) for j in range(8) for i in range(j, 8)}
        up = [row_of(rows, j) for j in range(8)]
        inv = [row_of(ident, j) for j in range(8)]
        last = min(panels - 1, (k // per + 1) * per - 1 + ahead)
        below = {
            b: [lane_of(work[b][0], 8 * k + j) for j in range(8)]
            for b in range(k + 1, last + 1)
        }
        for j in range(8):
            r = lax.rsqrt(d[j, j])
            for i in range(j + 1, 8):
                d[i, j] = d[i, j] * r
            for i in range(j + 1, 8):
                for m in range(j + 1, i + 1):
                    d[i, m] = d[i, m] - d[i, j] * d[m, j]
            up[j] = up[j] * r
            inv[j] = inv[j] * r
            for i in range(j + 1, 8):
                up[i] = up[i] - d[i, j] * up[j]
                inv[i] = inv[i] - d[i, j] * inv[j]
            for b, c in below.items():
                c[j] = c[j] * r
                for i in range(j + 1, 8):
                    c[i] = c[i] - d[i, j] * c[j]
                work[b] = [work[b][0] - c[j] * up[j], work[b][1] - c[j] * inv[j]]
        u, w = up[0], inv[0]
        for j in range(1, 8):
            u = jnp.where(sub == j, up[j], u)
            w = jnp.where(sub == j, inv[j], w)
        out.append(w)
        held.append((u, w))
        first = k + 1 + ahead
        if k % per == per - 1 and first < panels:
            us = jnp.concatenate([p[0] for p in held], 0)
            ws = jnp.concatenate([p[1] for p in held], 0)
            uh, um, ul = parts(us)
            wh, wm, wl = parts(ws)
            right = jnp.concatenate(
                [
                    jnp.concatenate([uh, um, ul, uh, um, uh], 0),
                    jnp.concatenate([wh, wm, wl, wh, wm, wh], 0),
                ],
                1,
            ).astype(BF16)
            left = jnp.concatenate([uh, uh, uh, um, um, ul], 0).T
            left = left[8 * first :, :].astype(BF16)
            change = jnp.dot(left, right, preferred_element_type=F32)
            for b in range(first, panels):
                part = change[8 * (b - first) : 8 * (b - first + 1), :]
                work[b] = [work[b][0] - part[:, :n], work[b][1] - part[:, n:]]
        if k % per == per - 1:
            held = []
    return jnp.concatenate(out, 0)


def dot(a, b):
    return jnp.dot(a, b, precision=EXACT, preferred_element_type=F32)


def dot_t(a, b):
    return lax.dot_general(
        a, b, (((1,), (1,)), ((), ())), precision=EXACT, preferred_element_type=F32
    )


def dot3_t(a, b):
    ah, bh = a.astype(BF16), b.astype(BF16)
    al, bl = (a - ah.astype(F32)).astype(BF16), (b - bh.astype(F32)).astype(BF16)

    def product(x, y):
        return lax.dot_general(x, y, (((1,), (1,)), ((), ())), preferred_element_type=F32)

    return product(ah, bl) + product(al, bh) + product(ah, bh)


def factor_pair(a):
    h = a.shape[0] // 2
    w11 = factor_inverse(a[:h, :h])
    l21 = dot_t(a[h:, :h], w11)
    w22 = factor_inverse(a[h:, h:] - dot_t(l21, l21))
    w21 = -dot(w22, dot(l21, w11))
    return w11, w21, w22


def store_inverse(ref, blocks):
    w11, w21, w22 = blocks
    h = w11.shape[0]
    ref[:h, :h] = w11
    ref[:h, h:] = jnp.zeros_like(w11)
    ref[h:, :h] = w21
    ref[h:, h:] = w22


def symmetric(a):
    return (a + a.T) * 0.5


def place_of(tags):
    return tags[0, 0].astype(jnp.int32)


def add_block(ref, block, place, tile, start=0):
    down = pl.multiple_of(place // 2 * tile, tile)
    right = pl.multiple_of(start + place % 2 * tile, tile)
    ref[pl.ds(down, tile), pl.ds(right, tile)] += block


def add_band_blocks(ref, blocks, width):
    for b in blocks:
        tile = b.shape[1]
        for owner in range(2):
            tag = b[2 * tile + 8 * owner : 2 * tile + 8 * owner + 8, :]
            block = b[owner * tile : (owner + 1) * tile, :]
            add_block(ref, block, place_of(tag), tile, owner * width)


def square_ids(n):
    return lax.broadcasted_iota(jnp.int32, (n, n), 0), lax.broadcasted_iota(jnp.int32, (n, n), 1)


def pack(ref, s):
    n = s.shape[0] // 2
    row, col = square_ids(n)
    ref[:n, :] = jnp.where(row >= col, s[:n, :n], s[n:, n:])
    ref[n : 2 * n, :] = s[n:, :n]
    diag = jnp.sum(jnp.where(row == col, s[n:, n:], 0.0), 0, keepdims=True)
    ref[2 * n : 2 * n + 8, :] = jnp.broadcast_to(diag, (8, n))


def unpack(ref):
    n = ref.shape[1]
    row, col = square_ids(n)
    both, low = ref[:n, :], ref[n : 2 * n, :]
    turned = both.T
    s00 = jnp.where(row >= col, both, turned)
    s11 = jnp.where(row < col, both, jnp.where(row > col, turned, ref[2 * n : 2 * n + 1, :]))
    return jnp.concatenate(
        [jnp.concatenate([s00, low.T], 1), jnp.concatenate([low, s11], 1)], 0
    )


def put_rows(ref, start, rows):
    n = ref.shape[1]
    ref[start : start + n, :] = rows[:, :n]
    ref[start + n : start + 2 * n, :] = rows[:, n:]


def get_rows(ref, start):
    n = ref.shape[1]
    return jnp.concatenate([ref[start : start + n, :], ref[start + n : start + 2 * n, :]], 1)


def sort_kernel(owner, slot, info, updates, front, out_ref, pay_ref, diag_ref):
    sends, tile = updates.shape[:2]
    width = front.shape[1]
    out_ref[...] = jnp.zeros_like(out_ref)
    for j in range(sends):
        out_ref[owner[j], :tile, :] = updates[j]
        out_ref[owner[j], tile:, :] = jnp.full((8, tile), slot[j].astype(F32))
    for o in range(2):
        pay_ref[o * tile : (o + 1) * tile, :] = out_ref[o, :tile, :]
        pay_ref[2 * tile + 8 * o : 2 * tile + 8 * o + 8, :] = out_ref[o, tile:, :]

    @pl.when(info[3] == 0)
    def _():
        pack(diag_ref, front[:width, :])
        put_rows(diag_ref, width + 8, front[width : width + tile, :])

    @pl.when(info[3] == 1)
    def _():
        pack(diag_ref, front[width:, :])
        put_rows(diag_ref, width + 8, front[:width, tile:].T)


def rows_kernel(info, front, turned, diag, hop1, hop2, *refs):
    blocks, (diag_ref, out_ref, band, part) = refs[:8], refs[8:]
    width = front.shape[1]
    tile = width // 2
    group, layer, core = info[0], info[1], info[2]

    @pl.when((group == 0) | (group == layer))
    def _():
        band[...] = jnp.zeros_like(band)
        add_band_blocks(band, blocks, width)

    @pl.when(group == 0)
    def _():
        for z, d in enumerate((diag, hop2, hop1, hop2)):

            @pl.when(layer == z)
            def _(d=d):
                diag_ref[...] = d[...]

        @pl.when(core == 0)
        def _():
            pack(part, symmetric(band[:width, :width]))
            put_rows(part, width + 8, band[width : width + tile, :width])

        @pl.when(core == 1)
        def _():
            pack(part, symmetric(band[width:, width:]))
            put_rows(part, width + 8, band[width + tile :, :width])

        diag_ref[...] += part[...]

    @pl.when((group == layer) & (group > 0))
    def _():
        start = pl.multiple_of(core * width, width)
        out_ref[...] = turned[...].T + band[pl.ds(start, width), :]


def factor_kernel(info, here, there, w_ref, l_ref, v_ref, top, bottom):
    tile = here.shape[1]
    width = 2 * tile

    @pl.when(info[2] == 0)
    def _():
        top[...] = here[...]
        bottom[...] = there[...]

    @pl.when(info[2] == 1)
    def _():
        top[...] = there[...]
        bottom[...] = here[...]

    store_inverse(w_ref, factor_pair(unpack(top)))
    w = w_ref[...]
    l_ref[:tile, :] = dot_t(get_rows(top, width + 8), w)
    l_ref[tile:, :] = dot_t(get_rows(bottom, width + 8), w)
    lower = l_ref[...]
    store_inverse(v_ref, factor_pair(unpack(bottom) - dot_t(lower, lower)))


def last_kernel(info, shard, arrived, piece, piece2, matched, m1, m2, m3, w, lower, v, *refs):
    blocks, (out_ref, band, line, work) = refs[:8], refs[8:]
    tile = arrived.shape[2]
    nrows, width = shard.shape
    group, layer, core, column = info[0], info[1], info[2], info[4]
    out_ref[...] = shard[...]
    for i in range(arrived.shape[0]):
        add_block(out_ref, arrived[i, :tile, :], place_of(arrived[i, tile:, :]), tile)
    for k, m in enumerate((matched, m1, m2, m3)):

        @pl.when((group ^ layer) == k)
        def _(m=m):
            line[...] = m[...]

    w1, l21 = w[...], lower[...]
    by_rows = (layer > 0) & (((group == 1) & (layer < 3)) | ((group > 1) & (layer > 1)))
    for c, (same, swapped) in enumerate(((piece, piece2), (piece2, piece))):

        @pl.when(by_rows & (core == 0))
        def _(c=c, p=same):
            band[c * width : (c + 1) * width, :] = p[...].T

        @pl.when(by_rows & (core == 1))
        def _(c=c, p=swapped):
            band[c * width : (c + 1) * width, :] = p[...].T

        @pl.when(~by_rows & (core == 0))
        def _(c=c, p=same):
            band[:, c * width : (c + 1) * width] = p[...]

        @pl.when(~by_rows & (core == 1))
        def _(c=c, p=swapped):
            band[:, c * width : (c + 1) * width] = p[...]

    @pl.when(group > 0)
    def _():
        add_band_blocks(band, blocks, width)

    @pl.when(column == 0)
    def _():
        out_ref[...] = dot3_t(out_ref[...], w1)

    @pl.when(column > 0)
    def _():
        @pl.when(group == 0)
        def _():
            work[:width, :] = jnp.zeros((width, width), F32)
            work[width:, :] = l21

        @pl.when(group > 0)
        def _():
            work[...] = dot3_t(band[:, :width], w1)

        first = work[...]

        @pl.when(column == 1)
        def _():
            rows = group * nrows + lax.broadcasted_iota(jnp.int32, (nrows, width), 0)
            own = out_ref[...]
            out_ref[...] = jnp.where(rows >= width, dot3_t(own - dot3_t(first, l21), v[...]), own)

        @pl.when(column > 1)
        def _():
            mine = dot3_t(line[:, :width], w1)
            out_ref[...] -= dot3_t(first, mine)

            @pl.when(group > 0)
            def _():
                second = dot3_t(band[:, width:] - dot3_t(first, l21), v[...])
                out_ref[...] -= dot3_t(second, dot3_t(line[:, width:] - dot3_t(mine, l21), v[...]))


def kernel(body, outs, args, smem=1, scratch=(), flops=1 << 20):
    spec = [pl.BlockSpec(memory_space=pltpu.SMEM)] * smem
    spec += [pl.BlockSpec(memory_space=pltpu.VMEM)] * (len(args) - smem)
    sizes = [a.size for a in args[smem:]] + [o.size for o in jax.tree.leaves(outs)]
    need = 4 * (sum(sizes) + sum(math.prod(s) for s in scratch)) + (6 << 20)
    return pl.pallas_call(
        body,
        out_shape=outs,
        in_specs=spec,
        scratch_shapes=[pltpu.VMEM(s, F32) for s in scratch],
        compiler_params=pltpu.CompilerParams(vmem_limit_bytes=need),
        cost_estimate=pl.CostEstimate(flops=flops, bytes_accessed=1 << 20, transcendentals=0),
    )(*args)


def aligned(front, updates, target_owner, target_slot):
    nrows, width = front.shape
    tile = updates.shape[1]
    nleaf, nfront = lax.axis_size("leaf"), lax.axis_size("front")
    groups, layers = range(nleaf), range(nfront // 2)
    group, column = lax.axis_index("leaf"), lax.axis_index("front")
    layer, core = column // 2, column % 2
    info = jnp.stack([group, layer, core, group * nfront + column, column]).astype(jnp.int32)

    def dev(g, z, c):
        return g * nfront + 2 * z + c

    def send(x, pairs):
        return lax.ppermute(x, AXES, pairs)

    def out(*shape):
        return jax.ShapeDtypeStruct(shape, F32)

    both = range(2)
    swap = [(dev(g, z, c), dev(g, z, 1 - c)) for g in groups for z in layers for c in both]

    packed = out(2 * width + 8, tile)
    outgoing, payload, diag = kernel(
        sort_kernel,
        (out(nfront, tile + 8, tile), out(2 * tile + 16, tile), packed),
        (target_owner, target_slot, info, updates, front),
        smem=3,
    )
    blocks = [payload]
    for s in layers[1:]:
        pairs = [(dev(g, z, c), dev(g, z ^ s, c)) for g in groups for z in layers for c in both]
        blocks.append(send(payload, pairs))
    blocks += [send(b, swap) for b in blocks]
    hop1 = send(diag, [(dev(0, 0, c), dev(0, 2, c)) for c in both])
    hop2 = send(
        jnp.where(layer == 0, diag, hop1), [(dev(0, z, c), dev(0, z + 1, c)) for z in (0, 2) for c in both]
    )
    early, outgoing, info = lax.optimization_barrier((front, outgoing, info))
    turned = send(early, [(dev(0, z, c), dev(z, z, c)) for z in layers[1:] for c in both])
    near = send(
        early, [(dev(g, 0, c), dev(g, z, c)) for g, z in ((1, 3), (2, 1), (3, 1)) for c in both]
    )
    far = send(
        turned,
        [(dev(g, z, c), dev(g, y, c)) for g, z, y in ((1, 1, 2), (2, 2, 3), (3, 3, 2)) for c in both],
    )

    diag, matched = kernel(
        rows_kernel,
        (packed, out(width, 2 * width)),
        (info, front, turned, diag, hop1, hop2, *blocks),
        scratch=[(nrows, 2 * width), packed.shape],
    )
    diag, outgoing = lax.optimization_barrier((diag, outgoing))
    arrived = lax.all_to_all(outgoing, "front", split_axis=0, concat_axis=0, tiled=True)
    got = [
        send(diag, [(dev(0, z, c), dev(s, z, c)) for z in layers for c in both]) for s in groups[1:]
    ]
    away = [
        send(matched, [(dev(z, z, c), dev(z ^ s, z, c)) for z in layers[1:] for c in both])
        for s in groups[1:]
    ]
    diag = jnp.where(group == 0, diag, got[0] + got[1] + got[2])
    diag2 = send(diag, swap)

    piece = jnp.where(layer == 0, front, jnp.where(group == layer, turned, near + far))
    piece2 = send(piece, swap)

    square = out(width, width)
    w1, l21, w2 = kernel(
        factor_kernel, (square,) * 3, (info, diag, diag2), scratch=[packed.shape] * 2, flops=1 << 33
    )
    return kernel(
        last_kernel,
        out(nrows, width),
        (info, front, arrived, piece, piece2, matched, *away, w1, l21, w2, *blocks),
        scratch=[(nrows, 2 * width), (width, 2 * width), (nrows, width)],
        flops=1 << 31,
    )


def solution(mesh):
    nleaf, nfront = mesh.shape["leaf"], mesh.shape["front"]

    def shards(front, updates, target_owner, target_slot):
        nrows, width = front.shape
        tile = updates.shape[1]
        lines_up = (
            nrows == 2 * width
            and width == 2 * tile
            and nleaf == 4
            and nfront == 8
        )
        plan = aligned if lines_up else general
        return plan(front, updates, target_owner, target_slot)

    return jax.shard_map(
        shards,
        mesh=mesh,
        in_specs=(
            P("leaf", "front"),
            P(("leaf", "front"), None, None),
            P(("leaf", "front")),
            P(("leaf", "front")),
        ),
        out_specs=P("leaf", "front"),
        check_vma=False,
    )
```

```python
import math

import jax
import jax.numpy as jnp
from jax import lax
from jax.experimental import pallas as pl
from jax.experimental.pallas import tpu as pltpu
from jax.sharding import PartitionSpec as P

F32 = jnp.float32
BF16 = jnp.bfloat16
AXES = ("leaf", "front")
EXACT = lax.Precision.HIGHEST


def spread(value, axis, source):
    kept = jnp.where(lax.axis_index(axis) == source, value, 0).astype(value.dtype)
    return lax.psum(kept, axis)


def assemble(front, updates, target_owner, target_slot):
    nrows, width = front.shape
    tile = updates.shape[1]
    nfront = lax.axis_size("front")
    buffer = jnp.zeros((nfront, tile, tile), F32).at[target_owner].set(updates)
    labels = jnp.zeros((nfront,), F32).at[target_owner].set(target_slot.astype(F32))
    arrived, places = (
        lax.all_to_all(buffer, "front", split_axis=0, concat_axis=0, tiled=True),
        lax.all_to_all(labels, "front", split_axis=0, concat_axis=0, tiled=True),
    )
    places = places.astype(jnp.int32)
    col_tiles = width // tile
    grid = front.reshape(nrows // tile, tile, col_tiles, tile)
    grid = grid.at[places // col_tiles, :, places % col_tiles, :].add(arrived)
    return grid.reshape(nrows, width)


def eliminate(shard, panel, start, row_ids, col_ids, column):
    nrows, width = panel.shape
    diag = spread(panel[start : start + width], "leaf", 0)
    chol = jnp.linalg.cholesky(diag)
    eye = jnp.eye(width, dtype=F32)
    inverse = lax.linalg.triangular_solve(chol, eye, left_side=True, lower=True)
    prod = jnp.dot(panel, inverse.T, precision=EXACT)
    lower = jnp.where(row_ids[:, None] >= start, prod, panel)
    owner_row = column * width // nrows
    offset = column * width - owner_row * nrows
    mine = lax.dynamic_slice_in_dim(lower, offset, width, 0)
    across = spread(mine, "leaf", owner_row)
    trail = jnp.where(row_ids[:, None] >= start + width, lower, 0.0)
    updated = shard - jnp.dot(trail, across.T, precision=EXACT)
    updated = jnp.where(col_ids[None, :] >= start + width, updated, shard)
    return (jnp.where(column == start // width, lower, updated), lower)


def general(front, updates, target_owner, target_slot):
    nrows, width = front.shape
    column = lax.axis_index("front")
    row_ids = lax.axis_index("leaf") * nrows + jnp.arange(nrows, dtype=jnp.int32)
    col_ids = column * width + jnp.arange(width, dtype=jnp.int32)
    shard = assemble(front, updates, target_owner, target_slot)
    first = spread(shard, "front", 0)
    shard, lower = eliminate(shard, first, 0, row_ids, col_ids, column)
    second = spread(shard, "front", 1)
    shard, lower = eliminate(shard, second, width, row_ids, col_ids, column)
    return shard


def lane_of(x, c):
    return jnp.take_along_axis(x, jnp.full(x.shape, c, jnp.int32), axis=1)


def row_of(x, i):
    return jnp.broadcast_to(x[i : i + 1, :], x.shape)


def parts(x):
    high = x.astype(BF16).astype(F32)
    rest = x - high
    mid = rest.astype(BF16).astype(F32)
    return high, mid, (rest - mid).astype(BF16).astype(F32)


def factor_inverse(a):
    n = a.shape[0]
    panels, per, ahead = n // 8, 2, 2
    sub = lax.broadcasted_iota(jnp.int32, (8, n), 0)
    lane = lax.broadcasted_iota(jnp.int32, (8, n), 1)
    work = [
        [a[8 * k : 8 * k + 8, :], jnp.where(lane == sub + 8 * k, 1.0, 0.0).astype(F32)]
        for k in range(panels)
    ]
    out, held = [], []
    for k in range(panels):
        rows, ident = work[k]
        cols = [lane_of(rows, 8 * k + j) for j in range(8)]
        d = {(i, j): row_of(cols[j], i) for j in range(8) for i in range(j, 8)}
        up = [row_of(rows, j) for j in range(8)]
        inv = [row_of(ident, j) for j in range(8)]
        last = min(panels - 1, (k // per + 1) * per - 1 + ahead)
        below = {
            b: [lane_of(work[b][0], 8 * k + j) for j in range(8)]
            for b in range(k + 1, last + 1)
        }
        for j in range(8):
            r = lax.rsqrt(d[j, j])
            for i in range(j + 1, 8):
                d[i, j] = d[i, j] * r
            for i in range(j + 1, 8):
                for m in range(j + 1, i + 1):
                    d[i, m] = d[i, m] - d[i, j] * d[m, j]
            up[j] = up[j] * r
            inv[j] = inv[j] * r
            for i in range(j + 1, 8):
                up[i] = up[i] - d[i, j] * up[j]
                inv[i] = inv[i] - d[i, j] * inv[j]
            for b, c in below.items():
                c[j] = c[j] * r
                for i in range(j + 1, 8):
                    c[i] = c[i] - d[i, j] * c[j]
                work[b] = [work[b][0] - c[j] * up[j], work[b][1] - c[j] * inv[j]]
        u, w = up[0], inv[0]
        for j in range(1, 8):
            u = jnp.where(sub == j, up[j], u)
            w = jnp.where(sub == j, inv[j], w)
        out.append(w)
        held.append((u, w))
        first = k + 1 + ahead
        if k % per == per - 1 and first < panels:
            us = jnp.concatenate([p[0] for p in held], 0)
            ws = jnp.concatenate([p[1] for p in held], 0)
            uh, um, ul = parts(us)
            wh, wm, wl = parts(ws)
            right = jnp.concatenate(
                [
                    jnp.concatenate([uh, um, ul, uh, um, uh], 0),
                    jnp.concatenate([wh, wm, wl, wh, wm, wh], 0),
                ],
                1,
            ).astype(BF16)
            left = jnp.concatenate([uh, uh, uh, um, um, ul], 0).T
            left = left[8 * first :, :].astype(BF16)
            change = jnp.dot(left, right, preferred_element_type=F32)
            for b in range(first, panels):
                part = change[8 * (b - first) : 8 * (b - first + 1), :]
                work[b] = [work[b][0] - part[:, :n], work[b][1] - part[:, n:]]
        if k % per == per - 1:
            held = []
    return jnp.concatenate(out, 0)


def dot(a, b):
    return jnp.dot(a, b, precision=EXACT, preferred_element_type=F32)


def dot_t(a, b):
    return lax.dot_general(
        a, b, (((1,), (1,)), ((), ())), precision=EXACT, preferred_element_type=F32
    )


def dot3_t(a, b):
    ah, bh = a.astype(BF16), b.astype(BF16)
    al, bl = (a - ah.astype(F32)).astype(BF16), (b - bh.astype(F32)).astype(BF16)

    def product(x, y):
        return lax.dot_general(x, y, (((1,), (1,)), ((), ())), preferred_element_type=F32)

    return product(ah, bl) + product(al, bh) + product(ah, bh)


def factor_pair(a):
    h = a.shape[0] // 2
    w11 = factor_inverse(a[:h, :h])
    l21 = dot_t(a[h:, :h], w11)
    w22 = factor_inverse(a[h:, h:] - dot_t(l21, l21))
    w21 = -dot(w22, dot(l21, w11))
    return w11, w21, w22


def store_inverse(ref, blocks):
    w11, w21, w22 = blocks
    h = w11.shape[0]
    ref[:h, :h] = w11
    ref[:h, h:] = jnp.zeros_like(w11)
    ref[h:, :h] = w21
    ref[h:, h:] = w22


def symmetric(a):
    return (a + a.T) * 0.5


def place_of(tags):
    return tags[0, 0].astype(jnp.int32)


def add_block(ref, block, place, tile, start=0):
    down = pl.multiple_of(place // 2 * tile, tile)
    right = pl.multiple_of(start + place % 2 * tile, tile)
    ref[pl.ds(down, tile), pl.ds(right, tile)] += block


def add_band_blocks(ref, blocks, width):
    for b in blocks:
        tile = b.shape[1]
        for owner in range(2):
            tag = b[2 * tile + 8 * owner : 2 * tile + 8 * owner + 8, :]
            block = b[owner * tile : (owner + 1) * tile, :]
            add_block(ref, block, place_of(tag), tile, owner * width)


def square_ids(n):
    return lax.broadcasted_iota(jnp.int32, (n, n), 0), lax.broadcasted_iota(jnp.int32, (n, n), 1)


def pack(ref, s):
    n = s.shape[0] // 2
    row, col = square_ids(n)
    ref[:n, :] = jnp.where(row >= col, s[:n, :n], s[n:, n:])
    ref[n : 2 * n, :] = s[n:, :n]
    diag = jnp.sum(jnp.where(row == col, s[n:, n:], 0.0), 0, keepdims=True)
    ref[2 * n : 2 * n + 8, :] = jnp.broadcast_to(diag, (8, n))


def unpack(ref):
    n = ref.shape[1]
    row, col = square_ids(n)
    both, low = ref[:n, :], ref[n : 2 * n, :]
    turned = both.T
    s00 = jnp.where(row >= col, both, turned)
    s11 = jnp.where(row < col, both, jnp.where(row > col, turned, ref[2 * n : 2 * n + 1, :]))
    return jnp.concatenate(
        [jnp.concatenate([s00, low.T], 1), jnp.concatenate([low, s11], 1)], 0
    )


def put_rows(ref, start, rows):
    n = ref.shape[1]
    ref[start : start + n, :] = rows[:, :n]
    ref[start + n : start + 2 * n, :] = rows[:, n:]


def get_rows(ref, start):
    n = ref.shape[1]
    return jnp.concatenate([ref[start : start + n, :], ref[start + n : start + 2 * n, :]], 1)


def sort_kernel(owner, slot, info, updates, front, out_ref, pay_ref, diag_ref, square, sems, side):
    sends, tile = updates.shape[:2]
    width = front.shape[1]
    near_diag = info[3] < 2
    corner = pltpu.make_async_copy(front, square, side)

    @pl.when(near_diag)
    def _():
        corner.start()

    out_ref[...] = jnp.zeros_like(out_ref)
    copies = [
        pltpu.make_async_copy(updates.at[j], out_ref.at[owner[j], pl.ds(0, tile), :], sems.at[j])
        for j in range(sends)
    ]
    for j in range(sends):
        copies[j].start()
        out_ref[owner[j], tile:, :] = jnp.full((8, tile), slot[j].astype(F32))

    @pl.when(near_diag)
    def _():
        corner.wait()

    @pl.when(info[3] == 0)
    def _():
        pack(diag_ref, square[:width, :])
        put_rows(diag_ref, width + 8, square[width : width + tile, :])

    @pl.when(info[3] == 1)
    def _():
        pack(diag_ref, square[width:, :])
        put_rows(diag_ref, width + 8, square[:width, tile:].T)

    for c in copies:
        c.wait()
    for o in range(2):
        pay_ref[o * tile : (o + 1) * tile, :] = out_ref[o, :tile, :]
        pay_ref[2 * tile + 8 * o : 2 * tile + 8 * o + 8, :] = out_ref[o, tile:, :]


def rows_kernel(info, front, direct, diag, hop1, hop2, *refs):
    blocks, (diag_ref, out_ref, band, part) = refs[:8], refs[8:]
    width = front.shape[1]
    tile = width // 2
    group, layer, core = info[0], info[1], info[2]

    @pl.when((group == 0) | (group == layer))
    def _():
        band[...] = jnp.zeros_like(band)
        add_band_blocks(band, blocks, width)

    @pl.when(group == 0)
    def _():
        for z, d in enumerate((diag, hop2, hop1, hop2)):

            @pl.when(layer == z)
            def _(d=d):
                diag_ref[...] = d[...]

        @pl.when(core == 0)
        def _():
            pack(part, symmetric(band[:width, :width]))
            put_rows(part, width + 8, band[width : width + tile, :width])

        @pl.when(core == 1)
        def _():
            pack(part, symmetric(band[width:, width:]))
            put_rows(part, width + 8, band[width + tile :, :width])

        diag_ref[...] += part[...]

    @pl.when((group == layer) & (group > 0))
    def _():
        start = pl.multiple_of(core * width, width)
        out_ref[...] = direct[...].T + band[pl.ds(start, width), :]


def factor_kernel(info, here, there, w_ref, l_ref, v_ref, top, bottom):
    tile = here.shape[1]
    width = 2 * tile

    @pl.when(info[2] == 0)
    def _():
        top[...] = here[...]
        bottom[...] = there[...]

    @pl.when(info[2] == 1)
    def _():
        top[...] = there[...]
        bottom[...] = here[...]

    store_inverse(w_ref, factor_pair(unpack(top)))
    w = w_ref[...]
    l_ref[:tile, :] = dot_t(get_rows(top, width + 8), w)
    l_ref[tile:, :] = dot_t(get_rows(bottom, width + 8), w)
    lower = l_ref[...]
    store_inverse(v_ref, factor_pair(unpack(bottom) - dot_t(lower, lower)))


def last_kernel(info, *refs):
    (shard, arrived, piece, piece2, matched, m1, m2, m3, w, lower, v), blocks = refs[:11], refs[11:19]
    out_ref, band, line, work, halves, came, pays, tri, sems = refs[19:]
    tile = came.shape[2]
    nrows, width = out_ref.shape
    group, layer, core, column = info[0], info[1], info[2], info[4]
    copies = [
        pltpu.make_async_copy(src, dst, sems.at[i])
        for i, (src, dst) in enumerate(
            [
                (shard, out_ref),
                (arrived, came),
                (piece, halves.at[0]),
                (piece2, halves.at[1]),
                (w, tri.at[0]),
                (lower, tri.at[1]),
                (v, tri.at[2]),
            ]
            + [(b, pays.at[i]) for i, b in enumerate(blocks)]
        )
    ]
    last = len(copies)
    for c in copies:
        c.start()
    for k, m in enumerate((matched, m1, m2, m3)):

        @pl.when((group ^ layer) == k)
        def _(m=m):
            pltpu.make_async_copy(m, line, sems.at[last]).start()

    copies[0].wait()
    copies[1].wait()
    for i in range(came.shape[0]):
        add_block(out_ref, came[i, :tile, :], place_of(came[i, tile:, :]), tile)
    copies[2].wait()
    copies[3].wait()
    by_rows = (layer > 0) & (((group == 1) & (layer < 3)) | ((group > 1) & (layer > 1)))
    for c in range(2):
        side = jnp.where(core == 0, c, 1 - c)

        @pl.when(by_rows)
        def _(c=c, side=side):
            band[c * width : (c + 1) * width, :] = halves[side].T

        @pl.when(~by_rows)
        def _(c=c, side=side):
            band[:, c * width : (c + 1) * width] = halves[side]

    for c in copies[4:]:
        c.wait()
    pltpu.make_async_copy(matched, line, sems.at[last]).wait()

    @pl.when(group > 0)
    def _():
        add_band_blocks(band, [pays.at[i] for i in range(len(blocks))], width)

    w1, l21, v = tri[0], tri[1], tri.at[2]

    @pl.when(column == 0)
    def _():
        out_ref[...] = dot3_t(out_ref[...], w1)

    @pl.when(column > 0)
    def _():
        @pl.when(group == 0)
        def _():
            work[:width, :] = jnp.zeros((width, width), F32)
            work[width:, :] = l21

        @pl.when(group > 0)
        def _():
            work[...] = dot3_t(band[:, :width], w1)

        first = work[...]

        @pl.when(column == 1)
        def _():
            rows = group * nrows + lax.broadcasted_iota(jnp.int32, (nrows, width), 0)
            own = out_ref[...]
            out_ref[...] = jnp.where(rows >= width, dot3_t(own - dot3_t(first, l21), v[...]), own)

        @pl.when(column > 1)
        def _():
            mine = dot3_t(line[:, :width], w1)
            out_ref[...] -= dot3_t(first, mine)

            @pl.when(group > 0)
            def _():
                second = dot3_t(band[:, width:] - dot3_t(first, l21), v[...])
                out_ref[...] -= dot3_t(second, dot3_t(line[:, width:] - dot3_t(mine, l21), v[...]))


def kernel(body, outs, args, smem=1, scratch=(), flops=1 << 20, sems=(), away=False):
    space = pl.ANY if away else pltpu.VMEM
    spec = [pl.BlockSpec(memory_space=pltpu.SMEM)] * smem
    spec += [pl.BlockSpec(memory_space=space)] * (len(args) - smem)
    sizes = [o.size for o in jax.tree.leaves(outs)] + [math.prod(s) for s in scratch]
    if not away:
        sizes += [a.size for a in args[smem:]]
    return pl.pallas_call(
        body,
        out_shape=outs,
        in_specs=spec,
        scratch_shapes=[pltpu.VMEM(s, F32) for s in scratch]
        + [pltpu.SemaphoreType.DMA(s) for s in sems],
        compiler_params=pltpu.CompilerParams(vmem_limit_bytes=4 * sum(sizes) + (6 << 20)),
        cost_estimate=pl.CostEstimate(flops=flops, bytes_accessed=1 << 20, transcendentals=0),
    )(*args)


def aligned(front, updates, target_owner, target_slot):
    nrows, width = front.shape
    tile = updates.shape[1]
    nleaf, nfront = lax.axis_size("leaf"), lax.axis_size("front")
    groups, layers = range(nleaf), range(nfront // 2)
    group, column = lax.axis_index("leaf"), lax.axis_index("front")
    layer, core = column // 2, column % 2
    info = jnp.stack([group, layer, core, group * nfront + column, column]).astype(jnp.int32)

    def dev(g, z, c):
        return g * nfront + 2 * z + c

    def send(x, pairs):
        return lax.ppermute(x, AXES, pairs)

    def out(*shape):
        return jax.ShapeDtypeStruct(shape, F32)

    both = range(2)
    swap = [(dev(g, z, c), dev(g, z, 1 - c)) for g in groups for z in layers for c in both]

    packed = out(2 * width + 8, tile)
    outgoing, payload, diag = kernel(
        sort_kernel,
        (out(nfront, tile + 8, tile), out(2 * tile + 16, tile), packed),
        (target_owner, target_slot, info, updates, front),
        smem=3,
        scratch=[(nrows, width)],
        sems=[(updates.shape[0],), ()],
        away=True,
    )
    blocks = [payload]
    for s in layers[1:]:
        pairs = [(dev(g, z, c), dev(g, z ^ s, c)) for g in groups for z in layers for c in both]
        blocks.append(send(payload, pairs))
    blocks += [send(b, swap) for b in blocks]
    hop1 = send(diag, [(dev(0, 0, c), dev(0, 2, c)) for c in both])
    hop2 = send(
        jnp.where(layer == 0, diag, hop1), [(dev(0, z, c), dev(0, z + 1, c)) for z in (0, 2) for c in both]
    )
    early, info = lax.optimization_barrier((front, info))
    direct = send(
        early,
        [(dev(0, z, c), dev(z, z, c)) for z in layers[1:] for c in both]
        + [(dev(g, 0, c), dev(g, z, c)) for g, z in ((1, 3), (2, 1), (3, 1)) for c in both],
    )
    on = send(
        direct,
        [(dev(g, z, c), dev(g, y, c)) for g, z, y in ((1, 1, 2), (2, 2, 3), (3, 3, 2)) for c in both],
    )

    diag, matched = kernel(
        rows_kernel,
        (packed, out(width, 2 * width)),
        (info, front, direct, diag, hop1, hop2, *blocks),
        scratch=[(nrows, 2 * width), packed.shape],
    )
    diag, outgoing = lax.optimization_barrier((diag, outgoing))
    arrived = lax.all_to_all(outgoing, "front", split_axis=0, concat_axis=0, tiled=True)
    got = [
        send(diag, [(dev(0, z, c), dev(s, z, c)) for z in layers for c in both]) for s in groups[1:]
    ]
    away = [
        send(matched, [(dev(z, z, c), dev(z ^ s, z, c)) for z in layers[1:] for c in both])
        for s in groups[1:]
    ]
    diag = jnp.where(group == 0, diag, got[0] + got[1] + got[2])
    diag2 = send(diag, swap)

    piece = jnp.where(layer == 0, front, direct + on)
    piece2 = send(piece, swap)

    square = out(width, width)
    w1, l21, w2 = kernel(
        factor_kernel, (square,) * 3, (info, diag, diag2), scratch=[packed.shape] * 2, flops=1 << 33
    )
    return kernel(
        last_kernel,
        out(nrows, width),
        (info, front, arrived, piece, piece2, matched, *away, w1, l21, w2, *blocks),
        scratch=[
            (nrows, 2 * width),
            (width, 2 * width),
            (nrows, width),
            (2, nrows, width),
            arrived.shape,
            (8,) + payload.shape,
            (3, width, width),
        ],
        flops=1 << 31,
        sems=[(16,)],
        away=True,
    )


def solution(mesh):
    nleaf, nfront = mesh.shape["leaf"], mesh.shape["front"]

    def shards(front, updates, target_owner, target_slot):
        nrows, width = front.shape
        tile = updates.shape[1]
        lines_up = (
            nrows == 2 * width
            and width == 2 * tile
            and nleaf == 4
            and nfront == 8
        )
        plan = aligned if lines_up else general
        return plan(front, updates, target_owner, target_slot)

    return jax.shard_map(
        shards,
        mesh=mesh,
        in_specs=(
            P("leaf", "front"),
            P(("leaf", "front"), None, None),
            P(("leaf", "front")),
            P(("leaf", "front")),
        ),
        out_specs=P("leaf", "front"),
        check_vma=False,
    )
```

```python
import math

import jax
import jax.numpy as jnp
from jax import lax
from jax.experimental import pallas as pl
from jax.experimental.pallas import tpu as pltpu
from jax.sharding import PartitionSpec as P

F32 = jnp.float32
BF16 = jnp.bfloat16
AXES = ("leaf", "front")
EXACT = lax.Precision.HIGHEST


def spread(value, axis, source):
    kept = jnp.where(lax.axis_index(axis) == source, value, 0).astype(value.dtype)
    return lax.psum(kept, axis)


def assemble(front, updates, target_owner, target_slot):
    nrows, width = front.shape
    tile = updates.shape[1]
    nfront = lax.axis_size("front")
    buffer = jnp.zeros((nfront, tile, tile), F32).at[target_owner].set(updates)
    labels = jnp.zeros((nfront,), F32).at[target_owner].set(target_slot.astype(F32))
    arrived, places = (
        lax.all_to_all(buffer, "front", split_axis=0, concat_axis=0, tiled=True),
        lax.all_to_all(labels, "front", split_axis=0, concat_axis=0, tiled=True),
    )
    places = places.astype(jnp.int32)
    col_tiles = width // tile
    grid = front.reshape(nrows // tile, tile, col_tiles, tile)
    grid = grid.at[places // col_tiles, :, places % col_tiles, :].add(arrived)
    return grid.reshape(nrows, width)


def eliminate(shard, panel, start, row_ids, col_ids, column):
    nrows, width = panel.shape
    diag = spread(panel[start : start + width], "leaf", 0)
    chol = jnp.linalg.cholesky(diag)
    eye = jnp.eye(width, dtype=F32)
    inverse = lax.linalg.triangular_solve(chol, eye, left_side=True, lower=True)
    prod = jnp.dot(panel, inverse.T, precision=EXACT)
    lower = jnp.where(row_ids[:, None] >= start, prod, panel)
    owner_row = column * width // nrows
    offset = column * width - owner_row * nrows
    mine = lax.dynamic_slice_in_dim(lower, offset, width, 0)
    across = spread(mine, "leaf", owner_row)
    trail = jnp.where(row_ids[:, None] >= start + width, lower, 0.0)
    updated = shard - jnp.dot(trail, across.T, precision=EXACT)
    updated = jnp.where(col_ids[None, :] >= start + width, updated, shard)
    return (jnp.where(column == start // width, lower, updated), lower)


def general(front, updates, target_owner, target_slot):
    nrows, width = front.shape
    column = lax.axis_index("front")
    row_ids = lax.axis_index("leaf") * nrows + jnp.arange(nrows, dtype=jnp.int32)
    col_ids = column * width + jnp.arange(width, dtype=jnp.int32)
    shard = assemble(front, updates, target_owner, target_slot)
    first = spread(shard, "front", 0)
    shard, lower = eliminate(shard, first, 0, row_ids, col_ids, column)
    second = spread(shard, "front", 1)
    shard, lower = eliminate(shard, second, width, row_ids, col_ids, column)
    return shard


def lane_of(x, c):
    return jnp.take_along_axis(x, jnp.full(x.shape, c, jnp.int32), axis=1)


def row_of(x, i):
    return jnp.broadcast_to(x[i : i + 1, :], x.shape)


def parts(x):
    high = x.astype(BF16).astype(F32)
    rest = x - high
    mid = rest.astype(BF16).astype(F32)
    return high, mid, (rest - mid).astype(BF16).astype(F32)


def factor_inverse(a):
    n = a.shape[0]
    panels, per, ahead = n // 8, 2, 2
    sub = lax.broadcasted_iota(jnp.int32, (8, n), 0)
    lane = lax.broadcasted_iota(jnp.int32, (8, n), 1)
    work = [
        [a[8 * k : 8 * k + 8, :], jnp.where(lane == sub + 8 * k, 1.0, 0.0).astype(F32)]
        for k in range(panels)
    ]
    out, held = [], []
    for k in range(panels):
        rows, ident = work[k]
        cols = [lane_of(rows, 8 * k + j) for j in range(8)]
        d = {(i, j): row_of(cols[j], i) for j in range(8) for i in range(j, 8)}
        up = [row_of(rows, j) for j in range(8)]
        inv = [row_of(ident, j) for j in range(8)]
        last = min(panels - 1, (k // per + 1) * per - 1 + ahead)
        below = {
            b: [lane_of(work[b][0], 8 * k + j) for j in range(8)]
            for b in range(k + 1, last + 1)
        }
        for j in range(8):
            r = lax.rsqrt(d[j, j])
            for i in range(j + 1, 8):
                d[i, j] = d[i, j] * r
            for i in range(j + 1, 8):
                for m in range(j + 1, i + 1):
                    d[i, m] = d[i, m] - d[i, j] * d[m, j]
            up[j] = up[j] * r
            inv[j] = inv[j] * r
            for i in range(j + 1, 8):
                up[i] = up[i] - d[i, j] * up[j]
                inv[i] = inv[i] - d[i, j] * inv[j]
            for b, c in below.items():
                c[j] = c[j] * r
                for i in range(j + 1, 8):
                    c[i] = c[i] - d[i, j] * c[j]
                work[b] = [work[b][0] - c[j] * up[j], work[b][1] - c[j] * inv[j]]
        u, w = up[0], inv[0]
        for j in range(1, 8):
            u = jnp.where(sub == j, up[j], u)
            w = jnp.where(sub == j, inv[j], w)
        out.append(w)
        held.append((u, w))
        first = k + 1 + ahead
        if k % per == per - 1 and first < panels:
            us = jnp.concatenate([p[0] for p in held], 0)
            ws = jnp.concatenate([p[1] for p in held], 0)
            uh, um, ul = parts(us)
            wh, wm, wl = parts(ws)
            right = jnp.concatenate(
                [
                    jnp.concatenate([uh, um, ul, uh, um, uh], 0),
                    jnp.concatenate([wh, wm, wl, wh, wm, wh], 0),
                ],
                1,
            ).astype(BF16)
            left = jnp.concatenate([uh, uh, uh, um, um, ul], 0).T
            left = left[8 * first :, :].astype(BF16)
            change = jnp.dot(left, right, preferred_element_type=F32)
            for b in range(first, panels):
                part = change[8 * (b - first) : 8 * (b - first + 1), :]
                work[b] = [work[b][0] - part[:, :n], work[b][1] - part[:, n:]]
        if k % per == per - 1:
            held = []
    return jnp.concatenate(out, 0)


def dot(a, b):
    return jnp.dot(a, b, precision=EXACT, preferred_element_type=F32)


def dot_t(a, b):
    return lax.dot_general(
        a, b, (((1,), (1,)), ((), ())), precision=EXACT, preferred_element_type=F32
    )


def dot3_t(a, b):
    ah, bh = a.astype(BF16), b.astype(BF16)
    al, bl = (a - ah.astype(F32)).astype(BF16), (b - bh.astype(F32)).astype(BF16)

    def product(x, y):
        return lax.dot_general(x, y, (((1,), (1,)), ((), ())), preferred_element_type=F32)

    return product(ah, bl) + product(al, bh) + product(ah, bh)


def factor_pair(a):
    h = a.shape[0] // 2
    w11 = factor_inverse(a[:h, :h])
    l21 = dot_t(a[h:, :h], w11)
    w22 = factor_inverse(a[h:, h:] - dot_t(l21, l21))
    w21 = -dot(w22, dot(l21, w11))
    return w11, w21, w22


def store_inverse(ref, blocks):
    w11, w21, w22 = blocks
    h = w11.shape[0]
    ref[:h, :h] = w11
    ref[:h, h:] = jnp.zeros_like(w11)
    ref[h:, :h] = w21
    ref[h:, h:] = w22


def symmetric(a):
    return (a + a.T) * 0.5


def place_of(tags):
    return tags[0, 0].astype(jnp.int32)


def add_block(ref, block, place, tile, start=0):
    down = pl.multiple_of(place // 2 * tile, tile)
    right = pl.multiple_of(start + place % 2 * tile, tile)
    ref[pl.ds(down, tile), pl.ds(right, tile)] += block


def add_band_blocks(ref, blocks, width):
    for b in blocks:
        tile = b.shape[1]
        for owner in range(2):
            tag = b[2 * tile + 8 * owner : 2 * tile + 8 * owner + 8, :]
            block = b[owner * tile : (owner + 1) * tile, :]
            add_block(ref, block, place_of(tag), tile, owner * width)


def square_ids(n):
    return lax.broadcasted_iota(jnp.int32, (n, n), 0), lax.broadcasted_iota(jnp.int32, (n, n), 1)


def pack(ref, s):
    n = s.shape[0] // 2
    row, col = square_ids(n)
    ref[:n, :] = jnp.where(row >= col, s[:n, :n], s[n:, n:])
    ref[n : 2 * n, :] = s[n:, :n]
    diag = jnp.sum(jnp.where(row == col, s[n:, n:], 0.0), 0, keepdims=True)
    ref[2 * n : 2 * n + 8, :] = jnp.broadcast_to(diag, (8, n))


def unpack(ref):
    n = ref.shape[1]
    row, col = square_ids(n)
    both, low = ref[:n, :], ref[n : 2 * n, :]
    turned = both.T
    s00 = jnp.where(row >= col, both, turned)
    s11 = jnp.where(row < col, both, jnp.where(row > col, turned, ref[2 * n : 2 * n + 1, :]))
    return jnp.concatenate(
        [jnp.concatenate([s00, low.T], 1), jnp.concatenate([low, s11], 1)], 0
    )


def put_rows(ref, start, rows):
    n = ref.shape[1]
    ref[start : start + n, :] = rows[:, :n]
    ref[start + n : start + 2 * n, :] = rows[:, n:]


def get_rows(ref, start):
    n = ref.shape[1]
    return jnp.concatenate([ref[start : start + n, :], ref[start + n : start + 2 * n, :]], 1)


def sort_kernel(owner, slot, info, updates, front, out_ref, pay_ref, diag_ref, square, sems, side):
    sends, tile = updates.shape[:2]
    width = front.shape[1]
    near_diag = info[3] < 2
    corner = pltpu.make_async_copy(front, square, side)

    @pl.when(near_diag)
    def _():
        corner.start()

    out_ref[...] = jnp.zeros_like(out_ref)
    copies = [
        pltpu.make_async_copy(updates.at[j], out_ref.at[owner[j], pl.ds(0, tile), :], sems.at[j])
        for j in range(sends)
    ]
    for j in range(sends):
        copies[j].start()
        out_ref[owner[j], tile:, :] = jnp.full((8, tile), slot[j].astype(F32))

    @pl.when(near_diag)
    def _():
        corner.wait()

    @pl.when(info[3] == 0)
    def _():
        pack(diag_ref, square[:width, :])
        put_rows(diag_ref, width + 8, square[width : width + tile, :])

    @pl.when(info[3] == 1)
    def _():
        pack(diag_ref, square[width:, :])
        put_rows(diag_ref, width + 8, square[:width, tile:].T)

    for c in copies:
        c.wait()
    for o in range(2):
        pay_ref[o * tile : (o + 1) * tile, :] = out_ref[o, :tile, :]
        pay_ref[2 * tile + 8 * o : 2 * tile + 8 * o + 8, :] = out_ref[o, tile:, :]


def diagonal_kernel(info, diag, hop1, hop2, *refs):
    blocks, (diag_ref, band, part) = refs[:8], refs[8:]
    tile = diag.shape[1]
    width = 2 * tile

    @pl.when(info[0] == 0)
    def _():
        band[...] = jnp.zeros_like(band)
        add_band_blocks(band, blocks, width)
        for z, d in enumerate((diag, hop2, hop1, hop2)):

            @pl.when(info[1] == z)
            def _(d=d):
                diag_ref[...] = d[...]

        @pl.when(info[2] == 0)
        def _():
            pack(part, symmetric(band[:width, :width]))
            put_rows(part, width + 8, band[width : width + tile, :width])

        @pl.when(info[2] == 1)
        def _():
            pack(part, symmetric(band[width:, width:]))
            put_rows(part, width + 8, band[width + tile :, :width])

        diag_ref[...] += part[...]


def matched_kernel(info, direct, *refs):
    blocks, (out_ref, band) = refs[:8], refs[8:]
    width = direct.shape[1]

    @pl.when((info[0] == info[1]) & (info[0] > 0))
    def _():
        band[...] = jnp.zeros_like(band)
        add_band_blocks(band, blocks, width)
        start = pl.multiple_of(info[2] * width, width)
        out_ref[...] = direct[...].T + band[pl.ds(start, width), :]


def factor_kernel(info, here, there, w_ref, l_ref, v_ref, top, bottom):
    tile = here.shape[1]
    width = 2 * tile

    @pl.when(info[2] == 0)
    def _():
        top[...] = here[...]
        bottom[...] = there[...]

    @pl.when(info[2] == 1)
    def _():
        top[...] = there[...]
        bottom[...] = here[...]

    store_inverse(w_ref, factor_pair(unpack(top)))
    w = w_ref[...]
    l_ref[:tile, :] = dot_t(get_rows(top, width + 8), w)
    l_ref[tile:, :] = dot_t(get_rows(bottom, width + 8), w)
    lower = l_ref[...]
    store_inverse(v_ref, factor_pair(unpack(bottom) - dot_t(lower, lower)))


def last_kernel(info, *refs):
    (shard, arrived, piece, piece2, matched, m1, m2, m3, w, lower, v), blocks = refs[:11], refs[11:19]
    out_ref, band, line, work, halves, came, pays, tri, sems = refs[19:]
    tile = came.shape[2]
    nrows, width = out_ref.shape
    group, layer, core, column = info[0], info[1], info[2], info[4]
    copies = [
        pltpu.make_async_copy(src, dst, sems.at[i])
        for i, (src, dst) in enumerate(
            [
                (shard, out_ref),
                (arrived, came),
                (piece, halves.at[0]),
                (piece2, halves.at[1]),
                (w, tri.at[0]),
                (lower, tri.at[1]),
                (v, tri.at[2]),
            ]
            + [(b, pays.at[i]) for i, b in enumerate(blocks)]
        )
    ]
    last = len(copies)
    for c in copies:
        c.start()
    for k, m in enumerate((matched, m1, m2, m3)):

        @pl.when((group ^ layer) == k)
        def _(m=m):
            pltpu.make_async_copy(m, line, sems.at[last]).start()

    copies[0].wait()
    copies[1].wait()
    for i in range(came.shape[0]):
        add_block(out_ref, came[i, :tile, :], place_of(came[i, tile:, :]), tile)
    copies[2].wait()
    copies[3].wait()
    by_rows = (layer > 0) & (((group == 1) & (layer < 3)) | ((group > 1) & (layer > 1)))
    for c in range(2):
        side = jnp.where(core == 0, c, 1 - c)

        @pl.when(by_rows)
        def _(c=c, side=side):
            band[c * width : (c + 1) * width, :] = halves[side].T

        @pl.when(~by_rows)
        def _(c=c, side=side):
            band[:, c * width : (c + 1) * width] = halves[side]

    for c in copies[4:]:
        c.wait()
    pltpu.make_async_copy(matched, line, sems.at[last]).wait()

    @pl.when(group > 0)
    def _():
        add_band_blocks(band, [pays.at[i] for i in range(len(blocks))], width)

    w1, l21, v = tri[0], tri[1], tri.at[2]

    @pl.when(column == 0)
    def _():
        out_ref[...] = dot3_t(out_ref[...], w1)

    @pl.when(column > 0)
    def _():
        @pl.when(group == 0)
        def _():
            work[:width, :] = jnp.zeros((width, width), F32)
            work[width:, :] = l21

        @pl.when(group > 0)
        def _():
            work[...] = dot3_t(band[:, :width], w1)

        first = work[...]

        @pl.when(column == 1)
        def _():
            rows = group * nrows + lax.broadcasted_iota(jnp.int32, (nrows, width), 0)
            own = out_ref[...]
            out_ref[...] = jnp.where(rows >= width, dot3_t(own - dot3_t(first, l21), v[...]), own)

        @pl.when(column > 1)
        def _():
            mine = dot3_t(line[:, :width], w1)
            out_ref[...] -= dot3_t(first, mine)

            @pl.when(group > 0)
            def _():
                second = dot3_t(band[:, width:] - dot3_t(first, l21), v[...])
                out_ref[...] -= dot3_t(second, dot3_t(line[:, width:] - dot3_t(mine, l21), v[...]))


def kernel(body, outs, args, smem=1, scratch=(), flops=1 << 20, sems=(), away=False):
    space = pltpu.HBM if away else pltpu.VMEM
    spec = [pl.BlockSpec(memory_space=pltpu.SMEM)] * smem
    spec += [pl.BlockSpec(memory_space=space)] * (len(args) - smem)
    if away:
        args = args[:smem] + tuple(pltpu.with_memory_space_constraint(a, pltpu.HBM) for a in args[smem:])
    sizes = [o.size for o in jax.tree.leaves(outs)] + [math.prod(s) for s in scratch]
    if not away:
        sizes += [a.size for a in args[smem:]]
    return pl.pallas_call(
        body,
        out_shape=outs,
        in_specs=spec,
        scratch_shapes=[pltpu.VMEM(s, F32) for s in scratch]
        + [pltpu.SemaphoreType.DMA(s) for s in sems],
        compiler_params=pltpu.CompilerParams(vmem_limit_bytes=4 * sum(sizes) + (6 << 20)),
        cost_estimate=pl.CostEstimate(flops=flops, bytes_accessed=1 << 20, transcendentals=0),
    )(*args)


def aligned(front, updates, target_owner, target_slot):
    nrows, width = front.shape
    tile = updates.shape[1]
    nleaf, nfront = lax.axis_size("leaf"), lax.axis_size("front")
    groups, layers = range(nleaf), range(nfront // 2)
    group, column = lax.axis_index("leaf"), lax.axis_index("front")
    layer, core = column // 2, column % 2
    info = jnp.stack([group, layer, core, group * nfront + column, column]).astype(jnp.int32)

    def dev(g, z, c):
        return g * nfront + 2 * z + c

    def send(x, pairs):
        return lax.ppermute(x, AXES, pairs)

    def out(*shape):
        return jax.ShapeDtypeStruct(shape, F32)

    both = range(2)
    swap = [(dev(g, z, c), dev(g, z, 1 - c)) for g in groups for z in layers for c in both]

    packed = out(2 * width + 8, tile)
    outgoing, payload, diag = kernel(
        sort_kernel,
        (out(nfront, tile + 8, tile), out(2 * tile + 16, tile), packed),
        (target_owner, target_slot, info, updates, front),
        smem=3,
        scratch=[(nrows, width)],
        sems=[(updates.shape[0],), ()],
        away=True,
    )
    blocks = [payload]
    for s in layers[1:]:
        pairs = [(dev(g, z, c), dev(g, z ^ s, c)) for g in groups for z in layers for c in both]
        blocks.append(send(payload, pairs))
    early, *blocks = lax.optimization_barrier((front, *blocks))
    blocks += [send(b, swap) for b in blocks]
    hop1 = send(diag, [(dev(0, 0, c), dev(0, 2, c)) for c in both])
    hop2 = send(
        jnp.where(layer == 0, diag, hop1), [(dev(0, z, c), dev(0, z + 1, c)) for z in (0, 2) for c in both]
    )
    direct = send(
        early,
        [(dev(0, z, c), dev(z, z, c)) for z in layers[1:] for c in both]
        + [(dev(g, 0, c), dev(g, z, c)) for g, z in ((1, 3), (2, 1), (3, 1)) for c in both],
    )
    on = send(
        direct,
        [(dev(g, z, c), dev(g, y, c)) for g, z, y in ((1, 1, 2), (2, 2, 3), (3, 3, 2)) for c in both],
    )

    diag = kernel(
        diagonal_kernel,
        packed,
        (info, diag, hop1, hop2, *blocks),
        scratch=[(nrows, 2 * width), packed.shape],
    )
    diag, outgoing = lax.optimization_barrier((diag, outgoing))
    got = [
        send(diag, [(dev(0, z, c), dev(s, z, c)) for z in layers for c in both]) for s in groups[1:]
    ]
    arrived = lax.all_to_all(outgoing, "front", split_axis=0, concat_axis=0, tiled=True)
    diag = jnp.where(group == 0, diag, got[0] + got[1] + got[2])
    diag2 = send(diag, swap)

    rows, diag = lax.optimization_barrier((direct, diag))
    matched = kernel(
        matched_kernel, out(width, 2 * width), (info, rows, *blocks), scratch=[(nrows, 2 * width)]
    )
    away = [
        send(matched, [(dev(z, z, c), dev(z ^ s, z, c)) for z in layers[1:] for c in both])
        for s in groups[1:]
    ]
    piece = jnp.where(layer == 0, front, direct + on)
    piece2 = send(piece, swap)

    square = out(width, width)
    w1, l21, w2 = kernel(
        factor_kernel, (square,) * 3, (info, diag, diag2), scratch=[packed.shape] * 2, flops=1 << 33
    )
    return kernel(
        last_kernel,
        out(nrows, width),
        (info, front, arrived, piece, piece2, matched, *away, w1, l21, w2, *blocks),
        scratch=[
            (nrows, 2 * width),
            (width, 2 * width),
            (nrows, width),
            (2, nrows, width),
            arrived.shape,
            (8,) + payload.shape,
            (3, width, width),
        ],
        flops=1 << 31,
        sems=[(16,)],
        away=True,
    )


def solution(mesh):
    nleaf, nfront = mesh.shape["leaf"], mesh.shape["front"]

    def shards(front, updates, target_owner, target_slot):
        nrows, width = front.shape
        tile = updates.shape[1]
        lines_up = (
            nrows == 2 * width
            and width == 2 * tile
            and nleaf == 4
            and nfront == 8
        )
        plan = aligned if lines_up else general
        return plan(front, updates, target_owner, target_slot)

    return jax.shard_map(
        shards,
        mesh=mesh,
        in_specs=(
            P("leaf", "front"),
            P(("leaf", "front"), None, None),
            P(("leaf", "front")),
            P(("leaf", "front")),
        ),
        out_specs=P("leaf", "front"),
        check_vma=False,
    )
```

```python
import math

import jax
import jax.numpy as jnp
from jax import lax
from jax.experimental import pallas as pl
from jax.experimental.pallas import tpu as pltpu
from jax.sharding import PartitionSpec as P

F32 = jnp.float32
BF16 = jnp.bfloat16
AXES = ("leaf", "front")
EXACT = lax.Precision.HIGHEST


def spread(value, axis, source):
    kept = jnp.where(lax.axis_index(axis) == source, value, 0).astype(value.dtype)
    return lax.psum(kept, axis)


def assemble(front, updates, target_owner, target_slot):
    nrows, width = front.shape
    tile = updates.shape[1]
    nfront = lax.axis_size("front")
    buffer = jnp.zeros((nfront, tile, tile), F32).at[target_owner].set(updates)
    labels = jnp.zeros((nfront,), F32).at[target_owner].set(target_slot.astype(F32))
    arrived, places = (
        lax.all_to_all(buffer, "front", split_axis=0, concat_axis=0, tiled=True),
        lax.all_to_all(labels, "front", split_axis=0, concat_axis=0, tiled=True),
    )
    places = places.astype(jnp.int32)
    col_tiles = width // tile
    grid = front.reshape(nrows // tile, tile, col_tiles, tile)
    grid = grid.at[places // col_tiles, :, places % col_tiles, :].add(arrived)
    return grid.reshape(nrows, width)


def eliminate(shard, panel, start, row_ids, col_ids, column):
    nrows, width = panel.shape
    diag = spread(panel[start : start + width], "leaf", 0)
    chol = jnp.linalg.cholesky(diag)
    eye = jnp.eye(width, dtype=F32)
    inverse = lax.linalg.triangular_solve(chol, eye, left_side=True, lower=True)
    prod = jnp.dot(panel, inverse.T, precision=EXACT)
    lower = jnp.where(row_ids[:, None] >= start, prod, panel)
    owner_row = column * width // nrows
    offset = column * width - owner_row * nrows
    mine = lax.dynamic_slice_in_dim(lower, offset, width, 0)
    across = spread(mine, "leaf", owner_row)
    trail = jnp.where(row_ids[:, None] >= start + width, lower, 0.0)
    updated = shard - jnp.dot(trail, across.T, precision=EXACT)
    updated = jnp.where(col_ids[None, :] >= start + width, updated, shard)
    return (jnp.where(column == start // width, lower, updated), lower)


def general(front, updates, target_owner, target_slot):
    nrows, width = front.shape
    column = lax.axis_index("front")
    row_ids = lax.axis_index("leaf") * nrows + jnp.arange(nrows, dtype=jnp.int32)
    col_ids = column * width + jnp.arange(width, dtype=jnp.int32)
    shard = assemble(front, updates, target_owner, target_slot)
    first = spread(shard, "front", 0)
    shard, lower = eliminate(shard, first, 0, row_ids, col_ids, column)
    second = spread(shard, "front", 1)
    shard, lower = eliminate(shard, second, width, row_ids, col_ids, column)
    return shard


def lane_of(x, c):
    return jnp.take_along_axis(x, jnp.full(x.shape, c, jnp.int32), axis=1)


def row_of(x, i):
    return jnp.broadcast_to(x[i : i + 1, :], x.shape)


def parts(x):
    high = x.astype(BF16).astype(F32)
    rest = x - high
    mid = rest.astype(BF16).astype(F32)
    return high, mid, (rest - mid).astype(BF16).astype(F32)


def factor_inverse(a):
    n = a.shape[0]
    panels, per, ahead = n // 8, 2, 2
    sub = lax.broadcasted_iota(jnp.int32, (8, n), 0)
    lane = lax.broadcasted_iota(jnp.int32, (8, n), 1)
    work = [
        [a[8 * k : 8 * k + 8, :], jnp.where(lane == sub + 8 * k, 1.0, 0.0).astype(F32)]
        for k in range(panels)
    ]
    out, held = [], []
    for k in range(panels):
        rows, ident = work[k]
        cols = [lane_of(rows, 8 * k + j) for j in range(8)]
        d = {(i, j): row_of(cols[j], i) for j in range(8) for i in range(j, 8)}
        up = [row_of(rows, j) for j in range(8)]
        inv = [row_of(ident, j) for j in range(8)]
        last = min(panels - 1, (k // per + 1) * per - 1 + ahead)
        below = {
            b: [lane_of(work[b][0], 8 * k + j) for j in range(8)]
            for b in range(k + 1, last + 1)
        }
        for j in range(8):
            r = lax.rsqrt(d[j, j])
            for i in range(j + 1, 8):
                d[i, j] = d[i, j] * r
            for i in range(j + 1, 8):
                for m in range(j + 1, i + 1):
                    d[i, m] = d[i, m] - d[i, j] * d[m, j]
            up[j] = up[j] * r
            inv[j] = inv[j] * r
            for i in range(j + 1, 8):
                up[i] = up[i] - d[i, j] * up[j]
                inv[i] = inv[i] - d[i, j] * inv[j]
            for b, c in below.items():
                c[j] = c[j] * r
                for i in range(j + 1, 8):
                    c[i] = c[i] - d[i, j] * c[j]
                work[b] = [work[b][0] - c[j] * up[j], work[b][1] - c[j] * inv[j]]
        u, w = up[0], inv[0]
        for j in range(1, 8):
            u = jnp.where(sub == j, up[j], u)
            w = jnp.where(sub == j, inv[j], w)
        out.append(w)
        held.append((u, w))
        first = k + 1 + ahead
        if k % per == per - 1 and first < panels:
            us = jnp.concatenate([p[0] for p in held], 0)
            ws = jnp.concatenate([p[1] for p in held], 0)
            uh, um, ul = parts(us)
            wh, wm, wl = parts(ws)
            right = jnp.concatenate(
                [
                    jnp.concatenate([uh, um, ul, uh, um, uh], 0),
                    jnp.concatenate([wh, wm, wl, wh, wm, wh], 0),
                ],
                1,
            ).astype(BF16)
            left = jnp.concatenate([uh, uh, uh, um, um, ul], 0).T
            left = left[8 * first :, :].astype(BF16)
            change = jnp.dot(left, right, preferred_element_type=F32)
            for b in range(first, panels):
                part = change[8 * (b - first) : 8 * (b - first + 1), :]
                work[b] = [work[b][0] - part[:, :n], work[b][1] - part[:, n:]]
        if k % per == per - 1:
            held = []
    return jnp.concatenate(out, 0)


def dot(a, b):
    return jnp.dot(a, b, precision=EXACT, preferred_element_type=F32)


def dot_t(a, b):
    return lax.dot_general(
        a, b, (((1,), (1,)), ((), ())), precision=EXACT, preferred_element_type=F32
    )


def dot3_t(a, b):
    ah, bh = a.astype(BF16), b.astype(BF16)
    al, bl = (a - ah.astype(F32)).astype(BF16), (b - bh.astype(F32)).astype(BF16)

    def product(x, y):
        return lax.dot_general(x, y, (((1,), (1,)), ((), ())), preferred_element_type=F32)

    return product(ah, bl) + product(al, bh) + product(ah, bh)


def factor_pair(a):
    h = a.shape[0] // 2
    w11 = factor_inverse(a[:h, :h])
    l21 = dot_t(a[h:, :h], w11)
    w22 = factor_inverse(a[h:, h:] - dot_t(l21, l21))
    w21 = -dot(w22, dot(l21, w11))
    return w11, w21, w22


def store_inverse(ref, blocks):
    w11, w21, w22 = blocks
    h = w11.shape[0]
    ref[:h, :h] = w11
    ref[:h, h:] = jnp.zeros_like(w11)
    ref[h:, :h] = w21
    ref[h:, h:] = w22


def symmetric(a):
    return (a + a.T) * 0.5


def place_of(tags):
    return tags[0, 0].astype(jnp.int32)


def add_block(ref, block, place, tile, start=0):
    down = pl.multiple_of(place // 2 * tile, tile)
    right = pl.multiple_of(start + place % 2 * tile, tile)
    ref[pl.ds(down, tile), pl.ds(right, tile)] += block


def add_band_blocks(ref, blocks, width):
    for b in blocks:
        tile = b.shape[1]
        for owner in range(2):
            tag = b[2 * tile + 8 * owner : 2 * tile + 8 * owner + 8, :]
            block = b[owner * tile : (owner + 1) * tile, :]
            add_block(ref, block, place_of(tag), tile, owner * width)


def square_ids(n):
    return lax.broadcasted_iota(jnp.int32, (n, n), 0), lax.broadcasted_iota(jnp.int32, (n, n), 1)


def pack(ref, s):
    n = s.shape[0] // 2
    row, col = square_ids(n)
    ref[:n, :] = jnp.where(row >= col, s[:n, :n], s[n:, n:])
    ref[n : 2 * n, :] = s[n:, :n]
    diag = jnp.sum(jnp.where(row == col, s[n:, n:], 0.0), 0, keepdims=True)
    ref[2 * n : 2 * n + 8, :] = jnp.broadcast_to(diag, (8, n))


def unpack(ref):
    n = ref.shape[1]
    row, col = square_ids(n)
    both, low = ref[:n, :], ref[n : 2 * n, :]
    turned = both.T
    s00 = jnp.where(row >= col, both, turned)
    s11 = jnp.where(row < col, both, jnp.where(row > col, turned, ref[2 * n : 2 * n + 1, :]))
    return jnp.concatenate(
        [jnp.concatenate([s00, low.T], 1), jnp.concatenate([low, s11], 1)], 0
    )


def put_rows(ref, start, rows):
    n = ref.shape[1]
    ref[start : start + n, :] = rows[:, :n]
    ref[start + n : start + 2 * n, :] = rows[:, n:]


def get_rows(ref, start):
    n = ref.shape[1]
    return jnp.concatenate([ref[start : start + n, :], ref[start + n : start + 2 * n, :]], 1)


def sort_kernel(owner, slot, info, updates, front, out_ref, pay_ref, diag_ref, square, sems, side):
    sends, tile = updates.shape[:2]
    width = front.shape[1]
    near_diag = info[3] < 2
    corner = pltpu.make_async_copy(front, square, side)

    @pl.when(near_diag)
    def _():
        corner.start()

    out_ref[...] = jnp.zeros_like(out_ref)
    copies = [
        pltpu.make_async_copy(updates.at[j], out_ref.at[owner[j], pl.ds(0, tile), :], sems.at[j])
        for j in range(sends)
    ]
    for j in range(sends):
        copies[j].start()
        out_ref[owner[j], tile:, :] = jnp.full((8, tile), slot[j].astype(F32))

    @pl.when(near_diag)
    def _():
        corner.wait()

    @pl.when(info[3] == 0)
    def _():
        pack(diag_ref, square[:width, :])
        put_rows(diag_ref, width + 8, square[width : width + tile, :])

    @pl.when(info[3] == 1)
    def _():
        pack(diag_ref, square[width:, :])
        put_rows(diag_ref, width + 8, square[:width, tile:].T)

    for c in copies:
        c.wait()
    for o in range(2):
        pay_ref[o * tile : (o + 1) * tile, :] = out_ref[o, :tile, :]
        pay_ref[2 * tile + 8 * o : 2 * tile + 8 * o + 8, :] = out_ref[o, tile:, :]


def diagonal_kernel(info, diag, hop1, hop2, *refs):
    blocks, (diag_ref, band, part) = refs[:8], refs[8:]
    tile = diag.shape[1]
    width = 2 * tile

    @pl.when(info[0] == 0)
    def _():
        band[...] = jnp.zeros_like(band)
        add_band_blocks(band, blocks, width)
        for z, d in enumerate((diag, hop2, hop1, hop2)):

            @pl.when(info[1] == z)
            def _(d=d):
                diag_ref[...] = d[...]

        @pl.when(info[2] == 0)
        def _():
            pack(part, symmetric(band[:width, :width]))
            put_rows(part, width + 8, band[width : width + tile, :width])

        @pl.when(info[2] == 1)
        def _():
            pack(part, symmetric(band[width:, width:]))
            put_rows(part, width + 8, band[width + tile :, :width])

        diag_ref[...] += part[...]


def matched_kernel(info, turned, *refs):
    blocks, (out_ref, band) = refs[:8], refs[8:]
    width = turned.shape[1]

    @pl.when((info[0] == info[1]) & (info[0] > 0))
    def _():
        band[...] = jnp.zeros_like(band)
        add_band_blocks(band, blocks, width)
        start = pl.multiple_of(info[2] * width, width)
        out_ref[...] = turned[...].T + band[pl.ds(start, width), :]


def factor_kernel(info, here, there, out_ref, top, bottom, done, sems):
    tile = here.shape[1]
    width = 2 * tile

    @pl.when(info[2] == 0)
    def _():
        top[...] = here[...]
        bottom[...] = there[...]

    @pl.when(info[2] == 1)
    def _():
        top[...] = there[...]
        bottom[...] = here[...]

    w_ref, l_ref = done.at[0], done.at[1]
    copies = [pltpu.make_async_copy(done.at[i], out_ref.at[i], sems.at[i]) for i in range(3)]
    store_inverse(w_ref, factor_pair(unpack(top)))
    copies[0].start()
    w = w_ref[...]
    l_ref[:tile, :] = dot_t(get_rows(top, width + 8), w)
    l_ref[tile:, :] = dot_t(get_rows(bottom, width + 8), w)
    copies[1].start()
    lower = l_ref[...]
    store_inverse(done.at[2], factor_pair(unpack(bottom) - dot_t(lower, lower)))
    copies[2].start()
    for c in copies:
        c.wait()


def last_kernel(info, *refs):
    (shard, arrived, piece, piece2, matched, m1, m2, m3, factors), blocks = refs[:9], refs[9:17]
    out_ref, band, line, work, halves, came, pays, tri, sems = refs[17:]
    tile = came.shape[2]
    nrows, width = out_ref.shape
    group, layer, core, column = info[0], info[1], info[2], info[4]
    copies = [
        pltpu.make_async_copy(src, dst, sems.at[i])
        for i, (src, dst) in enumerate(
            [
                (shard, out_ref),
                (arrived, came),
                (piece, halves.at[0]),
                (piece2, halves.at[1]),
                (factors, tri),
            ]
            + [(b, pays.at[i]) for i, b in enumerate(blocks)]
        )
    ]
    last = len(copies)
    for c in copies:
        c.start()
    for k, m in enumerate((matched, m1, m2, m3)):

        @pl.when((group ^ layer) == k)
        def _(m=m):
            pltpu.make_async_copy(m, line, sems.at[last]).start()

    copies[0].wait()
    copies[1].wait()
    for i in range(came.shape[0]):
        add_block(out_ref, came[i, :tile, :], place_of(came[i, tile:, :]), tile)
    copies[2].wait()
    copies[3].wait()
    by_rows = (layer > 0) & ((group == 1) | (layer > 1))
    for c in range(2):
        side = jnp.where(core == 0, c, 1 - c)

        @pl.when(by_rows)
        def _(c=c, side=side):
            band[c * width : (c + 1) * width, :] = halves[side].T

        @pl.when(~by_rows)
        def _(c=c, side=side):
            band[:, c * width : (c + 1) * width] = halves[side]

    for c in copies[4:]:
        c.wait()
    pltpu.make_async_copy(matched, line, sems.at[last]).wait()

    @pl.when(group > 0)
    def _():
        add_band_blocks(band, [pays.at[i] for i in range(len(blocks))], width)

    w1, l21, v = tri[0], tri[1], tri.at[2]

    @pl.when(column == 0)
    def _():
        out_ref[...] = dot3_t(out_ref[...], w1)

    @pl.when(column > 0)
    def _():
        @pl.when(group == 0)
        def _():
            work[:width, :] = jnp.zeros((width, width), F32)
            work[width:, :] = l21

        @pl.when(group > 0)
        def _():
            work[...] = dot3_t(band[:, :width], w1)

        first = work[...]

        @pl.when(column == 1)
        def _():
            rows = group * nrows + lax.broadcasted_iota(jnp.int32, (nrows, width), 0)
            own = out_ref[...]
            out_ref[...] = jnp.where(rows >= width, dot3_t(own - dot3_t(first, l21), v[...]), own)

        @pl.when(column > 1)
        def _():
            mine = dot3_t(line[:, :width], w1)
            out_ref[...] -= dot3_t(first, mine)

            @pl.when(group > 0)
            def _():
                second = dot3_t(band[:, width:] - dot3_t(first, l21), v[...])
                out_ref[...] -= dot3_t(second, dot3_t(line[:, width:] - dot3_t(mine, l21), v[...]))


def kernel(body, outs, args, smem=1, scratch=(), flops=1 << 20, sems=(), away=False):
    space = pltpu.HBM if away else pltpu.VMEM
    spec = [pl.BlockSpec(memory_space=pltpu.SMEM)] * smem
    out_space = pltpu.HBM if isinstance(outs, type(pltpu.HBM((8, 128), F32))) else pltpu.VMEM
    spec += [pl.BlockSpec(memory_space=space)] * (len(args) - smem)
    if away:
        args = args[:smem] + tuple(pltpu.with_memory_space_constraint(a, pltpu.HBM) for a in args[smem:])
    sizes = [math.prod(o.shape) for o in jax.tree.leaves(outs)] + [math.prod(s) for s in scratch]
    if not away:
        sizes += [a.size for a in args[smem:]]
    return pl.pallas_call(
        body,
        out_shape=outs,
        in_specs=spec,
        out_specs=jax.tree.map(lambda o: pl.BlockSpec(memory_space=out_space), outs),
        scratch_shapes=[pltpu.VMEM(s, F32) for s in scratch]
        + [pltpu.SemaphoreType.DMA(s) for s in sems],
        compiler_params=pltpu.CompilerParams(vmem_limit_bytes=4 * sum(sizes) + (6 << 20)),
        cost_estimate=pl.CostEstimate(flops=flops, bytes_accessed=1 << 20, transcendentals=0),
    )(*args)


def aligned(front, updates, target_owner, target_slot):
    nrows, width = front.shape
    tile = updates.shape[1]
    nleaf, nfront = lax.axis_size("leaf"), lax.axis_size("front")
    groups, layers = range(nleaf), range(nfront // 2)
    group, column = lax.axis_index("leaf"), lax.axis_index("front")
    layer, core = column // 2, column % 2
    info = jnp.stack([group, layer, core, group * nfront + column, column]).astype(jnp.int32)

    def dev(g, z, c):
        return g * nfront + 2 * z + c

    def send(x, pairs):
        return lax.ppermute(x, AXES, pairs)

    def out(*shape):
        return jax.ShapeDtypeStruct(shape, F32)

    both = range(2)
    swap = [(dev(g, z, c), dev(g, z, 1 - c)) for g in groups for z in layers for c in both]

    packed = out(2 * width + 8, tile)
    outgoing, payload, diag = kernel(
        sort_kernel,
        (out(nfront, tile + 8, tile), out(2 * tile + 16, tile), packed),
        (target_owner, target_slot, info, updates, front),
        smem=3,
        scratch=[(nrows, width)],
        sems=[(updates.shape[0],), ()],
        away=True,
    )
    blocks = [payload]
    for s in layers[1:]:
        pairs = [(dev(g, z, c), dev(g, z ^ s, c)) for g in groups for z in layers for c in both]
        blocks.append(send(payload, pairs))
    blocks += [send(b, swap) for b in blocks]
    hop1 = send(diag, [(dev(0, 0, c), dev(0, 2, c)) for c in both])
    hop2 = send(
        jnp.where(layer == 0, diag, hop1), [(dev(0, z, c), dev(0, z + 1, c)) for z in (0, 2) for c in both]
    )
    early, outgoing, info = lax.optimization_barrier((front, outgoing, info))
    turned = send(early, [(dev(0, z, c), dev(z, z, c)) for z in layers[1:] for c in both])
    diag, turned = lax.optimization_barrier((diag, turned))

    diag = kernel(
        diagonal_kernel,
        packed,
        (info, diag, hop1, hop2, *blocks),
        scratch=[(nrows, 2 * width), packed.shape],
    )
    diag, outgoing, early, turned = lax.optimization_barrier((diag, outgoing, early, turned))
    got = [
        send(diag, [(dev(0, z, c), dev(s, z, c)) for z in layers for c in both]) for s in groups[1:]
    ]
    arrived = lax.all_to_all(outgoing, "front", split_axis=0, concat_axis=0, tiled=True)
    diag = jnp.where(group == 0, diag, got[0] + got[1] + got[2])
    diag2 = send(diag, swap)

    far = send(
        turned,
        [(dev(g, z, c), dev(g, y, c)) for g, z, y in ((1, 1, 2), (2, 2, 3), (3, 3, 2)) for c in both],
    )

    matched = kernel(
        matched_kernel, out(width, 2 * width), (info, turned, *blocks), scratch=[(nrows, 2 * width)]
    )
    matched, early, diag = lax.optimization_barrier((matched, early, diag))
    near = send(
        early,
        [(dev(g, 0, c), dev(g, 1, c)) for g in (2, 3) for c in both]
        + [(dev(0, 1, c), dev(1, 3, c)) for c in both],
    )
    away = [
        send(matched, [(dev(z, z, c), dev(z ^ s, z, c)) for z in layers[1:] for c in both])
        for s in groups[1:]
    ]

    diag, diag2, far = lax.optimization_barrier((diag, diag2, far))
    factors = kernel(
        factor_kernel,
        pltpu.HBM((3, width, width), F32),
        (info, diag, diag2),
        scratch=[packed.shape] * 2 + [(3, width, width)],
        flops=1 << 33,
        sems=[(3,)],
    )
    factors, near, far = lax.optimization_barrier((factors, near, far))
    piece = jnp.where(layer == 0, front, jnp.where(group == layer, turned, near + far))
    piece2 = send(piece, swap)
    return kernel(
        last_kernel,
        out(nrows, width),
        (info, front, arrived, piece, piece2, matched, *away, factors, *blocks),
        scratch=[
            (nrows, 2 * width),
            (width, 2 * width),
            (nrows, width),
            (2, nrows, width),
            arrived.shape,
            (8,) + payload.shape,
            (3, width, width),
        ],
        flops=1 << 31,
        sems=[(16,)],
        away=True,
    )


def solution(mesh):
    nleaf, nfront = mesh.shape["leaf"], mesh.shape["front"]

    def shards(front, updates, target_owner, target_slot):
        nrows, width = front.shape
        tile = updates.shape[1]
        lines_up = (
            nrows == 2 * width
            and width == 2 * tile
            and nleaf == 4
            and nfront == 8
        )
        plan = aligned if lines_up else general
        return plan(front, updates, target_owner, target_slot)

    return jax.shard_map(
        shards,
        mesh=mesh,
        in_specs=(
            P("leaf", "front"),
            P(("leaf", "front"), None, None),
            P(("leaf", "front")),
            P(("leaf", "front")),
        ),
        out_specs=P("leaf", "front"),
        check_vma=False,
    )
```

```python
import math

import jax
import jax.numpy as jnp
from jax import lax
from jax.experimental import pallas as pl
from jax.experimental.pallas import tpu as pltpu
from jax.sharding import PartitionSpec as P

F32 = jnp.float32
BF16 = jnp.bfloat16
AXES = ("leaf", "front")
EXACT = lax.Precision.HIGHEST


def spread(value, axis, source):
    kept = jnp.where(lax.axis_index(axis) == source, value, 0).astype(value.dtype)
    return lax.psum(kept, axis)


def assemble(front, updates, target_owner, target_slot):
    nrows, width = front.shape
    tile = updates.shape[1]
    nfront = lax.axis_size("front")
    buffer = jnp.zeros((nfront, tile, tile), F32).at[target_owner].set(updates)
    labels = jnp.zeros((nfront,), F32).at[target_owner].set(target_slot.astype(F32))
    arrived, places = (
        lax.all_to_all(buffer, "front", split_axis=0, concat_axis=0, tiled=True),
        lax.all_to_all(labels, "front", split_axis=0, concat_axis=0, tiled=True),
    )
    places = places.astype(jnp.int32)
    col_tiles = width // tile
    grid = front.reshape(nrows // tile, tile, col_tiles, tile)
    grid = grid.at[places // col_tiles, :, places % col_tiles, :].add(arrived)
    return grid.reshape(nrows, width)


def eliminate(shard, panel, start, row_ids, col_ids, column):
    nrows, width = panel.shape
    diag = spread(panel[start : start + width], "leaf", 0)
    chol = jnp.linalg.cholesky(diag)
    eye = jnp.eye(width, dtype=F32)
    inverse = lax.linalg.triangular_solve(chol, eye, left_side=True, lower=True)
    prod = jnp.dot(panel, inverse.T, precision=EXACT)
    lower = jnp.where(row_ids[:, None] >= start, prod, panel)
    owner_row = column * width // nrows
    offset = column * width - owner_row * nrows
    mine = lax.dynamic_slice_in_dim(lower, offset, width, 0)
    across = spread(mine, "leaf", owner_row)
    trail = jnp.where(row_ids[:, None] >= start + width, lower, 0.0)
    updated = shard - jnp.dot(trail, across.T, precision=EXACT)
    updated = jnp.where(col_ids[None, :] >= start + width, updated, shard)
    return (jnp.where(column == start // width, lower, updated), lower)


def general(front, updates, target_owner, target_slot):
    nrows, width = front.shape
    column = lax.axis_index("front")
    row_ids = lax.axis_index("leaf") * nrows + jnp.arange(nrows, dtype=jnp.int32)
    col_ids = column * width + jnp.arange(width, dtype=jnp.int32)
    shard = assemble(front, updates, target_owner, target_slot)
    first = spread(shard, "front", 0)
    shard, lower = eliminate(shard, first, 0, row_ids, col_ids, column)
    second = spread(shard, "front", 1)
    shard, lower = eliminate(shard, second, width, row_ids, col_ids, column)
    return shard


def lane_of(x, c):
    return jnp.take_along_axis(x, jnp.full(x.shape, c, jnp.int32), axis=1)


def row_of(x, i):
    return jnp.broadcast_to(x[i : i + 1, :], x.shape)


def parts(x):
    high = x.astype(BF16).astype(F32)
    rest = x - high
    mid = rest.astype(BF16).astype(F32)
    return high, mid, (rest - mid).astype(BF16).astype(F32)


def factor_inverse(a):
    n = a.shape[0]
    panels, per, ahead = n // 8, 2, 2
    sub = lax.broadcasted_iota(jnp.int32, (8, n), 0)
    lane = lax.broadcasted_iota(jnp.int32, (8, n), 1)
    work = [
        [a[8 * k : 8 * k + 8, :], jnp.where(lane == sub + 8 * k, 1.0, 0.0).astype(F32)]
        for k in range(panels)
    ]
    out, held = [], []
    for k in range(panels):
        rows, ident = work[k]
        cols = [lane_of(rows, 8 * k + j) for j in range(8)]
        d = {(i, j): row_of(cols[j], i) for j in range(8) for i in range(j, 8)}
        up = [row_of(rows, j) for j in range(8)]
        inv = [row_of(ident, j) for j in range(8)]
        last = min(panels - 1, (k // per + 1) * per - 1 + ahead)
        below = {
            b: [lane_of(work[b][0], 8 * k + j) for j in range(8)]
            for b in range(k + 1, last + 1)
        }
        for j in range(8):
            r = lax.rsqrt(d[j, j])
            for i in range(j + 1, 8):
                d[i, j] = d[i, j] * r
            for i in range(j + 1, 8):
                for m in range(j + 1, i + 1):
                    d[i, m] = d[i, m] - d[i, j] * d[m, j]
            up[j] = up[j] * r
            inv[j] = inv[j] * r
            for i in range(j + 1, 8):
                up[i] = up[i] - d[i, j] * up[j]
                inv[i] = inv[i] - d[i, j] * inv[j]
            for b, c in below.items():
                c[j] = c[j] * r
                for i in range(j + 1, 8):
                    c[i] = c[i] - d[i, j] * c[j]
                work[b] = [work[b][0] - c[j] * up[j], work[b][1] - c[j] * inv[j]]
        u, w = up[0], inv[0]
        for j in range(1, 8):
            u = jnp.where(sub == j, up[j], u)
            w = jnp.where(sub == j, inv[j], w)
        out.append(w)
        held.append((u, w))
        first = k + 1 + ahead
        if k % per == per - 1 and first < panels:
            us = jnp.concatenate([p[0] for p in held], 0)
            ws = jnp.concatenate([p[1] for p in held], 0)
            uh, um, ul = parts(us)
            wh, wm, wl = parts(ws)
            right = jnp.concatenate(
                [
                    jnp.concatenate([uh, um, ul, uh, um, uh], 0),
                    jnp.concatenate([wh, wm, wl, wh, wm, wh], 0),
                ],
                1,
            ).astype(BF16)
            left = jnp.concatenate([uh, uh, uh, um, um, ul], 0).T
            left = left[8 * first :, :].astype(BF16)
            change = jnp.dot(left, right, preferred_element_type=F32)
            for b in range(first, panels):
                part = change[8 * (b - first) : 8 * (b - first + 1), :]
                work[b] = [work[b][0] - part[:, :n], work[b][1] - part[:, n:]]
        if k % per == per - 1:
            held = []
    return jnp.concatenate(out, 0)


def dot(a, b):
    return jnp.dot(a, b, precision=EXACT, preferred_element_type=F32)


def dot_t(a, b):
    return lax.dot_general(
        a, b, (((1,), (1,)), ((), ())), precision=EXACT, preferred_element_type=F32
    )


def two_parts(a):
    high = a.astype(BF16)
    return high, (a - high.astype(F32)).astype(BF16)


def wide(a):
    high, low = two_parts(a)
    return jnp.concatenate([high, low, high], 1)


def times(a, b):
    high, low = two_parts(b)
    return lax.dot_general(
        a,
        jnp.concatenate([high, high, low], 1),
        (((1,), (1,)), ((), ())),
        preferred_element_type=F32,
    )


def store_inverse(ref, blocks):
    w11, w21, w22 = blocks
    h = w11.shape[0]
    ref[:h, :h] = w11
    ref[:h, h:] = jnp.zeros_like(w11)
    ref[h:, :h] = w21
    ref[h:, h:] = w22


def symmetric(a):
    return (a + a.T) * 0.5


def place_of(tags):
    return tags[0, 0].astype(jnp.int32)


def add_block(ref, block, place, tile, start=0):
    down = pl.multiple_of(place // 2 * tile, tile)
    right = pl.multiple_of(start + place % 2 * tile, tile)
    ref[pl.ds(down, tile), pl.ds(right, tile)] += block


def add_band_blocks(ref, blocks, width):
    for b in blocks:
        tile = b.shape[1]
        for owner in range(2):
            tag = b[2 * tile + 8 * owner : 2 * tile + 8 * owner + 8, :]
            block = b[owner * tile : (owner + 1) * tile, :]
            add_block(ref, block, place_of(tag), tile, owner * width)


def square_ids(n):
    return lax.broadcasted_iota(jnp.int32, (n, n), 0), lax.broadcasted_iota(jnp.int32, (n, n), 1)


def pack(ref, s):
    n = s.shape[0] // 2
    row, col = square_ids(n)
    ref[:n, :] = jnp.where(row >= col, s[:n, :n], s[n:, n:])
    ref[n : 2 * n, :] = s[n:, :n]
    diag = jnp.sum(jnp.where(row == col, s[n:, n:], 0.0), 0, keepdims=True)
    ref[2 * n : 2 * n + 8, :] = jnp.broadcast_to(diag, (8, n))


def unpack(ref):
    n = ref.shape[1]
    row, col = square_ids(n)
    both, low = ref[:n, :], ref[n : 2 * n, :]
    turned = both.T
    s00 = jnp.where(row >= col, both, turned)
    s11 = jnp.where(row < col, both, jnp.where(row > col, turned, ref[2 * n : 2 * n + 1, :]))
    return jnp.concatenate(
        [jnp.concatenate([s00, low.T], 1), jnp.concatenate([low, s11], 1)], 0
    )


def put_rows(ref, start, rows):
    n = ref.shape[1]
    ref[start : start + n, :] = rows[:, :n]
    ref[start + n : start + 2 * n, :] = rows[:, n:]


def get_rows(ref, start):
    n = ref.shape[1]
    return jnp.concatenate([ref[start : start + n, :], ref[start + n : start + 2 * n, :]], 1)


def sort_kernel(owner, slot, info, updates, front, out_ref, pay_ref, diag_ref, square, sems, side):
    sends, tile = updates.shape[:2]
    width = front.shape[1]
    near_diag = info[3] < 2
    corner = pltpu.make_async_copy(front, square, side)

    @pl.when(near_diag)
    def _():
        corner.start()

    out_ref[...] = jnp.zeros_like(out_ref)
    copies = [
        pltpu.make_async_copy(updates.at[j], out_ref.at[owner[j], pl.ds(0, tile), :], sems.at[j])
        for j in range(sends)
    ]
    for j in range(sends):
        copies[j].start()
        out_ref[owner[j], tile:, :] = jnp.full((8, tile), slot[j].astype(F32))

    @pl.when(near_diag)
    def _():
        corner.wait()

    @pl.when(info[3] == 0)
    def _():
        pack(diag_ref, square[:width, :])
        put_rows(diag_ref, width + 8, square[width : width + tile, :])

    @pl.when(info[3] == 1)
    def _():
        pack(diag_ref, square[width:, :])
        put_rows(diag_ref, width + 8, square[:width, tile:].T)

    for c in copies:
        c.wait()
    for o in range(2):
        pay_ref[o * tile : (o + 1) * tile, :] = out_ref[o, :tile, :]
        pay_ref[2 * tile + 8 * o : 2 * tile + 8 * o + 8, :] = out_ref[o, tile:, :]


def diagonal_kernel(info, diag, hop1, hop2, *refs):
    blocks, (diag_ref, band, part) = refs[:8], refs[8:]
    tile = diag.shape[1]
    width = 2 * tile

    @pl.when(info[0] == 0)
    def _():
        band[...] = jnp.zeros_like(band)
        add_band_blocks(band, blocks, width)
        for z, d in enumerate((diag, hop2, hop1, hop2)):

            @pl.when(info[1] == z)
            def _(d=d):
                diag_ref[...] = d[...]

        @pl.when(info[2] == 0)
        def _():
            pack(part, symmetric(band[:width, :width]))
            put_rows(part, width + 8, band[width : width + tile, :width])

        @pl.when(info[2] == 1)
        def _():
            pack(part, symmetric(band[width:, width:]))
            put_rows(part, width + 8, band[width + tile :, :width])

        diag_ref[...] += part[...]


def matched_kernel(info, turned, *refs):
    blocks, (out_ref, band) = refs[:8], refs[8:]
    width = turned.shape[1]

    @pl.when((info[0] == info[1]) & (info[0] > 0))
    def _():
        band[...] = jnp.zeros_like(band)
        add_band_blocks(band, blocks, width)
        start = pl.multiple_of(info[2] * width, width)
        out_ref[...] = turned[...].T + band[pl.ds(start, width), :]


def factor_kernel(info, here, there, out_ref, top, bottom, done, sems):
    tile = here.shape[1]
    width = 2 * tile

    @pl.when(info[2] == 0)
    def _():
        top[...] = here[...]
        bottom[...] = there[...]

    @pl.when(info[2] == 1)
    def _():
        top[...] = there[...]
        bottom[...] = here[...]

    copies = [pltpu.make_async_copy(done.at[i], out_ref.at[i], sems.at[i]) for i in range(3)]
    a = unpack(top)
    d = jnp.concatenate([get_rows(top, width + 8), get_rows(bottom, width + 8)], 0)
    w11 = factor_inverse(a[:tile, :tile])
    low = dot_t(a[tile:, :tile], w11)
    left = dot_t(d[:, :tile], w11)
    w22 = factor_inverse(a[tile:, tile:] - dot_t(low, low))
    rest = d[:, tile:] - dot_t(left, low)
    s = unpack(bottom) - dot_t(left, left)
    right = dot_t(rest, w22)
    store_inverse(done.at[0], (w11, -dot(w22, dot(low, w11)), w22))
    done[1] = jnp.concatenate([left, right], 1)
    copies[0].start()
    copies[1].start()
    upper, lower = right[:tile, :], right[tile:, :]
    w11 = factor_inverse(s[:tile, :tile] - dot_t(upper, upper))
    low = dot_t(s[tile:, :tile] - dot_t(lower, upper), w11)
    w22 = factor_inverse(s[tile:, tile:] - dot_t(lower, lower) - dot_t(low, low))
    store_inverse(done.at[2], (w11, -dot(w22, dot(low, w11)), w22))
    copies[2].start()
    for c in copies:
        c.wait()


def last_kernel(info, *refs):
    (shard, arrived, piece, piece2, matched, m1, m2, m3, factors), blocks = refs[:9], refs[9:17]
    out_ref, band, line, work, halves, came, pays, tri, sems = refs[17:]
    tile = came.shape[2]
    nrows, width = out_ref.shape
    group, layer, core, column = info[0], info[1], info[2], info[4]
    copies = [
        pltpu.make_async_copy(src, dst, sems.at[i])
        for i, (src, dst) in enumerate(
            [
                (shard, out_ref),
                (arrived, came),
                (piece, halves.at[0]),
                (piece2, halves.at[1]),
                (factors, tri),
            ]
            + [(b, pays.at[i]) for i, b in enumerate(blocks)]
        )
    ]
    last = len(copies)
    for c in copies:
        c.start()
    way = jnp.where(group == 0, 3, jnp.where((group == 2) | ((group == 3) & (layer == 2)), 1, 2))
    way = jnp.where(group == layer, 0, way)
    for k, m in enumerate((matched, m1, m2, m3)):

        @pl.when(way == k)
        def _(m=m):
            pltpu.make_async_copy(m, line, sems.at[last]).start()

    copies[0].wait()
    copies[1].wait()
    for i in range(came.shape[0]):
        add_block(out_ref, came[i, :tile, :], place_of(came[i, tile:, :]), tile)
    copies[2].wait()
    copies[3].wait()
    by_rows = (layer > 0) & ((group == 1) | (layer > 1))
    for c in range(2):
        side = jnp.where(core == 0, c, 1 - c)

        @pl.when(by_rows)
        def _(c=c, side=side):
            band[c * width : (c + 1) * width, :] = halves[side].T

        @pl.when(~by_rows)
        def _(c=c, side=side):
            band[:, c * width : (c + 1) * width] = halves[side]

    for c in copies[4:]:
        c.wait()
    pltpu.make_async_copy(matched, line, sems.at[last]).wait()

    @pl.when(group > 0)
    def _():
        add_band_blocks(band, [pays.at[i] for i in range(len(blocks))], width)

    w1, l21, v = tri[0], tri[1], tri[2]

    @pl.when(column == 0)
    def _():
        out_ref[...] = times(wide(out_ref[...]), w1)

    @pl.when(column > 0)
    def _():
        @pl.when(group == 0)
        def _():
            work[:width, :] = jnp.zeros((width, width), F32)
            work[width:, :] = l21

        @pl.when(group > 0)
        def _():
            work[...] = times(wide(band[:, :width]), w1)

        first = wide(work[...])

        @pl.when(column == 1)
        def _():
            rows = group * nrows + lax.broadcasted_iota(jnp.int32, (nrows, width), 0)
            own = out_ref[...]
            second = times(wide(own - times(first, l21)), v)
            out_ref[...] = jnp.where(rows >= width, second, own)

        @pl.when((column > 1) & (group == 0))
        def _():
            out_ref[...] -= times(first, times(wide(line[:, :width]), w1))

        @pl.when((column > 1) & (group > 0))
        def _():
            mine = times(wide(line[:, :width]), w1)
            rest = times(wide(line[:, width:] - times(wide(mine), l21)), v)
            second = times(wide(band[:, width:] - times(first, l21)), v)
            out_ref[...] = out_ref[...] - times(first, mine) - times(wide(second), rest)


def kernel(body, outs, args, smem=1, scratch=(), flops=1 << 20, sems=(), away=False, anywhere=()):
    space = pltpu.HBM if away else pltpu.VMEM
    spec = [pl.BlockSpec(memory_space=pltpu.SMEM)] * smem
    out_space = pltpu.HBM if isinstance(outs, type(pltpu.HBM((8, 128), F32))) else pltpu.VMEM
    spec += [
        pl.BlockSpec(memory_space=pl.ANY if i in anywhere else space) for i in range(len(args) - smem)
    ]
    if away:
        args = args[:smem] + tuple(
            a if i in anywhere else pltpu.with_memory_space_constraint(a, pltpu.HBM)
            for i, a in enumerate(args[smem:])
        )
    sizes = [math.prod(o.shape) for o in jax.tree.leaves(outs)] + [math.prod(s) for s in scratch]
    if not away:
        sizes += [a.size for a in args[smem:]]
    return pl.pallas_call(
        body,
        out_shape=outs,
        in_specs=spec,
        out_specs=jax.tree.map(lambda o: pl.BlockSpec(memory_space=out_space), outs),
        scratch_shapes=[pltpu.VMEM(s, F32) for s in scratch]
        + [pltpu.SemaphoreType.DMA(s) for s in sems],
        compiler_params=pltpu.CompilerParams(vmem_limit_bytes=4 * sum(sizes) + (6 << 20)),
        cost_estimate=pl.CostEstimate(flops=flops, bytes_accessed=1 << 20, transcendentals=0),
    )(*args)


def aligned(front, updates, target_owner, target_slot):
    nrows, width = front.shape
    tile = updates.shape[1]
    nleaf, nfront = lax.axis_size("leaf"), lax.axis_size("front")
    groups, layers = range(nleaf), range(nfront // 2)
    group, column = lax.axis_index("leaf"), lax.axis_index("front")
    layer, core = column // 2, column % 2
    info = jnp.stack([group, layer, core, group * nfront + column, column]).astype(jnp.int32)

    def dev(g, z, c):
        return g * nfront + 2 * z + c

    def send(x, pairs):
        return lax.ppermute(x, AXES, pairs)

    def out(*shape):
        return jax.ShapeDtypeStruct(shape, F32)

    both = range(2)
    swap = [(dev(g, z, c), dev(g, z, 1 - c)) for g in groups for z in layers for c in both]

    packed = out(2 * width + 8, tile)
    outgoing, payload, diag = kernel(
        sort_kernel,
        (out(nfront, tile + 8, tile), out(2 * tile + 16, tile), packed),
        (target_owner, target_slot, info, updates, front),
        smem=3,
        scratch=[(nrows, width)],
        sems=[(updates.shape[0],), ()],
        away=True,
    )
    blocks = [payload]
    for s in layers[1:]:
        pairs = [(dev(g, z, c), dev(g, z ^ s, c)) for g in groups for z in layers for c in both]
        blocks.append(send(payload, pairs))
    blocks += [send(b, swap) for b in blocks]
    hop1 = send(diag, [(dev(0, 0, c), dev(0, 2, c)) for c in both])
    hop2 = send(
        jnp.where(layer == 0, diag, hop1), [(dev(0, z, c), dev(0, z + 1, c)) for z in (0, 2) for c in both]
    )
    early, outgoing, info = lax.optimization_barrier((front, outgoing, info))
    turned = send(early, [(dev(0, z, c), dev(z, z, c)) for z in layers[1:] for c in both])
    diag, turned = lax.optimization_barrier((diag, turned))

    diag = kernel(
        diagonal_kernel,
        packed,
        (info, diag, hop1, hop2, *blocks),
        scratch=[(nrows, 2 * width), packed.shape],
    )
    diag, outgoing, early, turned = lax.optimization_barrier((diag, outgoing, early, turned))
    got = [
        send(diag, [(dev(0, z, c), dev(s, z, c)) for z in layers for c in both]) for s in groups[1:]
    ]
    arrived = lax.all_to_all(outgoing, "front", split_axis=0, concat_axis=0, tiled=True)
    diag = jnp.where(group == 0, diag, got[0] + got[1] + got[2])
    diag2 = send(diag, swap)

    far = send(
        turned,
        [(dev(g, z, c), dev(g, y, c)) for g, z, y in ((1, 1, 2), (2, 2, 3), (3, 3, 2)) for c in both],
    )

    matched = kernel(
        matched_kernel, out(width, 2 * width), (info, turned, *blocks), scratch=[(nrows, 2 * width)]
    )
    matched, early, diag = lax.optimization_barrier((matched, early, diag))
    near = send(
        early,
        [(dev(g, 0, c), dev(g, 1, c)) for g in (2, 3) for c in both]
        + [(dev(0, 1, c), dev(1, 3, c)) for c in both],
    )
    away = [
        send(matched, [(dev(z, z, c), dev(g, z, c)) for z, g in pairs for c in both])
        for pairs in (((1, 2), (2, 3), (3, 2)), ((1, 3), (2, 1), (3, 1)), ((1, 0), (2, 0), (3, 0)))
    ]

    diag, diag2, far = lax.optimization_barrier((diag, diag2, far))
    factors = kernel(
        factor_kernel,
        pltpu.HBM((3, width, width), F32),
        (info, diag, diag2),
        scratch=[packed.shape] * 2 + [(3, width, width)],
        flops=1 << 33,
        sems=[(3,)],
    )
    factors, near, far = lax.optimization_barrier((factors, near, far))
    piece = jnp.where(layer == 0, front, jnp.where(group == layer, turned, near + far))
    piece2 = send(piece, swap)
    return kernel(
        last_kernel,
        out(nrows, width),
        (info, front, arrived, piece, piece2, matched, *away, factors, *blocks),
        scratch=[
            (nrows, 2 * width),
            (width, 2 * width),
            (nrows, width),
            (2, nrows, width),
            arrived.shape,
            (8,) + payload.shape,
            (3, width, width),
        ],
        flops=1 << 31,
        sems=[(16,)],
        away=True,
        anywhere=(2, 3, 5, 6, 7),
    )


def solution(mesh):
    nleaf, nfront = mesh.shape["leaf"], mesh.shape["front"]

    def shards(front, updates, target_owner, target_slot):
        nrows, width = front.shape
        tile = updates.shape[1]
        lines_up = (
            nrows == 2 * width
            and width == 2 * tile
            and nleaf == 4
            and nfront == 8
        )
        plan = aligned if lines_up else general
        return plan(front, updates, target_owner, target_slot)

    return jax.shard_map(
        shards,
        mesh=mesh,
        in_specs=(
            P("leaf", "front"),
            P(("leaf", "front"), None, None),
            P(("leaf", "front")),
            P(("leaf", "front")),
        ),
        out_specs=P("leaf", "front"),
        check_vma=False,
    )
```

```python
import math

import jax
import jax.numpy as jnp
from jax import lax
from jax.experimental import pallas as pl
from jax.experimental.pallas import tpu as pltpu
from jax.sharding import PartitionSpec as P

F32 = jnp.float32
BF16 = jnp.bfloat16
AXES = ("leaf", "front")
EXACT = lax.Precision.HIGHEST


def spread(value, axis, source):
    kept = jnp.where(lax.axis_index(axis) == source, value, 0).astype(value.dtype)
    return lax.psum(kept, axis)


def assemble(front, updates, target_owner, target_slot):
    nrows, width = front.shape
    tile = updates.shape[1]
    nfront = lax.axis_size("front")
    buffer = jnp.zeros((nfront, tile, tile), F32).at[target_owner].set(updates)
    labels = jnp.zeros((nfront,), F32).at[target_owner].set(target_slot.astype(F32))
    arrived, places = (
        lax.all_to_all(buffer, "front", split_axis=0, concat_axis=0, tiled=True),
        lax.all_to_all(labels, "front", split_axis=0, concat_axis=0, tiled=True),
    )
    places = places.astype(jnp.int32)
    col_tiles = width // tile
    grid = front.reshape(nrows // tile, tile, col_tiles, tile)
    grid = grid.at[places // col_tiles, :, places % col_tiles, :].add(arrived)
    return grid.reshape(nrows, width)


def eliminate(shard, panel, start, row_ids, col_ids, column):
    nrows, width = panel.shape
    diag = spread(panel[start : start + width], "leaf", 0)
    chol = jnp.linalg.cholesky(diag)
    eye = jnp.eye(width, dtype=F32)
    inverse = lax.linalg.triangular_solve(chol, eye, left_side=True, lower=True)
    prod = jnp.dot(panel, inverse.T, precision=EXACT)
    lower = jnp.where(row_ids[:, None] >= start, prod, panel)
    owner_row = column * width // nrows
    offset = column * width - owner_row * nrows
    mine = lax.dynamic_slice_in_dim(lower, offset, width, 0)
    across = spread(mine, "leaf", owner_row)
    trail = jnp.where(row_ids[:, None] >= start + width, lower, 0.0)
    updated = shard - jnp.dot(trail, across.T, precision=EXACT)
    updated = jnp.where(col_ids[None, :] >= start + width, updated, shard)
    return (jnp.where(column == start // width, lower, updated), lower)


def general(front, updates, target_owner, target_slot):
    nrows, width = front.shape
    column = lax.axis_index("front")
    row_ids = lax.axis_index("leaf") * nrows + jnp.arange(nrows, dtype=jnp.int32)
    col_ids = column * width + jnp.arange(width, dtype=jnp.int32)
    shard = assemble(front, updates, target_owner, target_slot)
    first = spread(shard, "front", 0)
    shard, lower = eliminate(shard, first, 0, row_ids, col_ids, column)
    second = spread(shard, "front", 1)
    shard, lower = eliminate(shard, second, width, row_ids, col_ids, column)
    return shard


def lane_of(x, c):
    return jnp.take_along_axis(x, jnp.full(x.shape, c, jnp.int32), axis=1)


def row_of(x, i):
    return jnp.broadcast_to(x[i : i + 1, :], x.shape)


def parts(x):
    high = x.astype(BF16).astype(F32)
    rest = x - high
    mid = rest.astype(BF16).astype(F32)
    return high, mid, (rest - mid).astype(BF16).astype(F32)


def factor_inverse(a):
    n = a.shape[0]
    panels, per, ahead = n // 8, 2, 2
    sub = lax.broadcasted_iota(jnp.int32, (8, n), 0)
    lane = lax.broadcasted_iota(jnp.int32, (8, n), 1)
    work = [
        [a[8 * k : 8 * k + 8, :], jnp.where(lane == sub + 8 * k, 1.0, 0.0).astype(F32)]
        for k in range(panels)
    ]
    out, held = [], []
    for k in range(panels):
        rows, ident = work[k]
        if k == 0:
            cols = [lane_of(rows, j) for j in range(8)]
        last = min(panels - 1, max(k + 1, (k // per + 1) * per - 1 + ahead))
        below = {
            b: [lane_of(work[b][0], 8 * k + j) for j in range(8)]
            for b in range(k + 1, last + 1)
        }
        if k + 1 < panels:
            following = [lane_of(work[k + 1][0], 8 * k + 8 + j) for j in range(8)]
        scale = jnp.zeros((8, n), F32)
        for j in range(8):
            s = {i: row_of(cols[j], i) for i in range(j, 8)}
            r = lax.rsqrt(s[j])
            inverse = r * r
            ratio = {i: s[i] * inverse for i in range(j + 1, 8)}
            if j < 7:
                cols[j + 1] = cols[j + 1] - (cols[j] * s[j + 1]) * inverse
            for i in range(j + 2, 8):
                cols[i] = cols[i] - cols[j] * ratio[i]
            up, ue = row_of(rows, j), row_of(ident, j)
            if j < 7:
                part = jnp.where(sub > j, cols[j] * inverse, 0.0)
                rows, ident = rows - part * up, ident - part * ue
            scale = jnp.where(sub == j, r, scale)
            for b, c in below.items():
                cj = c[j] * inverse
                if b == k + 1:
                    for i in range(8):
                        following[i] = following[i] - cj * row_of(c[j], i)
                for i in range(j + 1, 8):
                    c[i] = c[i] - c[j] * ratio[i]
                work[b] = [work[b][0] - cj * up, work[b][1] - cj * ue]
        if k + 1 < panels:
            cols = following
        u, w = rows * scale, ident * scale
        out.append(w)
        held.append((u, w))
        first = k + 1 + ahead
        if k % per == per - 1 and first < panels:
            us = jnp.concatenate([p[0] for p in held], 0)
            ws = jnp.concatenate([p[1] for p in held], 0)
            uh, um, ul = parts(us)
            wh, wm, wl = parts(ws)
            right = jnp.concatenate(
                [
                    jnp.concatenate([uh, um, ul, uh, um, uh], 0),
                    jnp.concatenate([wh, wm, wl, wh, wm, wh], 0),
                ],
                1,
            ).astype(BF16)
            left = jnp.concatenate([uh, uh, uh, um, um, ul], 0).T
            left = left[8 * first :, :].astype(BF16)
            change = jnp.dot(left, right, preferred_element_type=F32)
            for b in range(first, panels):
                part = change[8 * (b - first) : 8 * (b - first + 1), :]
                work[b] = [work[b][0] - part[:, :n], work[b][1] - part[:, n:]]
        if k % per == per - 1:
            held = []
    return jnp.concatenate(out, 0)


def dot(a, b):
    return jnp.dot(a, b, precision=EXACT, preferred_element_type=F32)


def dot_t(a, b):
    return lax.dot_general(
        a, b, (((1,), (1,)), ((), ())), precision=EXACT, preferred_element_type=F32
    )


def two_parts(a):
    high = a.astype(BF16)
    return high, (a - high.astype(F32)).astype(BF16)


def wide(a):
    high, low = two_parts(a)
    return jnp.concatenate([high, low, high], 1)


def times(a, b):
    high, low = two_parts(b)
    return lax.dot_general(
        a,
        jnp.concatenate([high, high, low], 1),
        (((1,), (1,)), ((), ())),
        preferred_element_type=F32,
    )


def store_inverse(ref, blocks):
    w11, w21, w22 = blocks
    h = w11.shape[0]
    ref[:h, :h] = w11
    ref[:h, h:] = jnp.zeros_like(w11)
    ref[h:, :h] = w21
    ref[h:, h:] = w22


def symmetric(a):
    return (a + a.T) * 0.5


def place_of(tags):
    return tags[0, 0].astype(jnp.int32)


def add_block(ref, block, place, tile, start=0):
    down = pl.multiple_of(place // 2 * tile, tile)
    right = pl.multiple_of(start + place % 2 * tile, tile)
    ref[pl.ds(down, tile), pl.ds(right, tile)] += block


def add_band_blocks(ref, blocks, width):
    for b in blocks:
        tile = b.shape[1]
        for owner in range(2):
            tag = b[2 * tile + 8 * owner : 2 * tile + 8 * owner + 8, :]
            block = b[owner * tile : (owner + 1) * tile, :]
            add_block(ref, block, place_of(tag), tile, owner * width)


def square_ids(n):
    return lax.broadcasted_iota(jnp.int32, (n, n), 0), lax.broadcasted_iota(jnp.int32, (n, n), 1)


def pack(ref, s):
    n = s.shape[0] // 2
    row, col = square_ids(n)
    ref[:n, :] = jnp.where(row >= col, s[:n, :n], s[n:, n:])
    ref[n : 2 * n, :] = s[n:, :n]
    diag = jnp.sum(jnp.where(row == col, s[n:, n:], 0.0), 0, keepdims=True)
    ref[2 * n : 2 * n + 8, :] = jnp.broadcast_to(diag, (8, n))


def unpack(ref):
    n = ref.shape[1]
    row, col = square_ids(n)
    both, low = ref[:n, :], ref[n : 2 * n, :]
    turned = both.T
    s00 = jnp.where(row >= col, both, turned)
    s11 = jnp.where(row < col, both, jnp.where(row > col, turned, ref[2 * n : 2 * n + 1, :]))
    return jnp.concatenate(
        [jnp.concatenate([s00, low.T], 1), jnp.concatenate([low, s11], 1)], 0
    )


def put_rows(ref, start, rows):
    n = ref.shape[1]
    ref[start : start + n, :] = rows[:, :n]
    ref[start + n : start + 2 * n, :] = rows[:, n:]


def get_rows(ref, start):
    n = ref.shape[1]
    return jnp.concatenate([ref[start : start + n, :], ref[start + n : start + 2 * n, :]], 1)


def sort_kernel(owner, slot, info, updates, front, out_ref, pay_ref, diag_ref, square, sems, side):
    sends, tile = updates.shape[:2]
    width = front.shape[1]
    near_diag = info[3] < 2
    corner = pltpu.make_async_copy(front, square, side)

    @pl.when(near_diag)
    def _():
        corner.start()

    out_ref[...] = jnp.zeros_like(out_ref)
    copies = [
        pltpu.make_async_copy(updates.at[j], out_ref.at[owner[j], pl.ds(0, tile), :], sems.at[j])
        for j in range(sends)
    ]
    for j in range(sends):
        copies[j].start()
        out_ref[owner[j], tile:, :] = jnp.full((8, tile), slot[j].astype(F32))

    @pl.when(near_diag)
    def _():
        corner.wait()

    @pl.when(info[3] == 0)
    def _():
        pack(diag_ref, square[:width, :])
        put_rows(diag_ref, width + 8, square[width : width + tile, :])

    @pl.when(info[3] == 1)
    def _():
        pack(diag_ref, square[width:, :])
        put_rows(diag_ref, width + 8, square[:width, tile:].T)

    for c in copies:
        c.wait()
    for o in range(2):
        pay_ref[o * tile : (o + 1) * tile, :] = out_ref[o, :tile, :]
        pay_ref[2 * tile + 8 * o : 2 * tile + 8 * o + 8, :] = out_ref[o, tile:, :]


def diagonal_kernel(info, diag, hop1, hop2, *refs):
    blocks, (diag_ref, band, part) = refs[:8], refs[8:]
    tile = diag.shape[1]
    width = 2 * tile

    @pl.when(info[0] == 0)
    def _():
        band[...] = jnp.zeros_like(band)
        add_band_blocks(band, blocks, width)
        for z, d in enumerate((diag, hop2, hop1, hop2)):

            @pl.when(info[1] == z)
            def _(d=d):
                diag_ref[...] = d[...]

        @pl.when(info[2] == 0)
        def _():
            pack(part, symmetric(band[:width, :width]))
            put_rows(part, width + 8, band[width : width + tile, :width])

        @pl.when(info[2] == 1)
        def _():
            pack(part, symmetric(band[width:, width:]))
            put_rows(part, width + 8, band[width + tile :, :width])

        diag_ref[...] += part[...]


def matched_kernel(info, turned, *refs):
    blocks, (out_ref, band) = refs[:8], refs[8:]
    width = turned.shape[1]

    @pl.when((info[0] == info[1]) & (info[0] > 0))
    def _():
        band[...] = jnp.zeros_like(band)
        add_band_blocks(band, blocks, width)
        start = pl.multiple_of(info[2] * width, width)
        out_ref[...] = turned[...].T + band[pl.ds(start, width), :]


def factor_kernel(info, here, there, out_ref, top, bottom, done, sems):
    tile = here.shape[1]
    width = 2 * tile

    @pl.when(info[2] == 0)
    def _():
        top[...] = here[...]
        bottom[...] = there[...]

    @pl.when(info[2] == 1)
    def _():
        top[...] = there[...]
        bottom[...] = here[...]

    copies = [pltpu.make_async_copy(done.at[i], out_ref.at[i], sems.at[i]) for i in range(3)]
    a = unpack(top)
    d = jnp.concatenate([get_rows(top, width + 8), get_rows(bottom, width + 8)], 0)
    w11 = factor_inverse(a[:tile, :tile])
    low = dot_t(a[tile:, :tile], w11)
    left = dot_t(d[:, :tile], w11)
    w22 = factor_inverse(a[tile:, tile:] - dot_t(low, low))
    rest = d[:, tile:] - dot_t(left, low)
    s = unpack(bottom) - dot_t(left, left)
    right = dot_t(rest, w22)
    store_inverse(done.at[0], (w11, -dot(w22, dot(low, w11)), w22))
    done[1] = jnp.concatenate([left, right], 1)
    copies[0].start()
    copies[1].start()
    upper, lower = right[:tile, :], right[tile:, :]
    w11 = factor_inverse(s[:tile, :tile] - dot_t(upper, upper))
    low = dot_t(s[tile:, :tile] - dot_t(lower, upper), w11)
    w22 = factor_inverse(s[tile:, tile:] - dot_t(lower, lower) - dot_t(low, low))
    store_inverse(done.at[2], (w11, -dot(w22, dot(low, w11)), w22))
    copies[2].start()
    for c in copies:
        c.wait()


def last_kernel(info, *refs):
    (shard, arrived, piece, piece2, matched, m1, m2, m3, factors), blocks = refs[:9], refs[9:17]
    out_ref, band, line, work, halves, came, pays, tri, sems = refs[17:]
    tile = came.shape[2]
    nrows, width = out_ref.shape
    group, layer, core, column = info[0], info[1], info[2], info[4]
    copies = [
        pltpu.make_async_copy(src, dst, sems.at[i])
        for i, (src, dst) in enumerate(
            [
                (shard, out_ref),
                (arrived, came),
                (piece, halves.at[0]),
                (piece2, halves.at[1]),
                (factors, tri),
            ]
            + [(b, pays.at[i]) for i, b in enumerate(blocks)]
        )
    ]
    last = len(copies)
    for c in copies:
        c.start()
    way = jnp.where(group == 0, 3, jnp.where((group == 2) | ((group == 3) & (layer == 2)), 1, 2))
    way = jnp.where(group == layer, 0, way)
    for k, m in enumerate((matched, m1, m2, m3)):

        @pl.when(way == k)
        def _(m=m):
            pltpu.make_async_copy(m, line, sems.at[last]).start()

    copies[0].wait()
    copies[1].wait()
    for i in range(came.shape[0]):
        add_block(out_ref, came[i, :tile, :], place_of(came[i, tile:, :]), tile)
    copies[2].wait()
    copies[3].wait()
    by_rows = (layer > 0) & (((group == 1) & (layer < 3)) | ((group > 1) & (layer > 1)))
    for c in range(2):
        side = jnp.where(core == 0, c, 1 - c)

        @pl.when(by_rows)
        def _(c=c, side=side):
            band[c * width : (c + 1) * width, :] = halves[side].T

        @pl.when(~by_rows)
        def _(c=c, side=side):
            band[:, c * width : (c + 1) * width] = halves[side]

    for c in copies[4:]:
        c.wait()
    pltpu.make_async_copy(matched, line, sems.at[last]).wait()

    @pl.when(group > 0)
    def _():
        add_band_blocks(band, [pays.at[i] for i in range(len(blocks))], width)

    w1, l21, v = tri[0], tri[1], tri[2]

    @pl.when(column == 0)
    def _():
        out_ref[...] = times(wide(out_ref[...]), w1)

    @pl.when(column > 0)
    def _():
        @pl.when(group == 0)
        def _():
            work[:width, :] = jnp.zeros((width, width), F32)
            work[width:, :] = l21

        @pl.when(group > 0)
        def _():
            work[...] = times(wide(band[:, :width]), w1)

        first = wide(work[...])

        @pl.when(column == 1)
        def _():
            rows = group * nrows + lax.broadcasted_iota(jnp.int32, (nrows, width), 0)
            own = out_ref[...]
            second = times(wide(own - times(first, l21)), v)
            out_ref[...] = jnp.where(rows >= width, second, own)

        @pl.when((column > 1) & (group == 0))
        def _():
            out_ref[...] -= times(first, times(wide(line[:, :width]), w1))

        @pl.when((column > 1) & (group > 0))
        def _():
            mine = times(wide(line[:, :width]), w1)
            rest = times(wide(line[:, width:] - times(wide(mine), l21)), v)
            second = times(wide(band[:, width:] - times(first, l21)), v)
            out_ref[...] = out_ref[...] - times(first, mine) - times(wide(second), rest)


def kernel(body, outs, args, smem=1, scratch=(), flops=1 << 20, sems=(), away=False, anywhere=()):
    space = pltpu.HBM if away else pltpu.VMEM
    spec = [pl.BlockSpec(memory_space=pltpu.SMEM)] * smem
    out_space = pltpu.HBM if isinstance(outs, type(pltpu.HBM((8, 128), F32))) else pltpu.VMEM
    spec += [
        pl.BlockSpec(memory_space=pl.ANY if i in anywhere else space) for i in range(len(args) - smem)
    ]
    if away:
        args = args[:smem] + tuple(
            a if i in anywhere else pltpu.with_memory_space_constraint(a, pltpu.HBM)
            for i, a in enumerate(args[smem:])
        )
    sizes = [math.prod(o.shape) for o in jax.tree.leaves(outs)] + [math.prod(s) for s in scratch]
    if not away:
        sizes += [a.size for a in args[smem:]]
    return pl.pallas_call(
        body,
        out_shape=outs,
        in_specs=spec,
        out_specs=jax.tree.map(lambda o: pl.BlockSpec(memory_space=out_space), outs),
        scratch_shapes=[pltpu.VMEM(s, F32) for s in scratch]
        + [pltpu.SemaphoreType.DMA(s) for s in sems],
        compiler_params=pltpu.CompilerParams(vmem_limit_bytes=4 * sum(sizes) + (6 << 20)),
        cost_estimate=pl.CostEstimate(flops=flops, bytes_accessed=1 << 20, transcendentals=0),
    )(*args)


def aligned(front, updates, target_owner, target_slot):
    nrows, width = front.shape
    tile = updates.shape[1]
    nleaf, nfront = lax.axis_size("leaf"), lax.axis_size("front")
    groups, layers = range(nleaf), range(nfront // 2)
    group, column = lax.axis_index("leaf"), lax.axis_index("front")
    layer, core = column // 2, column % 2
    info = jnp.stack([group, layer, core, group * nfront + column, column]).astype(jnp.int32)

    def dev(g, z, c):
        return g * nfront + 2 * z + c

    def send(x, pairs):
        return lax.ppermute(x, AXES, pairs)

    def out(*shape):
        return jax.ShapeDtypeStruct(shape, F32)

    both = range(2)
    swap = [(dev(g, z, c), dev(g, z, 1 - c)) for g in groups for z in layers for c in both]

    packed = out(2 * width + 8, tile)
    outgoing, payload, diag = kernel(
        sort_kernel,
        (out(nfront, tile + 8, tile), out(2 * tile + 16, tile), packed),
        (target_owner, target_slot, info, updates, front),
        smem=3,
        scratch=[(nrows, width)],
        sems=[(updates.shape[0],), ()],
        away=True,
    )
    blocks = [payload]
    for s in layers[1:]:
        pairs = [(dev(g, z, c), dev(g, z ^ s, c)) for g in groups for z in layers for c in both]
        blocks.append(send(payload, pairs))
    blocks += [send(b, swap) for b in blocks]
    hop1 = send(diag, [(dev(0, 0, c), dev(0, 2, c)) for c in both])
    hop2 = send(
        jnp.where(layer == 0, diag, hop1), [(dev(0, z, c), dev(0, z + 1, c)) for z in (0, 2) for c in both]
    )
    early, outgoing, info = lax.optimization_barrier((front, outgoing, info))
    turned = send(early, [(dev(0, z, c), dev(z, z, c)) for z in layers[1:] for c in both])
    diag, turned = lax.optimization_barrier((diag, turned))

    diag = kernel(
        diagonal_kernel,
        packed,
        (info, diag, hop1, hop2, *blocks),
        scratch=[(nrows, 2 * width), packed.shape],
    )
    diag, outgoing, early, turned = lax.optimization_barrier((diag, outgoing, early, turned))
    got = [
        send(diag, [(dev(0, z, c), dev(s, z, c)) for z in layers for c in both]) for s in groups[1:]
    ]
    diag = jnp.where(group == 0, diag, got[0] + got[1] + got[2])
    diag2 = send(diag, swap)

    hops = ((1, 0, 3), (2, 0, 1), (3, 0, 1), (1, 1, 2), (2, 2, 3), (3, 3, 2))
    far = send(
        jnp.where(layer == 0, early, turned), [(dev(g, z, c), dev(g, y, c)) for g, z, y in hops for c in both]
    )

    matched = kernel(
        matched_kernel, out(width, 2 * width), (info, turned, *blocks), scratch=[(nrows, 2 * width)]
    )
    matched, diag, outgoing = lax.optimization_barrier((matched, diag, outgoing))
    arrived = lax.all_to_all(outgoing, "front", split_axis=0, concat_axis=0, tiled=True)
    away = [
        send(matched, [(dev(z, z, c), dev(g, z, c)) for z, g in pairs for c in both])
        for pairs in (((1, 2), (2, 3), (3, 2)), ((1, 3), (2, 1), (3, 1)), ((1, 0), (2, 0), (3, 0)))
    ]

    diag, diag2, far = lax.optimization_barrier((diag, diag2, far))
    factors = kernel(
        factor_kernel,
        pltpu.HBM((3, width, width), F32),
        (info, diag, diag2),
        scratch=[packed.shape] * 2 + [(3, width, width)],
        flops=1 << 33,
        sems=[(3,)],
    )
    factors, far = lax.optimization_barrier((factors, far))
    piece = jnp.where(layer == 0, front, jnp.where(group == layer, turned, far))
    piece2 = send(piece, swap)
    return kernel(
        last_kernel,
        out(nrows, width),
        (info, front, arrived, piece, piece2, matched, *away, factors, *blocks),
        scratch=[
            (nrows, 2 * width),
            (width, 2 * width),
            (nrows, width),
            (2, nrows, width),
            arrived.shape,
            (8,) + payload.shape,
            (3, width, width),
        ],
        flops=1 << 31,
        sems=[(16,)],
        away=True,
        anywhere=(2, 3, 5, 6, 7),
    )


def solution(mesh):
    nleaf, nfront = mesh.shape["leaf"], mesh.shape["front"]

    def shards(front, updates, target_owner, target_slot):
        nrows, width = front.shape
        tile = updates.shape[1]
        lines_up = (
            nrows == 2 * width
            and width == 2 * tile
            and nleaf == 4
            and nfront == 8
        )
        plan = aligned if lines_up else general
        return plan(front, updates, target_owner, target_slot)

    return jax.shard_map(
        shards,
        mesh=mesh,
        in_specs=(
            P("leaf", "front"),
            P(("leaf", "front"), None, None),
            P(("leaf", "front")),
            P(("leaf", "front")),
        ),
        out_specs=P("leaf", "front"),
        check_vma=False,
    )
```

```python
import math

import jax
import jax.numpy as jnp
from jax import lax
from jax.experimental import pallas as pl
from jax.experimental.pallas import tpu as pltpu
from jax.sharding import PartitionSpec as P

F32 = jnp.float32
BF16 = jnp.bfloat16
AXES = ("leaf", "front")
EXACT = lax.Precision.HIGHEST


def spread(value, axis, source):
    kept = jnp.where(lax.axis_index(axis) == source, value, 0).astype(value.dtype)
    return lax.psum(kept, axis)


def assemble(front, updates, target_owner, target_slot):
    nrows, width = front.shape
    tile = updates.shape[1]
    nfront = lax.axis_size("front")
    buffer = jnp.zeros((nfront, tile, tile), F32).at[target_owner].set(updates)
    labels = jnp.zeros((nfront,), F32).at[target_owner].set(target_slot.astype(F32))
    arrived, places = (
        lax.all_to_all(buffer, "front", split_axis=0, concat_axis=0, tiled=True),
        lax.all_to_all(labels, "front", split_axis=0, concat_axis=0, tiled=True),
    )
    places = places.astype(jnp.int32)
    col_tiles = width // tile
    grid = front.reshape(nrows // tile, tile, col_tiles, tile)
    grid = grid.at[places // col_tiles, :, places % col_tiles, :].add(arrived)
    return grid.reshape(nrows, width)


def eliminate(shard, panel, start, row_ids, col_ids, column):
    nrows, width = panel.shape
    diag = spread(panel[start : start + width], "leaf", 0)
    chol = jnp.linalg.cholesky(diag)
    eye = jnp.eye(width, dtype=F32)
    inverse = lax.linalg.triangular_solve(chol, eye, left_side=True, lower=True)
    prod = jnp.dot(panel, inverse.T, precision=EXACT)
    lower = jnp.where(row_ids[:, None] >= start, prod, panel)
    owner_row = column * width // nrows
    offset = column * width - owner_row * nrows
    mine = lax.dynamic_slice_in_dim(lower, offset, width, 0)
    across = spread(mine, "leaf", owner_row)
    trail = jnp.where(row_ids[:, None] >= start + width, lower, 0.0)
    updated = shard - jnp.dot(trail, across.T, precision=EXACT)
    updated = jnp.where(col_ids[None, :] >= start + width, updated, shard)
    return (jnp.where(column == start // width, lower, updated), lower)


def general(front, updates, target_owner, target_slot):
    nrows, width = front.shape
    column = lax.axis_index("front")
    row_ids = lax.axis_index("leaf") * nrows + jnp.arange(nrows, dtype=jnp.int32)
    col_ids = column * width + jnp.arange(width, dtype=jnp.int32)
    shard = assemble(front, updates, target_owner, target_slot)
    first = spread(shard, "front", 0)
    shard, lower = eliminate(shard, first, 0, row_ids, col_ids, column)
    second = spread(shard, "front", 1)
    shard, lower = eliminate(shard, second, width, row_ids, col_ids, column)
    return shard


def lane_of(x, c):
    return jnp.take_along_axis(x, jnp.full(x.shape, c, jnp.int32), axis=1)


def row_of(x, i):
    return jnp.broadcast_to(x[i : i + 1, :], x.shape)


def parts(x):
    high = x.astype(BF16).astype(F32)
    rest = x - high
    mid = rest.astype(BF16).astype(F32)
    return high, mid, (rest - mid).astype(BF16).astype(F32)


def factor_inverse(a):
    n = a.shape[0]
    panels, per, ahead = n // 8, 2, 2
    sub = lax.broadcasted_iota(jnp.int32, (8, n), 0)
    lane = lax.broadcasted_iota(jnp.int32, (8, n), 1)
    work = [
        [a[8 * k : 8 * k + 8, :], jnp.where(lane == sub + 8 * k, 1.0, 0.0).astype(F32)]
        for k in range(panels)
    ]
    out, held = [], []
    for k in range(panels):
        rows, ident = work[k]
        if k == 0:
            cols = [lane_of(rows, j) for j in range(8)]
        last = min(panels - 1, max(k + 1, (k // per + 1) * per - 1 + ahead))
        below = {
            b: [lane_of(work[b][0], 8 * k + j) for j in range(8)]
            for b in range(k + 1, last + 1)
        }
        if k + 1 < panels:
            following = [lane_of(work[k + 1][0], 8 * k + 8 + j) for j in range(8)]
        scale = jnp.zeros((8, n), F32)
        for j in range(8):
            s = {i: row_of(cols[j], i) for i in range(j, 8)}
            r = lax.rsqrt(s[j])
            inverse = r * r
            ratio = {i: s[i] * inverse for i in range(j + 1, 8)}
            if j < 7:
                cols[j + 1] = cols[j + 1] - (cols[j] * s[j + 1]) * inverse
            for i in range(j + 2, 8):
                cols[i] = cols[i] - cols[j] * ratio[i]
            up, ue = row_of(rows, j), row_of(ident, j)
            if j < 7:
                part = jnp.where(sub > j, cols[j] * inverse, 0.0)
                rows, ident = rows - part * up, ident - part * ue
            scale = jnp.where(sub == j, r, scale)
            for b, c in below.items():
                cj = c[j] * inverse
                if b == k + 1:
                    for i in range(8):
                        following[i] = following[i] - cj * row_of(c[j], i)
                for i in range(j + 1, 8):
                    c[i] = c[i] - c[j] * ratio[i]
                work[b] = [work[b][0] - cj * up, work[b][1] - cj * ue]
        if k + 1 < panels:
            cols = following
        u, w = rows * scale, ident * scale
        out.append(w)
        held.append((u, w))
        first = k + 1 + ahead
        if k % per == per - 1 and first < panels:
            us = jnp.concatenate([p[0] for p in held], 0)
            ws = jnp.concatenate([p[1] for p in held], 0)
            uh, um, ul = parts(us)
            wh, wm, wl = parts(ws)
            right = jnp.concatenate(
                [
                    jnp.concatenate([uh, um, ul, uh, um, uh], 0),
                    jnp.concatenate([wh, wm, wl, wh, wm, wh], 0),
                ],
                1,
            ).astype(BF16)
            left = jnp.concatenate([uh, uh, uh, um, um, ul], 0).T
            left = left[8 * first :, :].astype(BF16)
            change = jnp.dot(left, right, preferred_element_type=F32)
            for b in range(first, panels):
                part = change[8 * (b - first) : 8 * (b - first + 1), :]
                work[b] = [work[b][0] - part[:, :n], work[b][1] - part[:, n:]]
        if k % per == per - 1:
            held = []
    return jnp.concatenate(out, 0)


def dot(a, b):
    return jnp.dot(a, b, precision=EXACT, preferred_element_type=F32)


def dot_t(a, b):
    return lax.dot_general(
        a, b, (((1,), (1,)), ((), ())), precision=EXACT, preferred_element_type=F32
    )


def two_parts(a):
    high = a.astype(BF16)
    return high, (a - high.astype(F32)).astype(BF16)


def wide(a):
    high, low = two_parts(a)
    return jnp.concatenate([high, low, high], 1)


def times(a, b):
    high, low = two_parts(b)
    return lax.dot_general(
        a,
        jnp.concatenate([high, high, low], 1),
        (((1,), (1,)), ((), ())),
        preferred_element_type=F32,
    )


def store_inverse(ref, blocks):
    w11, w21, w22 = blocks
    h = w11.shape[0]
    ref[:h, :h] = w11
    ref[:h, h:] = jnp.zeros_like(w11)
    ref[h:, :h] = w21
    ref[h:, h:] = w22


def symmetric(a):
    return (a + a.T) * 0.5


def place_of(tags):
    return tags[0, 0].astype(jnp.int32)


def add_block(ref, block, place, tile, start=0):
    down = pl.multiple_of(place // 2 * tile, tile)
    right = pl.multiple_of(start + place % 2 * tile, tile)
    ref[pl.ds(down, tile), pl.ds(right, tile)] += block


def add_band_blocks(ref, blocks, width):
    for b in blocks:
        tile = b.shape[1]
        for owner in range(2):
            tag = b[2 * tile + 8 * owner : 2 * tile + 8 * owner + 8, :]
            block = b[owner * tile : (owner + 1) * tile, :]
            add_block(ref, block, place_of(tag), tile, owner * width)


def square_ids(n):
    return lax.broadcasted_iota(jnp.int32, (n, n), 0), lax.broadcasted_iota(jnp.int32, (n, n), 1)


def pack(ref, s):
    n = s.shape[0] // 2
    row, col = square_ids(n)
    ref[:n, :] = jnp.where(row >= col, s[:n, :n], s[n:, n:])
    ref[n : 2 * n, :] = s[n:, :n]
    diag = jnp.sum(jnp.where(row == col, s[n:, n:], 0.0), 0, keepdims=True)
    ref[2 * n : 2 * n + 8, :] = jnp.broadcast_to(diag, (8, n))


def unpack(ref):
    n = ref.shape[1]
    row, col = square_ids(n)
    both, low = ref[:n, :], ref[n : 2 * n, :]
    turned = both.T
    s00 = jnp.where(row >= col, both, turned)
    s11 = jnp.where(row < col, both, jnp.where(row > col, turned, ref[2 * n : 2 * n + 1, :]))
    return jnp.concatenate(
        [jnp.concatenate([s00, low.T], 1), jnp.concatenate([low, s11], 1)], 0
    )


def put_rows(ref, start, rows):
    n = ref.shape[1]
    ref[start : start + n, :] = rows[:, :n]
    ref[start + n : start + 2 * n, :] = rows[:, n:]


def get_rows(ref, start):
    n = ref.shape[1]
    return jnp.concatenate([ref[start : start + n, :], ref[start + n : start + 2 * n, :]], 1)


def sort_kernel(owner, slot, info, updates, front, out_ref, pay_ref, diag_ref, square, sems, side):
    sends, tile = updates.shape[:2]
    width = front.shape[1]
    near_diag = info[3] < 2
    corner = pltpu.make_async_copy(front, square, side)

    @pl.when(near_diag)
    def _():
        corner.start()

    out_ref[...] = jnp.zeros_like(out_ref)
    copies = [
        pltpu.make_async_copy(updates.at[j], out_ref.at[owner[j], pl.ds(0, tile), :], sems.at[j])
        for j in range(sends)
    ]
    for j in range(sends):
        copies[j].start()
        out_ref[owner[j], tile:, :] = jnp.full((8, tile), slot[j].astype(F32))

    @pl.when(near_diag)
    def _():
        corner.wait()

    @pl.when(info[3] == 0)
    def _():
        pack(diag_ref, square[:width, :])
        put_rows(diag_ref, width + 8, square[width : width + tile, :])

    @pl.when(info[3] == 1)
    def _():
        pack(diag_ref, square[width:, :])
        put_rows(diag_ref, width + 8, square[:width, tile:].T)

    for c in copies:
        c.wait()
    for o in range(2):
        pay_ref[o * tile : (o + 1) * tile, :] = out_ref[o, :tile, :]
        pay_ref[2 * tile + 8 * o : 2 * tile + 8 * o + 8, :] = out_ref[o, tile:, :]


def diagonal_kernel(info, diag, hop1, hop2, *refs):
    blocks, (diag_ref, band, part) = refs[:8], refs[8:]
    tile = diag.shape[1]
    width = 2 * tile

    @pl.when(info[0] == 0)
    def _():
        band[...] = jnp.zeros_like(band)
        add_band_blocks(band, blocks, width)
        for z, d in enumerate((diag, hop2, hop1, hop2)):

            @pl.when(info[1] == z)
            def _(d=d):
                diag_ref[...] = d[...]

        @pl.when(info[2] == 0)
        def _():
            pack(part, symmetric(band[:width, :width]))
            put_rows(part, width + 8, band[width : width + tile, :width])

        @pl.when(info[2] == 1)
        def _():
            pack(part, symmetric(band[width:, width:]))
            put_rows(part, width + 8, band[width + tile :, :width])

        diag_ref[...] += part[...]


def matched_kernel(info, turned, *refs):
    blocks, (out_ref, band) = refs[:8], refs[8:]
    width = turned.shape[1]

    @pl.when((info[0] == info[1]) & (info[0] > 0))
    def _():
        band[...] = jnp.zeros_like(band)
        add_band_blocks(band, blocks, width)
        start = pl.multiple_of(info[2] * width, width)
        out_ref[...] = turned[...].T + band[pl.ds(start, width), :]


def factor_kernel(info, here, there, out_ref, top, bottom, done, sems):
    tile = here.shape[1]
    width = 2 * tile

    @pl.when(info[2] == 0)
    def _():
        top[...] = here[...]
        bottom[...] = there[...]

    @pl.when(info[2] == 1)
    def _():
        top[...] = there[...]
        bottom[...] = here[...]

    copies = [pltpu.make_async_copy(done.at[i], out_ref.at[i], sems.at[i]) for i in range(3)]
    a = unpack(top)
    d = jnp.concatenate([get_rows(top, width + 8), get_rows(bottom, width + 8)], 0)
    w11 = factor_inverse(a[:tile, :tile])
    low = dot_t(a[tile:, :tile], w11)
    left = dot_t(d[:, :tile], w11)
    w22 = factor_inverse(a[tile:, tile:] - dot_t(low, low))
    rest = d[:, tile:] - dot_t(left, low)
    s = unpack(bottom) - dot_t(left, left)
    right = dot_t(rest, w22)
    store_inverse(done.at[0], (w11, -dot(w22, dot(low, w11)), w22))
    done[1] = jnp.concatenate([left, right], 1)
    copies[0].start()
    copies[1].start()
    upper, lower = right[:tile, :], right[tile:, :]
    w11 = factor_inverse(s[:tile, :tile] - dot_t(upper, upper))
    low = dot_t(s[tile:, :tile] - dot_t(lower, upper), w11)
    w22 = factor_inverse(s[tile:, tile:] - dot_t(lower, lower) - dot_t(low, low))
    store_inverse(done.at[2], (w11, -dot(w22, dot(low, w11)), w22))
    copies[2].start()
    for c in copies:
        c.wait()


def last_kernel(info, *refs):
    (shard, arrived, piece, piece2, matched, m1, m2, m3, factors), blocks = refs[:9], refs[9:17]
    out_ref, band, line, work, halves, came, pays, tri, sems = refs[17:]
    tile = came.shape[2]
    nrows, width = out_ref.shape
    group, layer, core, column = info[0], info[1], info[2], info[4]
    copies = [
        pltpu.make_async_copy(src, dst, sems.at[i])
        for i, (src, dst) in enumerate(
            [
                (shard, out_ref),
                (arrived, came),
                (piece, halves.at[0]),
                (piece2, halves.at[1]),
                (factors, tri),
            ]
            + [(b, pays.at[i]) for i, b in enumerate(blocks)]
        )
    ]
    last = len(copies)
    for c in copies:
        c.start()
    way = jnp.where(group == 0, 1, jnp.where((group == 2) | ((group == 3) & (layer == 2)), 3, 2))
    way = jnp.where(group == layer, 0, way)
    for k, m in enumerate((matched, m1, m2, m3)):

        @pl.when(way == k)
        def _(m=m):
            pltpu.make_async_copy(m, line, sems.at[last]).start()

    copies[0].wait()
    copies[1].wait()
    for i in range(came.shape[0]):
        add_block(out_ref, came[i, :tile, :], place_of(came[i, tile:, :]), tile)
    copies[2].wait()
    copies[3].wait()
    by_rows = (layer > 0) & (((group == 1) & (layer < 3)) | ((group > 1) & (layer > 1)))
    for c in range(2):
        side = jnp.where(core == 0, c, 1 - c)

        @pl.when(by_rows)
        def _(c=c, side=side):
            band[c * width : (c + 1) * width, :] = halves[side].T

        @pl.when(~by_rows)
        def _(c=c, side=side):
            band[:, c * width : (c + 1) * width] = halves[side]

    for c in copies[4:]:
        c.wait()
    pltpu.make_async_copy(matched, line, sems.at[last]).wait()

    @pl.when(group > 0)
    def _():
        add_band_blocks(band, [pays.at[i] for i in range(len(blocks))], width)

    w1, l21, v = tri[0], tri[1], tri[2]

    @pl.when(column == 0)
    def _():
        out_ref[...] = times(wide(out_ref[...]), w1)

    @pl.when(column > 0)
    def _():
        @pl.when(group == 0)
        def _():
            work[:width, :] = jnp.zeros((width, width), F32)
            work[width:, :] = l21

        @pl.when(group > 0)
        def _():
            work[...] = times(wide(band[:, :width]), w1)

        first = wide(work[...])

        @pl.when(column == 1)
        def _():
            rows = group * nrows + lax.broadcasted_iota(jnp.int32, (nrows, width), 0)
            own = out_ref[...]
            second = times(wide(own - times(first, l21)), v)
            out_ref[...] = jnp.where(rows >= width, second, own)

        @pl.when((column > 1) & (group == 0))
        def _():
            out_ref[...] -= times(first, times(wide(line[:, :width]), w1))

        @pl.when((column > 1) & (group > 0))
        def _():
            mine = times(wide(line[:, :width]), w1)
            rest = times(wide(line[:, width:] - times(wide(mine), l21)), v)
            second = times(wide(band[:, width:] - times(first, l21)), v)
            out_ref[...] = out_ref[...] - times(first, mine) - times(wide(second), rest)


def kernel(body, outs, args, smem=1, scratch=(), flops=1 << 20, sems=(), away=False, anywhere=()):
    space = pltpu.HBM if away else pltpu.VMEM
    spec = [pl.BlockSpec(memory_space=pltpu.SMEM)] * smem
    out_space = pltpu.HBM if isinstance(outs, type(pltpu.HBM((8, 128), F32))) else pltpu.VMEM
    spec += [
        pl.BlockSpec(memory_space=pl.ANY if i in anywhere else space) for i in range(len(args) - smem)
    ]
    if away:
        args = args[:smem] + tuple(
            a if i in anywhere else pltpu.with_memory_space_constraint(a, pltpu.HBM)
            for i, a in enumerate(args[smem:])
        )
    sizes = [math.prod(o.shape) for o in jax.tree.leaves(outs)] + [math.prod(s) for s in scratch]
    if not away:
        sizes += [a.size for a in args[smem:]]
    return pl.pallas_call(
        body,
        out_shape=outs,
        in_specs=spec,
        out_specs=jax.tree.map(lambda o: pl.BlockSpec(memory_space=out_space), outs),
        scratch_shapes=[pltpu.VMEM(s, F32) for s in scratch]
        + [pltpu.SemaphoreType.DMA(s) for s in sems],
        compiler_params=pltpu.CompilerParams(vmem_limit_bytes=4 * sum(sizes) + (6 << 20)),
        cost_estimate=pl.CostEstimate(flops=flops, bytes_accessed=1 << 20, transcendentals=0),
    )(*args)


def aligned(front, updates, target_owner, target_slot):
    nrows, width = front.shape
    tile = updates.shape[1]
    nleaf, nfront = lax.axis_size("leaf"), lax.axis_size("front")
    groups, layers = range(nleaf), range(nfront // 2)
    group, column = lax.axis_index("leaf"), lax.axis_index("front")
    layer, core = column // 2, column % 2
    info = jnp.stack([group, layer, core, group * nfront + column, column]).astype(jnp.int32)

    def dev(g, z, c):
        return g * nfront + 2 * z + c

    def send(x, pairs):
        return lax.ppermute(x, AXES, pairs)

    def out(*shape):
        return jax.ShapeDtypeStruct(shape, F32)

    both = range(2)
    swap = [(dev(g, z, c), dev(g, z, 1 - c)) for g in groups for z in layers for c in both]

    packed = out(2 * width + 8, tile)
    outgoing, payload, diag = kernel(
        sort_kernel,
        (out(nfront, tile + 8, tile), out(2 * tile + 16, tile), packed),
        (target_owner, target_slot, info, updates, front),
        smem=3,
        scratch=[(nrows, width)],
        sems=[(updates.shape[0],), ()],
        away=True,
    )
    blocks = [payload]
    for s in layers[1:]:
        pairs = [(dev(g, z, c), dev(g, z ^ s, c)) for g in groups for z in layers for c in both]
        blocks.append(send(payload, pairs))
    blocks += [send(b, swap) for b in blocks]
    hop1 = send(diag, [(dev(0, 0, c), dev(0, 2, c)) for c in both])
    hop2 = send(
        jnp.where(layer == 0, diag, hop1), [(dev(0, z, c), dev(0, z + 1, c)) for z in (0, 2) for c in both]
    )
    early, outgoing, info = lax.optimization_barrier((front, outgoing, info))
    turned = send(early, [(dev(0, z, c), dev(z, z, c)) for z in layers[1:] for c in both])
    diag, turned = lax.optimization_barrier((diag, turned))

    diag = kernel(
        diagonal_kernel,
        packed,
        (info, diag, hop1, hop2, *blocks),
        scratch=[(nrows, 2 * width), packed.shape],
    )
    diag, outgoing, early, turned = lax.optimization_barrier((diag, outgoing, early, turned))
    got = [
        send(diag, [(dev(0, z, c), dev(s, z, c)) for z in layers for c in both]) for s in groups[1:]
    ]
    diag = jnp.where(group == 0, diag, got[0] + got[1] + got[2])
    diag2 = send(diag, swap)

    hops = ((1, 0, 3), (2, 0, 1), (3, 0, 1), (1, 1, 2), (2, 2, 3), (3, 3, 2))
    far = send(
        jnp.where(layer == 0, early, turned), [(dev(g, z, c), dev(g, y, c)) for g, z, y in hops for c in both]
    )

    matched = kernel(
        matched_kernel, out(width, 2 * width), (info, turned, *blocks), scratch=[(nrows, 2 * width)]
    )
    matched, diag, outgoing = lax.optimization_barrier((matched, diag, outgoing))
    arrived = lax.all_to_all(outgoing, "front", split_axis=0, concat_axis=0, tiled=True)
    away = [
        send(matched, [(dev(z, z, c), dev(g, z, c)) for z, g in pairs for c in both])
        for pairs in (((1, 0), (2, 0), (3, 0)), ((1, 3), (2, 1), (3, 1)), ((1, 2), (2, 3), (3, 2)))
    ]

    diag, diag2, far = lax.optimization_barrier((diag, diag2, far))
    piece = jnp.where(layer == 0, front, jnp.where(group == layer, turned, far))
    piece2 = send(piece, swap)
    factors = kernel(
        factor_kernel,
        pltpu.HBM((3, width, width), F32),
        (info, diag, diag2),
        scratch=[packed.shape] * 2 + [(3, width, width)],
        flops=1 << 33,
        sems=[(3,)],
    )
    return kernel(
        last_kernel,
        out(nrows, width),
        (info, front, arrived, piece, piece2, matched, *away, factors, *blocks),
        scratch=[
            (nrows, 2 * width),
            (width, 2 * width),
            (nrows, width),
            (2, nrows, width),
            arrived.shape,
            (8,) + payload.shape,
            (3, width, width),
        ],
        flops=1 << 31,
        sems=[(16,)],
        away=True,
        anywhere=(2, 3, 5, 6, 7),
    )


def solution(mesh):
    nleaf, nfront = mesh.shape["leaf"], mesh.shape["front"]

    def shards(front, updates, target_owner, target_slot):
        nrows, width = front.shape
        tile = updates.shape[1]
        lines_up = (
            nrows == 2 * width
            and width == 2 * tile
            and nleaf == 4
            and nfront == 8
        )
        plan = aligned if lines_up else general
        return plan(front, updates, target_owner, target_slot)

    return jax.shard_map(
        shards,
        mesh=mesh,
        in_specs=(
            P("leaf", "front"),
            P(("leaf", "front"), None, None),
            P(("leaf", "front")),
            P(("leaf", "front")),
        ),
        out_specs=P("leaf", "front"),
        check_vma=False,
    )
```

```python
import math

import jax
import jax.numpy as jnp
from jax import lax
from jax.experimental import pallas as pl
from jax.experimental.pallas import tpu as pltpu
from jax.sharding import PartitionSpec as P

F32 = jnp.float32
BF16 = jnp.bfloat16
AXES = ("leaf", "front")
EXACT = lax.Precision.HIGHEST


def spread(value, axis, source):
    kept = jnp.where(lax.axis_index(axis) == source, value, 0).astype(value.dtype)
    return lax.psum(kept, axis)


def assemble(front, updates, target_owner, target_slot):
    nrows, width = front.shape
    tile = updates.shape[1]
    nfront = lax.axis_size("front")
    buffer = jnp.zeros((nfront, tile, tile), F32).at[target_owner].set(updates)
    labels = jnp.zeros((nfront,), F32).at[target_owner].set(target_slot.astype(F32))
    arrived, places = (
        lax.all_to_all(buffer, "front", split_axis=0, concat_axis=0, tiled=True),
        lax.all_to_all(labels, "front", split_axis=0, concat_axis=0, tiled=True),
    )
    places = places.astype(jnp.int32)
    col_tiles = width // tile
    grid = front.reshape(nrows // tile, tile, col_tiles, tile)
    grid = grid.at[places // col_tiles, :, places % col_tiles, :].add(arrived)
    return grid.reshape(nrows, width)


def eliminate(shard, panel, start, row_ids, col_ids, column):
    nrows, width = panel.shape
    diag = spread(panel[start : start + width], "leaf", 0)
    chol = jnp.linalg.cholesky(diag)
    eye = jnp.eye(width, dtype=F32)
    inverse = lax.linalg.triangular_solve(chol, eye, left_side=True, lower=True)
    prod = jnp.dot(panel, inverse.T, precision=EXACT)
    lower = jnp.where(row_ids[:, None] >= start, prod, panel)
    owner_row = column * width // nrows
    offset = column * width - owner_row * nrows
    mine = lax.dynamic_slice_in_dim(lower, offset, width, 0)
    across = spread(mine, "leaf", owner_row)
    trail = jnp.where(row_ids[:, None] >= start + width, lower, 0.0)
    updated = shard - jnp.dot(trail, across.T, precision=EXACT)
    updated = jnp.where(col_ids[None, :] >= start + width, updated, shard)
    return (jnp.where(column == start // width, lower, updated), lower)


def general(front, updates, target_owner, target_slot):
    nrows, width = front.shape
    column = lax.axis_index("front")
    row_ids = lax.axis_index("leaf") * nrows + jnp.arange(nrows, dtype=jnp.int32)
    col_ids = column * width + jnp.arange(width, dtype=jnp.int32)
    shard = assemble(front, updates, target_owner, target_slot)
    first = spread(shard, "front", 0)
    shard, lower = eliminate(shard, first, 0, row_ids, col_ids, column)
    second = spread(shard, "front", 1)
    shard, lower = eliminate(shard, second, width, row_ids, col_ids, column)
    return shard


def lane_of(x, c):
    return jnp.take_along_axis(x, jnp.full(x.shape, c, jnp.int32), axis=1)


def row_of(x, i):
    return jnp.broadcast_to(x[i : i + 1, :], x.shape)


def parts(x):
    high = x.astype(BF16).astype(F32)
    rest = x - high
    mid = rest.astype(BF16).astype(F32)
    return high, mid, (rest - mid).astype(BF16).astype(F32)


def factor_inverse(a):
    n = a.shape[0]
    panels, per, ahead = n // 8, 2, 2
    sub = lax.broadcasted_iota(jnp.int32, (8, n), 0)
    lane = lax.broadcasted_iota(jnp.int32, (8, n), 1)
    work = [
        [a[8 * k : 8 * k + 8, :], jnp.where(lane == sub + 8 * k, 1.0, 0.0).astype(F32)]
        for k in range(panels)
    ]
    out, held = [], []
    for k in range(panels):
        rows, ident = work[k]
        if k == 0:
            cols = [lane_of(rows, j) for j in range(8)]
        last = min(panels - 1, max(k + 1, (k // per + 1) * per - 1 + ahead))
        below = {
            b: [lane_of(work[b][0], 8 * k + j) for j in range(8)]
            for b in range(k + 1, last + 1)
        }
        if k + 1 < panels:
            following = [lane_of(work[k + 1][0], 8 * k + 8 + j) for j in range(8)]
        scale = jnp.zeros((8, n), F32)
        for j in range(8):
            s = {i: row_of(cols[j], i) for i in range(j, 8)}
            r = lax.rsqrt(s[j])
            inverse = r * r
            ratio = {i: s[i] * inverse for i in range(j + 1, 8)}
            if j < 7:
                cols[j + 1] = cols[j + 1] - (cols[j] * s[j + 1]) * inverse
            for i in range(j + 2, 8):
                cols[i] = cols[i] - cols[j] * ratio[i]
            up, ue = row_of(rows, j), row_of(ident, j)
            if j < 7:
                part = jnp.where(sub > j, cols[j] * inverse, 0.0)
                rows, ident = rows - part * up, ident - part * ue
            scale = jnp.where(sub == j, r, scale)
            for b, c in below.items():
                cj = c[j] * inverse
                if b == k + 1:
                    for i in range(8):
                        following[i] = following[i] - cj * row_of(c[j], i)
                for i in range(j + 1, 8):
                    c[i] = c[i] - c[j] * ratio[i]
                work[b] = [work[b][0] - cj * up, work[b][1] - cj * ue]
        if k + 1 < panels:
            cols = following
        u, w = rows * scale, ident * scale
        out.append(w)
        held.append((u, w))
        first = k + 1 + ahead
        if k % per == per - 1 and first < panels:
            us = jnp.concatenate([p[0] for p in held], 0)
            ws = jnp.concatenate([p[1] for p in held], 0)
            uh, um, ul = parts(us)
            wh, wm, wl = parts(ws)
            right = jnp.concatenate(
                [
                    jnp.concatenate([uh, um, ul, uh, um, uh], 0),
                    jnp.concatenate([wh, wm, wl, wh, wm, wh], 0),
                ],
                1,
            ).astype(BF16)
            left = jnp.concatenate([uh, uh, uh, um, um, ul], 0).T
            left = left[8 * first :, :].astype(BF16)
            change = jnp.dot(left, right, preferred_element_type=F32)
            for b in range(first, panels):
                part = change[8 * (b - first) : 8 * (b - first + 1), :]
                work[b] = [work[b][0] - part[:, :n], work[b][1] - part[:, n:]]
        if k % per == per - 1:
            held = []
    return jnp.concatenate(out, 0)


def dot(a, b):
    return jnp.dot(a, b, precision=EXACT, preferred_element_type=F32)


def dot_t(a, b):
    return lax.dot_general(
        a, b, (((1,), (1,)), ((), ())), precision=EXACT, preferred_element_type=F32
    )


def two_parts(a):
    high = a.astype(BF16)
    return high, (a - high.astype(F32)).astype(BF16)


def wide(a):
    high, low = two_parts(a)
    return jnp.concatenate([high, low, high], 1)


def times(a, b):
    high, low = two_parts(b)
    return lax.dot_general(
        a,
        jnp.concatenate([high, high, low], 1),
        (((1,), (1,)), ((), ())),
        preferred_element_type=F32,
    )


def store_inverse(ref, blocks):
    w11, w21, w22 = blocks
    h = w11.shape[0]
    ref[:h, :h] = w11
    ref[:h, h:] = jnp.zeros_like(w11)
    ref[h:, :h] = w21
    ref[h:, h:] = w22


def symmetric(a):
    return (a + a.T) * 0.5


def place_of(tags):
    return tags[0, 0].astype(jnp.int32)


def add_block(ref, block, place, tile, start=0):
    down = pl.multiple_of(place // 2 * tile, tile)
    right = pl.multiple_of(start + place % 2 * tile, tile)
    ref[pl.ds(down, tile), pl.ds(right, tile)] += block


def add_band_blocks(ref, blocks, width):
    for b in blocks:
        tile = b.shape[1]
        for owner in range(2):
            tag = b[2 * tile + 8 * owner : 2 * tile + 8 * owner + 8, :]
            block = b[owner * tile : (owner + 1) * tile, :]
            add_block(ref, block, place_of(tag), tile, owner * width)


def square_ids(n):
    return lax.broadcasted_iota(jnp.int32, (n, n), 0), lax.broadcasted_iota(jnp.int32, (n, n), 1)


def pack(ref, s):
    n = s.shape[0] // 2
    row, col = square_ids(n)
    ref[:n, :] = jnp.where(row >= col, s[:n, :n], s[n:, n:])
    ref[n : 2 * n, :] = s[n:, :n]
    diag = jnp.sum(jnp.where(row == col, s[n:, n:], 0.0), 0, keepdims=True)
    ref[2 * n : 2 * n + 8, :] = jnp.broadcast_to(diag, (8, n))


def unpack(ref):
    n = ref.shape[1]
    row, col = square_ids(n)
    both, low = ref[:n, :], ref[n : 2 * n, :]
    turned = both.T
    s00 = jnp.where(row >= col, both, turned)
    s11 = jnp.where(row < col, both, jnp.where(row > col, turned, ref[2 * n : 2 * n + 1, :]))
    return jnp.concatenate(
        [jnp.concatenate([s00, low.T], 1), jnp.concatenate([low, s11], 1)], 0
    )


def put_rows(ref, start, rows):
    n = ref.shape[1]
    ref[start : start + n, :] = rows[:, :n]
    ref[start + n : start + 2 * n, :] = rows[:, n:]


def get_rows(ref, start):
    n = ref.shape[1]
    return jnp.concatenate([ref[start : start + n, :], ref[start + n : start + 2 * n, :]], 1)


def sort_kernel(owner, slot, info, updates, front, out_ref, pay_ref, diag_ref, square, sems, side):
    sends, tile = updates.shape[:2]
    width = front.shape[1]
    near_diag = info[3] < 2
    corner = pltpu.make_async_copy(front, square, side)

    @pl.when(near_diag)
    def _():
        corner.start()

    out_ref[...] = jnp.zeros_like(out_ref)
    copies = [
        pltpu.make_async_copy(updates.at[j], out_ref.at[owner[j], pl.ds(0, tile), :], sems.at[j])
        for j in range(sends)
    ]
    for j in range(sends):
        copies[j].start()
        out_ref[owner[j], tile:, :] = jnp.full((8, tile), slot[j].astype(F32))

    @pl.when(near_diag)
    def _():
        corner.wait()

    @pl.when(info[3] == 0)
    def _():
        pack(diag_ref, square[:width, :])
        put_rows(diag_ref, width + 8, square[width : width + tile, :])

    @pl.when(info[3] == 1)
    def _():
        pack(diag_ref, square[width:, :])
        put_rows(diag_ref, width + 8, square[:width, tile:].T)

    for c in copies:
        c.wait()
    for o in range(2):
        pay_ref[o * tile : (o + 1) * tile, :] = out_ref[o, :tile, :]
        pay_ref[2 * tile + 8 * o : 2 * tile + 8 * o + 8, :] = out_ref[o, tile:, :]


def diagonal_kernel(info, diag, hop1, hop2, *refs):
    blocks, (diag_ref, band, part) = refs[:8], refs[8:]
    tile = diag.shape[1]
    width = 2 * tile

    @pl.when(info[0] == 0)
    def _():
        band[...] = jnp.zeros_like(band)
        add_band_blocks(band, blocks, width)
        for z, d in enumerate((diag, hop2, hop1, hop2)):

            @pl.when(info[1] == z)
            def _(d=d):
                diag_ref[...] = d[...]

        @pl.when(info[2] == 0)
        def _():
            pack(part, symmetric(band[:width, :width]))
            put_rows(part, width + 8, band[width : width + tile, :width])

        @pl.when(info[2] == 1)
        def _():
            pack(part, symmetric(band[width:, width:]))
            put_rows(part, width + 8, band[width + tile :, :width])

        diag_ref[...] += part[...]


def matched_kernel(info, turned, *refs):
    blocks, (out_ref, band) = refs[:8], refs[8:]
    width = turned.shape[1]

    @pl.when((info[0] == info[1]) & (info[0] > 0))
    def _():
        band[...] = jnp.zeros_like(band)
        add_band_blocks(band, blocks, width)
        start = pl.multiple_of(info[2] * width, width)
        out_ref[...] = turned[...].T + band[pl.ds(start, width), :]


def factor_kernel(info, here, there, out_ref, top, bottom, done, sems):
    tile = here.shape[1]
    width = 2 * tile

    @pl.when(info[2] == 0)
    def _():
        top[...] = here[...]
        bottom[...] = there[...]

    @pl.when(info[2] == 1)
    def _():
        top[...] = there[...]
        bottom[...] = here[...]

    copies = [pltpu.make_async_copy(done.at[i], out_ref.at[i], sems.at[i]) for i in range(3)]
    a = unpack(top)
    d = jnp.concatenate([get_rows(top, width + 8), get_rows(bottom, width + 8)], 0)
    w11 = factor_inverse(a[:tile, :tile])
    low = dot_t(a[tile:, :tile], w11)
    left = dot_t(d[:, :tile], w11)
    w22 = factor_inverse(a[tile:, tile:] - dot_t(low, low))
    rest = d[:, tile:] - dot_t(left, low)
    s = unpack(bottom) - dot_t(left, left)
    right = dot_t(rest, w22)
    store_inverse(done.at[0], (w11, -dot(w22, dot(low, w11)), w22))
    done[1] = jnp.concatenate([left, right], 1)
    copies[0].start()
    copies[1].start()
    upper, lower = right[:tile, :], right[tile:, :]
    w11 = factor_inverse(s[:tile, :tile] - dot_t(upper, upper))
    low = dot_t(s[tile:, :tile] - dot_t(lower, upper), w11)
    w22 = factor_inverse(s[tile:, tile:] - dot_t(lower, lower) - dot_t(low, low))
    store_inverse(done.at[2], (w11, -dot(w22, dot(low, w11)), w22))
    copies[2].start()
    for c in copies:
        c.wait()


def last_kernel(info, *refs):
    (shard, arrived, piece, piece2, matched, m1, m2, m3, factors), blocks = refs[:9], refs[9:17]
    out_ref, band, line, work, halves, came, pays, tri, sems = refs[17:]
    tile = came.shape[2]
    nrows, width = out_ref.shape
    group, layer, core, column = info[0], info[1], info[2], info[4]
    copies = [
        pltpu.make_async_copy(src, dst, sems.at[i])
        for i, (src, dst) in enumerate(
            [
                (shard, out_ref),
                (arrived, came),
                (piece, halves.at[0]),
                (piece2, halves.at[1]),
                (factors, tri),
            ]
            + [(b, pays.at[i]) for i, b in enumerate(blocks)]
        )
    ]
    last = len(copies)
    for c in copies:
        c.start()
    way = jnp.where(group == 0, 1, jnp.where((group == 2) | ((group == 3) & (layer == 2)), 3, 2))
    way = jnp.where(group == layer, 0, way)
    for k, m in enumerate((matched, m1, m2, m3)):

        @pl.when(way == k)
        def _(m=m):
            pltpu.make_async_copy(m, line, sems.at[last]).start()

    copies[0].wait()
    copies[1].wait()
    for i in range(came.shape[0]):
        add_block(out_ref, came[i, :tile, :], place_of(came[i, tile:, :]), tile)
    copies[2].wait()
    copies[3].wait()
    by_rows = (layer > 0) & (((group == 1) & (layer < 3)) | ((group > 1) & (layer > 1)))
    for c in range(2):
        side = jnp.where(core == 0, c, 1 - c)

        @pl.when(by_rows)
        def _(c=c, side=side):
            band[c * width : (c + 1) * width, :] = halves[side].T

        @pl.when(~by_rows)
        def _(c=c, side=side):
            band[:, c * width : (c + 1) * width] = halves[side]

    for c in copies[4:]:
        c.wait()
    pltpu.make_async_copy(matched, line, sems.at[last]).wait()

    @pl.when(group > 0)
    def _():
        add_band_blocks(band, [pays.at[i] for i in range(len(blocks))], width)

    w1, l21, v = tri[0], tri[1], tri[2]

    @pl.when(column == 0)
    def _():
        out_ref[...] = times(wide(out_ref[...]), w1)

    @pl.when(column > 0)
    def _():
        @pl.when(group == 0)
        def _():
            work[:width, :] = jnp.zeros((width, width), F32)
            work[width:, :] = l21

        @pl.when(group > 0)
        def _():
            work[...] = times(wide(band[:, :width]), w1)

        first = wide(work[...])

        @pl.when(column == 1)
        def _():
            rows = group * nrows + lax.broadcasted_iota(jnp.int32, (nrows, width), 0)
            own = out_ref[...]
            second = times(wide(own - times(first, l21)), v)
            out_ref[...] = jnp.where(rows >= width, second, own)

        @pl.when((column > 1) & (group == 0))
        def _():
            out_ref[...] -= times(first, times(wide(line[:, :width]), w1))

        @pl.when((column > 1) & (group > 0))
        def _():
            mine = times(wide(line[:, :width]), w1)
            rest = times(wide(line[:, width:] - times(wide(mine), l21)), v)
            second = times(wide(band[:, width:] - times(first, l21)), v)
            out_ref[...] = out_ref[...] - times(first, mine) - times(wide(second), rest)


def kernel(body, outs, args, smem=1, scratch=(), flops=1 << 20, sems=(), away=False, anywhere=()):
    space = pltpu.HBM if away else pltpu.VMEM
    spec = [pl.BlockSpec(memory_space=pltpu.SMEM)] * smem
    out_space = pltpu.HBM if isinstance(outs, type(pltpu.HBM((8, 128), F32))) else pltpu.VMEM
    spec += [
        pl.BlockSpec(memory_space=pl.ANY if i in anywhere else space) for i in range(len(args) - smem)
    ]
    if away:
        args = args[:smem] + tuple(
            a if i in anywhere else pltpu.with_memory_space_constraint(a, pltpu.HBM)
            for i, a in enumerate(args[smem:])
        )
    sizes = [math.prod(o.shape) for o in jax.tree.leaves(outs)] + [math.prod(s) for s in scratch]
    if not away:
        sizes += [a.size for a in args[smem:]]
    return pl.pallas_call(
        body,
        out_shape=outs,
        in_specs=spec,
        out_specs=jax.tree.map(lambda o: pl.BlockSpec(memory_space=out_space), outs),
        scratch_shapes=[pltpu.VMEM(s, F32) for s in scratch]
        + [pltpu.SemaphoreType.DMA(s) for s in sems],
        compiler_params=pltpu.CompilerParams(vmem_limit_bytes=4 * sum(sizes) + (6 << 20)),
        cost_estimate=pl.CostEstimate(flops=flops, bytes_accessed=1 << 20, transcendentals=0),
    )(*args)


def aligned(front, updates, target_owner, target_slot):
    nrows, width = front.shape
    tile = updates.shape[1]
    nleaf, nfront = lax.axis_size("leaf"), lax.axis_size("front")
    groups, layers = range(nleaf), range(nfront // 2)
    group, column = lax.axis_index("leaf"), lax.axis_index("front")
    layer, core = column // 2, column % 2
    info = jnp.stack([group, layer, core, group * nfront + column, column]).astype(jnp.int32)

    def dev(g, z, c):
        return g * nfront + 2 * z + c

    def send(x, pairs):
        return lax.ppermute(x, AXES, pairs)

    def out(*shape):
        return jax.ShapeDtypeStruct(shape, F32)

    both = range(2)
    swap = [(dev(g, z, c), dev(g, z, 1 - c)) for g in groups for z in layers for c in both]

    packed = out(2 * width + 8, tile)
    outgoing, payload, diag = kernel(
        sort_kernel,
        (out(nfront, tile + 8, tile), out(2 * tile + 16, tile), packed),
        (target_owner, target_slot, info, updates, front),
        smem=3,
        scratch=[(nrows, width)],
        sems=[(updates.shape[0],), ()],
        away=True,
    )
    blocks = [payload]
    for s in (3, 2, 1):
        pairs = [(dev(g, z, c), dev(g, z ^ s, c)) for g in groups for z in layers for c in both]
        blocks.append(send(payload, pairs))
    blocks += [send(b, swap) for b in blocks]
    hop1 = send(diag, [(dev(0, 0, c), dev(0, 2, c)) for c in both])
    hop2 = send(
        jnp.where(layer == 0, diag, hop1), [(dev(0, z, c), dev(0, z + 1, c)) for z in (0, 2) for c in both]
    )
    early, outgoing, info = lax.optimization_barrier((front, outgoing, info))
    turned = send(early, [(dev(0, z, c), dev(z, z, c)) for z in layers[1:] for c in both])
    diag, turned = lax.optimization_barrier((diag, turned))

    diag = kernel(
        diagonal_kernel,
        packed,
        (info, diag, hop1, hop2, *blocks),
        scratch=[(nrows, 2 * width), packed.shape],
    )
    diag, outgoing, early, turned = lax.optimization_barrier((diag, outgoing, early, turned))
    got = [
        send(diag, [(dev(0, z, c), dev(s, z, c)) for z in layers for c in both]) for s in groups[1:]
    ]
    diag = jnp.where(group == 0, diag, got[0] + got[1] + got[2])
    diag2 = send(diag, swap)

    hops = ((1, 0, 3), (2, 0, 1), (3, 0, 1), (1, 1, 2), (2, 2, 3), (3, 3, 2))
    far = send(
        jnp.where(layer == 0, early, turned), [(dev(g, z, c), dev(g, y, c)) for g, z, y in hops for c in both]
    )

    matched = kernel(
        matched_kernel, out(width, 2 * width), (info, turned, *blocks), scratch=[(nrows, 2 * width)]
    )
    matched, diag, outgoing = lax.optimization_barrier((matched, diag, outgoing))
    arrived = lax.all_to_all(outgoing, "front", split_axis=0, concat_axis=0, tiled=True)
    away = [
        send(matched, [(dev(z, z, c), dev(g, z, c)) for z, g in pairs for c in both])
        for pairs in (((1, 0), (2, 0), (3, 0)), ((1, 3), (2, 1), (3, 1)), ((1, 2), (2, 3), (3, 2)))
    ]

    diag, diag2, far = lax.optimization_barrier((diag, diag2, far))
    piece = jnp.where(layer == 0, front, jnp.where(group == layer, turned, far))
    piece2 = send(piece, swap)
    factors = kernel(
        factor_kernel,
        pltpu.HBM((3, width, width), F32),
        (info, diag, diag2),
        scratch=[packed.shape] * 2 + [(3, width, width)],
        flops=1 << 33,
        sems=[(3,)],
    )
    return kernel(
        last_kernel,
        out(nrows, width),
        (info, front, arrived, piece, piece2, matched, *away, factors, *blocks),
        scratch=[
            (nrows, 2 * width),
            (width, 2 * width),
            (nrows, width),
            (2, nrows, width),
            arrived.shape,
            (8,) + payload.shape,
            (3, width, width),
        ],
        flops=1 << 31,
        sems=[(16,)],
        away=True,
        anywhere=(2, 3, 5, 6, 7),
    )


def solution(mesh):
    nleaf, nfront = mesh.shape["leaf"], mesh.shape["front"]

    def shards(front, updates, target_owner, target_slot):
        nrows, width = front.shape
        tile = updates.shape[1]
        lines_up = (
            nrows == 2 * width
            and width == 2 * tile
            and nleaf == 4
            and nfront == 8
        )
        plan = aligned if lines_up else general
        return plan(front, updates, target_owner, target_slot)

    return jax.shard_map(
        shards,
        mesh=mesh,
        in_specs=(
            P("leaf", "front"),
            P(("leaf", "front"), None, None),
            P(("leaf", "front")),
            P(("leaf", "front")),
        ),
        out_specs=P("leaf", "front"),
        check_vma=False,
    )
```
